32 devices in a mesh: groups: 2 (over x), dp: 16 (over z, y, core).
Axes of the slice: x: 2, y: 2, z: 4, core: 2. Of those that a mesh axis runs over, the one named last changes fastest.
Arguments:
- embeddings: float32 [24576, 512], P(('groups', 'dp')), parts along dimension 0, as said below
- owner_index: int32 [24576], P(('groups', 'dp')), parts along dimension 0, may hold values from 0 to 15, as said below
- sub_label: int32 [24576], P(('groups', 'dp')), parts along dimension 0, may hold values from 0 to 2, as said below
- run_start: int32 [32], P('groups'), parts along dimension 0, may hold values from 0 to 15, as said below
Outputs:
- nearest: float32 [24576], P(('groups', 'dp')), parts along dimension 0
The draws below stay inside these ranges and needn't reach their ends.
There are 2 independent parts, one for each index of `groups`. The reference program is written for one: setup_inputs(seed, part) draws one part's arguments, and reference() takes and returns one part's arrays. A program takes and returns all parts, laid end to end along the dimension named above; each array names one. Nothing has to cross between parts.
Inputs may be any that keep to these rules, and one draw needn't show every extreme that they name: `owner_index`: from the rows of one device at most 96 go to one owner; in every draw one owner receives exactly 96 rows from every device. From the rows of one device at most 48 with sub_label 0 go to one owner; in every draw one owner receives exactly 48 such rows from every device. Of the embeddings of one owner at most one has sub_label 3 - 1. Owners form groups of 1 to 3 consecutive indices covering all owners in order, with a group of 3 in every draw; run_start gives each owner the first index of its group. `embeddings`: finite real values.
All inputs are finite; a program needn't handle non-finite values.
Results may differ from the reference program's by a relative error of at most 0.00032.
Values may be sent and summed in bfloat16 or wider, within the bound.
No kernel may reach another device: no remote copies, remote signals or barrier semaphores. Data moves between devices by JAX's collectives and lax.ppermute only.
A program may use at most 64 MiB of HBM per device.

```python
import math
import jax
import jax.numpy as jnp
from jax import lax

D = 512
ROWS_DEV = 768
LABELS = 3
SEND = 96
ROWS = 12288
N_DP = 16


def layout(key):
    k_crowd, k_pool, k_lone, k_len = jax.random.split(key, 4)
    crowded = jax.random.randint(k_crowd, (), 0, N_DP).astype(jnp.int32)
    pool_index = jnp.arange((N_DP - 1) * SEND, dtype=jnp.int32)
    pool_owner = (pool_index // SEND).astype(jnp.int32)
    pool_owner = pool_owner + (pool_owner >= crowded).astype(jnp.int32)
    slot_pool = (pool_owner * SEND + pool_index % SEND).astype(jnp.int32)
    crowd_slots = (crowded * SEND + jnp.arange(SEND, dtype=jnp.int32)).astype(jnp.int32)

    def one_source(key_first, key_second):
        chosen = jax.random.permutation(key_first, slot_pool)[:ROWS_DEV - SEND]
        combined = jnp.concatenate([crowd_slots, chosen])
        return jax.random.permutation(key_second, combined)
    k_pool_a, k_pool_b = jax.random.split(k_pool, 2)
    keys_first = jax.random.split(k_pool_a, N_DP)
    keys_second = jax.random.split(k_pool_b, N_DP)
    slots = jax.vmap(one_source)(keys_first, keys_second).reshape(-1).astype(jnp.int32)
    owner_index = (slots // SEND).astype(jnp.int32)
    shared = slots % SEND < SEND // 2
    scores = jax.random.permutation(k_lone, ROWS).astype(jnp.int32)
    candidate = jnp.where(shared, ROWS, scores).astype(jnp.int32)
    lowest = jnp.full((N_DP,), ROWS, jnp.int32).at[owner_index].min(candidate)
    lone = jnp.logical_not(shared) & (candidate == lowest[owner_index])
    sub_label = jnp.where(shared, 0, jnp.where(lone, LABELS - 1, 1)).astype(jnp.int32)
    lengths = jax.random.randint(k_len, (N_DP,), 1, 4).astype(jnp.int32).at[0].set(3)
    run_ends = jnp.cumsum(lengths)
    indices = jnp.arange(N_DP, dtype=jnp.int32)
    starts_here = jnp.any(run_ends[None, :] == indices[:, None], axis=1) | (indices == 0)
    run_start = lax.cummax(jnp.where(starts_here, indices, 0), axis=0).astype(jnp.int32)
    return (owner_index, sub_label, run_start)


def draw_owner_index(key, part):
    return layout(key)[0]


def draw_sub_label(key, part):
    return layout(key)[1]


def draw_run_start(key, part):
    return layout(key)[2]


def draw_embeddings(key, part):
    owner_index, sub_label, run_start = layout(key)
    cluster = jnp.where(sub_label == 0, run_start[owner_index] * LABELS, owner_index * LABELS + sub_label)
    key = jax.random.fold_in(key, 11)
    k_cent, k_twin_tab, k_twin, k_jitter, k_spread = jax.random.split(key, 5)
    centers = jax.random.normal(k_cent, (N_DP * LABELS, D), jnp.float32)
    twin_table = jax.random.normal(k_twin_tab, (4096, D), jnp.float32)
    twin_index = jax.random.randint(k_twin, (ROWS,), 0, 64)
    twin_rows = (cluster * 64 + twin_index) % 4096
    spread = jnp.exp(jax.random.uniform(k_spread, (ROWS, 1), jnp.float32, math.log(0.4), math.log(1.2)))
    jitter = jax.random.normal(k_jitter, (ROWS, D), jnp.float32)
    values = centers[cluster] + 1.5 * twin_table[twin_rows] + spread * jitter
    return values.astype(jnp.float32)


def setup_inputs(seed: int = 0, part: int = 0) -> dict:
    key_list = jax.random.split(jax.random.key(seed), 5)
    part_splits = jax.random.split(jax.random.fold_in(key_list[4], part), 5)
    embeddings = draw_embeddings(jax.random.fold_in(jax.random.fold_in(key_list[4], part), 71), part)
    owner_index = draw_owner_index(jax.random.fold_in(jax.random.fold_in(key_list[4], part), 71), part)
    sub_label = draw_sub_label(jax.random.fold_in(jax.random.fold_in(key_list[4], part), 71), part)
    run_start = draw_run_start(jax.random.fold_in(jax.random.fold_in(key_list[4], part), 71), part)
    return dict(embeddings=embeddings, owner_index=owner_index, sub_label=sub_label, run_start=run_start)


def reference(embeddings, owner_index, sub_label, run_start):
    cluster = jnp.where(sub_label == 0, run_start[owner_index] * LABELS, owner_index * LABELS + sub_label).astype(jnp.int32)
    squares = lax.optimization_barrier(jnp.sum(embeddings * embeddings, axis=1, keepdims=True))
    unit_rows = (embeddings * lax.rsqrt(squares + 1e-06)).astype(jnp.bfloat16)
    capacity = N_DP * SEND
    padding = 5 * capacity
    ordering = jnp.argsort(owner_index, stable=True).astype(jnp.int32)
    sorted_unit = jnp.concatenate([unit_rows[ordering], jnp.zeros((padding, D), jnp.bfloat16)])
    sorted_cluster = jnp.concatenate([cluster[ordering], jnp.full((padding,), -1, jnp.int32)])
    sorted_owner = jnp.concatenate([owner_index[ordering], jnp.full((padding,), -1, jnp.int32)])
    owners = jnp.arange(N_DP, dtype=jnp.int32)
    starts = lax.optimization_barrier(jnp.sum((owner_index[None, :] < owners[:, None]).astype(jnp.int32), axis=1)).astype(jnp.int32)

    def per_owner(which):
        first = starts[which]
        window = starts[jnp.maximum(which - 2, 0)]
        queries = lax.dynamic_slice_in_dim(sorted_unit, first, capacity, 0).astype(jnp.float32)
        query_cluster = lax.dynamic_slice_in_dim(sorted_cluster, first, capacity, 0)
        query_owner = lax.dynamic_slice_in_dim(sorted_owner, first, capacity, 0)
        candidates = lax.dynamic_slice_in_dim(sorted_unit, window, 5 * capacity, 0).astype(jnp.float32)
        cand_cluster = lax.dynamic_slice_in_dim(sorted_cluster, window, 5 * capacity, 0)
        scores = jnp.dot(queries, candidates.T, precision=lax.Precision.HIGHEST, preferred_element_type=jnp.float32)
        query_pos = first + jnp.arange(capacity, dtype=jnp.int32)
        cand_pos = window + jnp.arange(5 * capacity, dtype=jnp.int32)
        matches = (query_cluster[:, None] == cand_cluster[None, :]) & (query_pos[:, None] != cand_pos[None, :]) & (cand_cluster[None, :] >= 0)
        best_row = lax.optimization_barrier(jnp.max(jnp.where(matches, scores, jnp.float32(-1.0)), axis=1))
        spots = jnp.where(query_owner == which, query_pos, ROWS + padding).astype(jnp.int32)
        return (best_row, spots)
    bests, spots = lax.map(per_owner, owners)
    sorted_out = jnp.full((ROWS,), -1.0, jnp.float32).at[spots.reshape(-1)].set(bests.reshape(-1), mode='drop')
    return jnp.zeros((ROWS,), jnp.float32).at[ordering].set(sorted_out)
```

```python
import jax
import jax.numpy as jnp
from jax import lax
from jax.sharding import PartitionSpec as P

LABELS = 3
CHUNK_BYTES = 7 * 2**20


def chunk_count(rows, width, peers):
    count = 1
    while rows % (2 * count) == 0 and (rows // count) * width * 2 * peers > CHUNK_BYTES:
        count *= 2
    return count


def best_in_chunk(queries, query_tags, query_ids, candidates, cand_tags, cand_ids):
    scores = lax.dot_general(
        queries, candidates, (((1,), (1,)), ((), ())), preferred_element_type=jnp.float32
    )
    matches = (query_tags[:, None] == cand_tags[None, :]) & (
        query_ids[:, None] != cand_ids[None, :]
    )
    return jnp.max(jnp.where(matches, scores, jnp.float32(-1.0)), axis=1)


def local(embeddings, owner_index, sub_label, run_start):
    rows, width = embeddings.shape
    peers = lax.axis_size("dp")
    me = lax.axis_index("dp")
    owners = jnp.arange(peers, dtype=jnp.int32)
    group_first = jnp.sum(
        jnp.where(owner_index[:, None] == owners[None, :], run_start[None, :], 0), axis=1
    )
    tags = jnp.where(sub_label == 0, group_first * LABELS, owner_index * LABELS + sub_label)
    all_tags = lax.all_gather(tags, "dp", axis=0)
    squares = jnp.sum(embeddings * embeddings, axis=1, keepdims=True)
    unit_rows = (embeddings * lax.rsqrt(squares + 1e-06)).astype(jnp.bfloat16)
    all_ids = jnp.arange(peers * rows, dtype=jnp.int32).reshape(peers, rows)
    my_ids = me * rows + jnp.arange(rows, dtype=jnp.int32)
    chunks = chunk_count(rows, width, peers)
    size = rows // chunks

    def step(k, best):
        part = lax.dynamic_slice_in_dim(unit_rows, k * size, size, 0)
        gathered = lax.all_gather(part, "dp", axis=0, tiled=True)
        part_tags = lax.dynamic_slice_in_dim(all_tags, k * size, size, 1).reshape(-1)
        part_ids = lax.dynamic_slice_in_dim(all_ids, k * size, size, 1).reshape(-1)
        found = best_in_chunk(unit_rows, tags, my_ids, gathered, part_tags, part_ids)
        return jnp.maximum(best, found)

    best = jnp.full((rows,), -1.0, jnp.float32)
    if chunks <= 4:
        for k in range(chunks):
            best = step(k, best)
        return best
    return lax.fori_loop(0, chunks, step, best)


def solution(mesh):
    in_specs = (P(("groups", "dp"), None), P(("groups", "dp")), P(("groups", "dp")), P("groups"))
    out_specs = P(("groups", "dp"))
    return jax.shard_map(local, mesh=mesh, in_specs=in_specs, out_specs=out_specs, check_vma=False)
```

```python
import functools

import jax
import jax.numpy as jnp
from jax import lax
from jax.experimental import pallas as pl
from jax.experimental.pallas import tpu as pltpu
from jax.sharding import PartitionSpec as P

LABELS = 3
PLANE = 4
PAD = 16
BASE = 64.0
TILE = 256
VMEM_LIMIT = 24 * 2**20


def whole(count):
    return [pl.BlockSpec(memory_space=pltpu.VMEM)] * count


def params():
    return pltpu.CompilerParams(vmem_limit_bytes=VMEM_LIMIT)


def pack_kernel(rows, embeddings_ref, tags_ref, block_ref):
    values = embeddings_ref[...]
    squares = jnp.sum(values * values, axis=1, keepdims=True)
    block_ref[0:rows, :] = (values * lax.rsqrt(squares + 1e-06)).astype(jnp.bfloat16)
    block_ref[rows : rows + PAD, :] = tags_ref[...].astype(jnp.bfloat16)


def tag_lanes(block_ref, rows):
    width = block_ref.shape[1]
    count = -(-rows // width)
    tail = block_ref[rows : rows + PAD, :].astype(jnp.float32)
    parts = [tail[2 * n : 2 * n + 1] * BASE + tail[2 * n + 1 : 2 * n + 2] for n in range(count)]
    return jnp.concatenate(parts, axis=1)[:, :rows]


def tag_columns(block_ref, rows):
    return jnp.transpose(jnp.broadcast_to(tag_lanes(block_ref, rows), (128, rows)))


def scores(rows_ref, lanes_ref, rows, first):
    return lax.dot_general(
        rows_ref[0:rows, :],
        lanes_ref[first : first + TILE, :],
        (((1,), (1,)), ((), ())),
        preferred_element_type=jnp.float32,
    )


def fold_sublanes(values):
    rows, lanes = values.shape
    return jnp.max(values.reshape(rows // 8, 8, lanes), axis=0)


def fold_lanes(values):
    return jnp.max(jnp.transpose(values), axis=0, keepdims=True)


def plane_kernel(rows, own_ref, *refs):
    others, best_ref = refs[:-1], refs[-1]
    own_tags = tag_lanes(own_ref, rows)
    for first in range(0, rows, TILE):
        lane_tags = own_tags[:, first : first + TILE]
        best = jnp.full((8, TILE), -1.0, jnp.float32)
        for which, block_ref in enumerate((own_ref,) + others):
            found = scores(block_ref, own_ref, rows, first)
            columns = tag_columns(block_ref, rows)
            match = jnp.concatenate([columns] * (TILE // 128), axis=1) == lane_tags
            if which == 0:
                row_id = lax.broadcasted_iota(jnp.int32, (rows, TILE), 0)
                lane_id = lax.broadcasted_iota(jnp.int32, (rows, TILE), 1) + first
                match = match & (row_id != lane_id)
            best = jnp.maximum(best, fold_sublanes(jnp.where(match, found, -1.0)))
        best_ref[:, first : first + TILE] = jnp.max(best, axis=0, keepdims=True)


def cross_kernel(rows, count, away_ref, *refs):
    blocks = refs[:count]
    away_best_ref, plane_best_ref = refs[count:]
    away_tags = tag_lanes(away_ref, rows)
    best = [jnp.full((8, TILE), -1.0, jnp.float32) for _ in range(0, rows, TILE)]
    for which, block_ref in enumerate(blocks):
        columns = tag_columns(block_ref, rows)
        wide = jnp.concatenate([columns] * (TILE // 128), axis=1)
        row_best = jnp.full((rows, 128), -1.0, jnp.float32)
        for n, first in enumerate(range(0, rows, TILE)):
            found = scores(block_ref, away_ref, rows, first)
            masked = jnp.where(wide == away_tags[:, first : first + TILE], found, -1.0)
            best[n] = jnp.maximum(best[n], fold_sublanes(masked))
            for lane in range(0, TILE, 128):
                row_best = jnp.maximum(row_best, masked[:, lane : lane + 128])
        plane_best_ref[which : which + 1, :] = fold_lanes(row_best)
    for n, first in enumerate(range(0, rows, TILE)):
        away_best_ref[:, first : first + TILE] = jnp.max(best[n], axis=0, keepdims=True)


def cost(pairs, rows, width):
    return pl.CostEstimate(
        flops=2 * pairs * rows * rows * width,
        bytes_accessed=5 * rows * width * 2,
        transcendentals=0,
    )


def plane_steps(planes):
    steps = []
    for distance in range(1, planes // 2 + 1):
        if 2 * distance < planes:
            steps.append([(z, (z + distance) % planes) for z in range(planes)])
        else:
            steps.append(
                [(z, z + distance) if z % 2 == 0 else (z + distance, z) for z in range(distance)]
            )
    return steps


def local(embeddings, owner_index, sub_label, run_start):
    rows, width = embeddings.shape
    peers = lax.axis_size("dp")
    planes = peers // PLANE
    me = lax.axis_index("dp")
    owners = jnp.arange(peers, dtype=jnp.int32)
    group_first = jnp.sum(
        jnp.where(owner_index[:, None] == owners[None, :], run_start[None, :], 0), axis=1
    )
    tags = 1 + jnp.where(sub_label == 0, group_first * LABELS, owner_index * LABELS + sub_label)
    base = int(BASE)
    padded = jnp.pad(tags, (0, -rows % width)).reshape(-1, width)
    digits = jnp.stack([padded // base, padded % base], axis=1).reshape(-1, width)
    digits = jnp.pad(digits, ((0, PAD - digits.shape[0]), (0, 0))).astype(jnp.float32)
    block = pl.pallas_call(
        functools.partial(pack_kernel, rows),
        out_shape=jax.ShapeDtypeStruct((rows + PAD, width), jnp.bfloat16),
        in_specs=whole(2),
        out_specs=pl.BlockSpec(memory_space=pltpu.VMEM),
        compiler_params=params(),
        name="pack",
    )(embeddings, digits)

    away = []
    for step in plane_steps(planes):
        pairs = [(s * PLANE + j, t * PLANE + j) for s, t in step for j in range(PLANE)]
        away.append((pairs, lax.ppermute(block, "dp", pairs)))
    mates = [
        lax.ppermute(block, "dp", [(i, i ^ m) for i in range(peers)]) for m in (2, 3, 1)
    ]
    best = pl.pallas_call(
        functools.partial(plane_kernel, rows),
        out_shape=jax.ShapeDtypeStruct((1, rows), jnp.float32),
        in_specs=whole(PLANE),
        out_specs=pl.BlockSpec(memory_space=pltpu.VMEM),
        compiler_params=params(),
        cost_estimate=cost(PLANE, rows, width),
        name="plane",
    )(block, *mates)
    plane_best = None
    for pairs, received in away:
        away_best, found = pl.pallas_call(
            functools.partial(cross_kernel, rows, PLANE),
            out_shape=(
                jax.ShapeDtypeStruct((1, rows), jnp.float32),
                jax.ShapeDtypeStruct((PLANE, rows), jnp.float32),
            ),
            in_specs=whole(1 + PLANE),
            out_specs=tuple(whole(2)),
            compiler_params=params(),
            cost_estimate=cost(PLANE, rows, width),
            name="cross",
        )(received, block, *mates)
        back = lax.ppermute(away_best, "dp", [(t, s) for s, t in pairs])
        if len(pairs) < peers:
            half = planes // 2
            z = me // PLANE
            sent = ((z % half) % 2 == 0) == (z < half)
            back = jnp.where(sent, back, -1.0)
        best = jnp.maximum(best, back)
        plane_best = found if plane_best is None else jnp.maximum(plane_best, found)
    best = jnp.maximum(best, plane_best[0:1])
    for n, m in enumerate((2, 3, 1)):
        back = lax.ppermute(plane_best[n + 1 : n + 2], "dp", [(i, i ^ m) for i in range(peers)])
        best = jnp.maximum(best, back)
    return best.reshape(rows)


def solution(mesh):
    in_specs = (P(("groups", "dp"), None), P(("groups", "dp")), P(("groups", "dp")), P("groups"))
    out_specs = P(("groups", "dp"))
    return jax.shard_map(local, mesh=mesh, in_specs=in_specs, out_specs=out_specs, check_vma=False)
```

```python
import functools

import jax
import jax.numpy as jnp
import numpy as np
from jax import lax
from jax.experimental import pallas as pl
from jax.experimental.pallas import tpu as pltpu
from jax.sharding import PartitionSpec as P

LABELS = 3
PLANE = 4
PAD = 16
BASE = 64.0
TILE = 256
HEAD = 256
VMEM_LIMIT = 24 * 2**20


def whole(count):
    return [pl.BlockSpec(memory_space=pltpu.VMEM)] * count


def params():
    return pltpu.CompilerParams(vmem_limit_bytes=VMEM_LIMIT)


def lanes_shape(rows):
    return jax.ShapeDtypeStruct((-(-rows // 1024) * 8, 128), jnp.float32)


def pack_kernel(
    rows, peers, embeddings, owner_ref, label_ref, run_ref, head_ref, tail_ref, held, sems
):
    copies = []
    for n, first in enumerate(range(0, rows, TILE)):
        part = pl.ds(first, TILE)
        copies.append(pltpu.make_async_copy(embeddings.at[part], held.at[part], sems.at[n]))
        copies[-1].start()
    owner = owner_ref[...]
    first_owner = jnp.zeros_like(owner)
    for n in range(peers):
        first_owner = jnp.where(owner == n, run_ref[n], first_owner)
    label = label_ref[...]
    tags = 1 + jnp.where(label == 0, first_owner * LABELS, owner * LABELS + label)
    tags = tags.astype(jnp.float32)
    high = jnp.floor(tags * (1.0 / BASE))
    digits = jnp.concatenate([high, tags - high * BASE], axis=0).astype(jnp.bfloat16)
    width = head_ref.shape[1]
    head_ref[0:PAD, :] = jnp.concatenate(
        [digits, jnp.zeros((PAD, width - 128), jnp.bfloat16)], axis=1
    )
    for n, first in enumerate(range(0, rows, TILE)):
        copies[n].wait()
        values = held[first : first + TILE, :]
        squares = jnp.sum(values * values, axis=1, keepdims=True)
        unit = (values * lax.rsqrt(squares + 1e-06)).astype(jnp.bfloat16)
        if first < HEAD:
            head_ref[PAD + first : PAD + first + TILE, :] = unit
        else:
            tail_ref[first - HEAD : first - HEAD + TILE, :] = unit


def tag_rows(block_ref):
    digits = block_ref[0:PAD, 0:128].astype(jnp.float32)
    return digits[0:8] * BASE + digits[8:16]


def tag_columns(block_ref, rows):
    tags = tag_rows(block_ref)
    return jnp.concatenate(
        [jnp.transpose(jnp.broadcast_to(tags[n : n + 1], (128, 128))) for n in range(rows // 128)],
        axis=0,
    )


def dot_rows(values, lanes):
    return lax.dot_general(
        values, lanes, (((1,), (1,)), ((), ())), preferred_element_type=jnp.float32
    )


def unit_rows(part_ref, has_tags):
    return part_ref.at[PAD:] if has_tags else part_ref


def unit_parts(refs):
    head, tail = unit_rows(refs[0], True), refs[1]
    return ((0, head), (head.shape[0], tail))


def fold_sublanes(values):
    rows, lanes = values.shape
    return jnp.max(values.reshape(rows // 8, 8, lanes), axis=0)


def fold_lanes(values):
    return jnp.concatenate(
        [
            jnp.max(jnp.transpose(values[first : first + 128]), axis=0, keepdims=True)
            for first in range(0, values.shape[0], 128)
        ],
        axis=0,
    )


def plane_kernel(rows, count, with_self, *refs):
    own, refs = refs[:2], refs[2:]
    blocks, refs = [refs[2 * n : 2 * n + 2] for n in range(count)], refs[2 * count :]
    before_ref, refs = (None, refs) if with_self else (refs[0], refs[1:])
    best_ref, column_refs = refs[0], refs[1:]
    own_tags = tag_rows(own[0])
    for block, column_ref in zip(blocks, column_refs):
        column_ref[...] = tag_columns(block[0], rows)
    if with_self:
        best_ref[...] = jnp.full(best_ref.shape, -1.0, jnp.float32)
    else:
        best_ref[...] = before_ref[...]
    for own_first, own_part in unit_parts(own):
        for tile in range(0, own_part.shape[0], TILE):
            lanes = own_part[tile : tile + TILE, :]
            for which, (block, column_ref) in enumerate(zip(blocks, column_refs)):
                for first, part in unit_parts(block):
                    count = part.shape[0]
                    found = dot_rows(part[...], lanes)
                    for lane in range(0, TILE, 128):
                        lane_row = own_first + tile + lane
                        row = lane_row // 128
                        match = column_ref[first : first + count, :] == own_tags[row : row + 1]
                        if with_self and which == 0 and first < lane_row + 128 <= first + count:
                            row_id = lax.broadcasted_iota(jnp.int32, (count, 128), 0) + first
                            lane_id = lax.broadcasted_iota(jnp.int32, (count, 128), 1) + lane_row
                            match = match & (row_id != lane_id)
                        masked = jnp.where(match, found[:, lane : lane + 128], -1.0)
                        folded = jnp.max(fold_sublanes(masked), axis=0, keepdims=True)
                        place = pl.ds(row, 1)
                        best_ref[place, :] = jnp.maximum(best_ref[place, :], folded)


def cross_kernel(rows, first, has_tags, tags_ref, part_ref, *refs):
    blocks, refs = [refs[2 * n : 2 * n + 2] for n in range(PLANE)], refs[2 * PLANE :]
    columns, refs = refs[:PLANE], refs[PLANE:]
    away_before, plane_before, away_best, plane_best = refs
    away_tags = tag_rows(tags_ref)
    away = unit_rows(part_ref, has_tags)
    away_best[...] = away_before[...]
    for which in range(PLANE):
        for start, part in unit_parts(blocks[which]):
            count = part.shape[0]
            row_best = jnp.full((count, 128), -1.0, jnp.float32)
            column = columns[which][start : start + count, :]
            for tile in range(0, away.shape[0], TILE):
                found = dot_rows(part[...], away[tile : tile + TILE, :])
                for lane in range(0, TILE, 128):
                    row = (first + tile + lane) // 128
                    match = column == away_tags[row : row + 1]
                    masked = jnp.where(match, found[:, lane : lane + 128], -1.0)
                    row_best = jnp.maximum(row_best, masked)
                    folded = jnp.max(fold_sublanes(masked), axis=0, keepdims=True)
                    place = pl.ds(row, 1)
                    away_best[place, :] = jnp.maximum(away_best[place, :], folded)
            place = pl.ds(start // 128, count // 128)
            folded = fold_lanes(row_best)
            plane_best[which, place, :] = jnp.maximum(folded, plane_before[which, place, :])


def cost(pairs, rows, width):
    return pl.CostEstimate(
        flops=int(2 * pairs * rows * rows * width),
        bytes_accessed=5 * rows * width * 2,
        transcendentals=0,
    )


def plane_steps(planes):
    steps = []
    for distance in range(1, planes // 2 + 1):
        if 2 * distance < planes:
            steps.append([(z, (z + distance) % planes) for z in range(planes)])
        else:
            steps.append(
                [(z, z + distance) if z % 2 == 0 else (z + distance, z) for z in range(distance)]
            )
    return steps


def after(value, *others):
    return lax.optimization_barrier((value,) + others)[0]


def local(embeddings, owner_index, sub_label, run_start):
    rows, width = embeddings.shape
    peers = lax.axis_size("dp")
    planes = peers // PLANE
    me = lax.axis_index("dp")
    lanes = lanes_shape(rows)

    def in_lanes(values):
        return jnp.pad(values, (0, lanes.shape[0] * 128 - rows)).reshape(lanes.shape)

    own = pl.pallas_call(
        functools.partial(pack_kernel, rows, peers),
        out_shape=(
            jax.ShapeDtypeStruct((PAD + HEAD, width), jnp.bfloat16),
            jax.ShapeDtypeStruct((rows - HEAD, width), jnp.bfloat16),
        ),
        in_specs=[pl.BlockSpec(memory_space=pltpu.HBM)]
        + whole(2)
        + [pl.BlockSpec(memory_space=pltpu.SMEM)],
        out_specs=tuple(whole(2)),
        scratch_shapes=[
            pltpu.VMEM((rows, width), jnp.float32),
            pltpu.SemaphoreType.DMA((rows // TILE,)),
        ],
        compiler_params=params(),
        name="pack",
    )(embeddings, in_lanes(owner_index), in_lanes(sub_label), run_start)

    def mate(value, distance):
        return lax.ppermute(value, "dp", [(i, i ^ distance) for i in range(peers)])

    away = []
    beside = tuple(mate(part, 2) for part in own)
    near = tuple(mate(part, 1) for part in own)
    across = ()
    for step in plane_steps(planes):
        pairs = [(s * PLANE + j, t * PLANE + j) for s, t in step for j in range(PLANE)]
        received = []
        for n, part in enumerate(own):
            if len(away) == 1:
                waited = (away[0][1][n], beside[n]) + across
                across += (mate(after(beside[n], *waited), 1),)
                part = after(part, *waited) if n else part
            elif away:
                part = after(part, away[-1][1][n])
            received.append(lax.ppermute(part, "dp", pairs))
        away.append((pairs, received))

    columns = jax.ShapeDtypeStruct((rows, 128), jnp.float32)
    best, own_columns, near_columns = pl.pallas_call(
        functools.partial(plane_kernel, rows, 2, True),
        out_shape=(lanes, columns, columns),
        in_specs=whole(6),
        out_specs=tuple(whole(3)),
        compiler_params=params(),
        cost_estimate=cost(2, rows, width),
        name="plane_near",
    )(*own, *own, *near)
    best, beside_columns, across_columns = pl.pallas_call(
        functools.partial(plane_kernel, rows, 2, False),
        out_shape=(lanes, columns, columns),
        in_specs=whole(7),
        out_specs=tuple(whole(3)),
        compiler_params=params(),
        cost_estimate=cost(2, rows, width),
        name="plane_far",
    )(*own, *beside, *across, best)

    plane = (*own, *near, *beside, *across)
    plane_columns = (own_columns, near_columns, beside_columns, across_columns)
    plane_best = jnp.full((PLANE,) + lanes.shape, -1.0, jnp.float32)
    for pairs, received in away:
        away_best = jnp.full(lanes.shape, -1.0, jnp.float32)
        first = 0
        for n, part in enumerate(received):
            part_rows = part.shape[0] - (PAD if n == 0 else 0)
            away_best, plane_best = pl.pallas_call(
                functools.partial(cross_kernel, rows, first, n == 0),
                out_shape=(lanes, jax.ShapeDtypeStruct(plane_best.shape, jnp.float32)),
                in_specs=whole(4 + 3 * PLANE),
                out_specs=tuple(whole(2)),
                compiler_params=params(),
                cost_estimate=cost(PLANE * part_rows / rows, rows, width),
                name="cross",
            )(received[0], part, *plane, *plane_columns, away_best, plane_best)
            first += part_rows
        back = lax.ppermute(away_best, "dp", [(t, s) for s, t in pairs])
        if len(pairs) < peers:
            sent = np.zeros((peers,), np.bool_)
            sent[[s for s, _ in pairs]] = True
            back = jnp.where(jnp.asarray(sent)[me], back, -1.0)
        best = jnp.maximum(best, back)
    best = jnp.maximum(best, plane_best[0])
    for n, distance in ((3, 3), (2, 2), (1, 1)):
        best = jnp.maximum(best, mate(plane_best[n], distance))
    return best.reshape(-1)[:rows]


def solution(mesh):
    in_specs = (P(("groups", "dp"), None), P(("groups", "dp")), P(("groups", "dp")), P("groups"))
    out_specs = P(("groups", "dp"))
    return jax.shard_map(local, mesh=mesh, in_specs=in_specs, out_specs=out_specs, check_vma=False)
```

```python
import functools

import jax
import jax.numpy as jnp
from jax import lax
from jax.experimental import pallas as pl
from jax.experimental.pallas import tpu as pltpu
from jax.sharding import PartitionSpec as P

LABELS = 3
PLANE = 4
PAD = 16
BASE = 64.0
TILE = 256
AWAY_CUT = (3,)
MATE_CUT = (1, 1)
NEAR_CUT = (3,)
VMEM_LIMIT = 24 * 2**20


def whole(count):
    return [pl.BlockSpec(memory_space=pltpu.VMEM)] * count


def params():
    return pltpu.CompilerParams(vmem_limit_bytes=VMEM_LIMIT)


def cuts(rows, cut):
    return [rows * share // sum(cut) + (PAD if n == 0 else 0) for n, share in enumerate(cut)]


def lanes_shape(rows):
    return jax.ShapeDtypeStruct((-(-rows // 1024) * 8, 128), jnp.float32)


def pack_kernel(rows, embeddings_ref, owner_ref, label_ref, run_ref, *part_refs):
    owner = owner_ref[...]
    runs = jnp.broadcast_to(run_ref[0:1, :], owner.shape)
    first_owner = jnp.take_along_axis(runs, owner, axis=1)
    label = label_ref[...]
    tags = 1 + jnp.where(label == 0, first_owner * LABELS, owner * LABELS + label)
    tags = tags.astype(jnp.float32)
    high = jnp.floor(tags * (1.0 / BASE))
    digits = jnp.concatenate([high, tags - high * BASE], axis=0).astype(jnp.bfloat16)
    width = embeddings_ref.shape[1]
    digits = jnp.concatenate([digits, jnp.zeros((PAD, width - 128), jnp.bfloat16)], axis=1)
    values = embeddings_ref[...]
    squares = jnp.sum(values * values, axis=1, keepdims=True)
    unit = (values * lax.rsqrt(squares + 1e-06)).astype(jnp.bfloat16)
    first = 0
    for part_ref in part_refs:
        if first == 0:
            part_ref[0:PAD, :] = digits
            count = part_ref.shape[0] - PAD
            part_ref[PAD:, :] = unit[0:count]
        else:
            count = part_ref.shape[0]
            part_ref[...] = unit[first : first + count]
        first = (first + count) % rows


def tag_rows(block_ref):
    digits = block_ref[0:PAD, 0:128].astype(jnp.float32)
    return digits[0:8] * BASE + digits[8:16]


def tag_columns(block_ref, rows):
    tags = tag_rows(block_ref)
    return jnp.concatenate(
        [jnp.transpose(jnp.broadcast_to(tags[n : n + 1], (128, 128))) for n in range(rows // 128)],
        axis=0,
    )


def dot_rows(values, lanes):
    return lax.dot_general(
        values, lanes, (((1,), (1,)), ((), ())), preferred_element_type=jnp.float32
    )


def unit_parts(refs):
    parts, first = [], 0
    for n, ref in enumerate(refs):
        part = ref if n else ref.at[PAD:]
        parts.append((first, part))
        first += part.shape[0]
    return parts


def take(refs, counts):
    groups = []
    for count in counts:
        groups.append(refs[:count])
        refs = refs[count:]
    return groups, refs


def fold_sublanes(values):
    rows, lanes = values.shape
    return jnp.max(values.reshape(rows // 8, 8, lanes), axis=0)


def fold_lanes(values):
    return jnp.concatenate(
        [
            jnp.max(jnp.transpose(values[first : first + 128]), axis=0, keepdims=True)
            for first in range(0, values.shape[0], 128)
        ],
        axis=0,
    )


def plane_kernel(rows, counts, with_self, own_ref, *refs):
    blocks, refs = take(refs, counts)
    best_ref, column_refs = refs[-1 - len(counts)], refs[-len(counts) :]
    if with_self:
        best_ref[...] = refs[0][...]
    else:
        best_ref[...] = jnp.full(best_ref.shape, -1.0, jnp.float32)
    own_tags = tag_rows(own_ref)
    for block, column_ref in zip(blocks, column_refs):
        column_ref[...] = tag_columns(block[0], rows)
    for tile in range(0, rows, TILE):
        lanes = own_ref[PAD + tile : PAD + tile + TILE, :]
        for which, (block, column_ref) in enumerate(zip(blocks, column_refs)):
            for first, part in unit_parts(block):
                count = part.shape[0]
                found = dot_rows(part[...], lanes)
                for lane in range(0, TILE, 128):
                    row = (tile + lane) // 128
                    match = column_ref[first : first + count, :] == own_tags[row : row + 1]
                    if with_self and which == 0:
                        row_id = lax.broadcasted_iota(jnp.int32, (count, 128), 0) + first
                        lane_id = lax.broadcasted_iota(jnp.int32, (count, 128), 1) + tile + lane
                        match = match & (row_id != lane_id)
                    masked = jnp.where(match, found[:, lane : lane + 128], -1.0)
                    folded = jnp.max(fold_sublanes(masked), axis=0, keepdims=True)
                    place = pl.ds(row, 1)
                    best_ref[place, :] = jnp.maximum(best_ref[place, :], folded)


def cross_kernel(rows, index, counts, tags_ref, away_ref, *refs):
    blocks, refs = take(refs, counts)
    columns, refs = refs[:PLANE], refs[PLANE:]
    away_before, plane_before, away_best, plane_best = refs
    away_tags = tag_rows(tags_ref)
    away = away_ref if index else away_ref.at[PAD:]
    away_rows = away.shape[0]
    away_best[...] = away_before[...]
    for which in range(PLANE):
        for start, part in unit_parts(blocks[which]):
            count = part.shape[0]
            row_best = jnp.full((count, 128), -1.0, jnp.float32)
            column = columns[which][start : start + count, :]
            for tile in range(0, away_rows, TILE):
                lanes = min(TILE, away_rows - tile)
                found = dot_rows(part[...], away[tile : tile + lanes, :])
                for lane in range(0, lanes, 128):
                    row = (index * away_rows + tile + lane) // 128
                    match = column == away_tags[row : row + 1]
                    masked = jnp.where(match, found[:, lane : lane + 128], -1.0)
                    row_best = jnp.maximum(row_best, masked)
                    folded = jnp.max(fold_sublanes(masked), axis=0, keepdims=True)
                    place = pl.ds(row, 1)
                    away_best[place, :] = jnp.maximum(away_best[place, :], folded)
            place = pl.ds(start // 128, count // 128)
            folded = fold_lanes(row_best)
            plane_best[which, place, :] = jnp.maximum(folded, plane_before[which, place, :])


def small_cost():
    return pl.CostEstimate(flops=1, bytes_accessed=1, transcendentals=0)


def plane_steps(planes):
    steps = []
    for distance in range(1, planes // 2 + 1):
        if 2 * distance < planes:
            steps.append([(z, (z + distance) % planes) for z in range(planes)])
        else:
            steps.append(
                [(z, z + distance) if z % 2 == 0 else (z + distance, z) for z in range(distance)]
            )
    return steps


def after(value, *others):
    return lax.optimization_barrier((value,) + others)[0]


def local(embeddings, owner_index, sub_label, run_start):
    rows, width = embeddings.shape
    peers = lax.axis_size("dp")
    planes = peers // PLANE
    me = lax.axis_index("dp")
    lanes = lanes_shape(rows)

    def in_lanes(values):
        space = lanes.shape[0] * 128 - values.shape[0]
        return jnp.pad(values, (0, space)).reshape(lanes.shape)

    ways = ((1,), AWAY_CUT, MATE_CUT, NEAR_CUT)
    sizes = sum((cuts(rows, way) for way in ways), [])
    packed = pl.pallas_call(
        functools.partial(pack_kernel, rows),
        out_shape=tuple(jax.ShapeDtypeStruct((size, width), jnp.bfloat16) for size in sizes),
        in_specs=whole(4),
        out_specs=tuple(whole(len(sizes))),
        compiler_params=params(),
        cost_estimate=small_cost(),
        name="pack",
    )(embeddings, in_lanes(owner_index), in_lanes(sub_label), in_lanes(run_start))
    own, to_away, to_mate, to_near = take(packed, [len(way) for way in ways])[0]

    def mate(value, distance):
        return lax.ppermute(value, "dp", [(i, i ^ distance) for i in range(peers)])

    away = []
    for n, step in enumerate(plane_steps(planes)):
        pairs = [(s * PLANE + j, t * PLANE + j) for s, t in step for j in range(PLANE)]
        parts = to_away if n else own
        if n > 1:
            parts = [after(part, away[-1][1][-1]) for part in parts]
        away.append((pairs, [lax.ppermute(part, "dp", pairs) for part in parts]))
    beside = [mate(part, 2) for part in to_mate]
    near = [mate(part, 1) for part in to_near]
    across = [mate(part, 1) for part in beside]

    columns = jax.ShapeDtypeStruct((rows, 128), jnp.float32)
    best, beside_columns, across_columns = pl.pallas_call(
        functools.partial(plane_kernel, rows, (len(beside), len(across)), False),
        out_shape=(lanes, columns, columns),
        in_specs=whole(1 + len(beside) + len(across)),
        out_specs=tuple(whole(3)),
        compiler_params=params(),
        cost_estimate=small_cost(),
        name="plane_far",
    )(own[0], *beside, *across)
    best, own_columns, near_columns = pl.pallas_call(
        functools.partial(plane_kernel, rows, (1, len(near)), True),
        out_shape=(lanes, columns, columns),
        in_specs=whole(3 + len(near)),
        out_specs=tuple(whole(3)),
        compiler_params=params(),
        cost_estimate=small_cost(),
        name="plane_near",
    )(own[0], own[0], *near, best)

    plane = (own[0], *near, *beside, *across)
    plane_columns = (own_columns, near_columns, beside_columns, across_columns)
    plane_best = jnp.full((PLANE,) + lanes.shape, -1.0, jnp.float32)
    counts = (1, len(near), len(beside), len(across))
    for pairs, received in away:
        away_best = jnp.full(lanes.shape, -1.0, jnp.float32)
        for n, part in enumerate(received):
            away_best, plane_best = pl.pallas_call(
                functools.partial(cross_kernel, rows, n, counts),
                out_shape=(lanes, jax.ShapeDtypeStruct(plane_best.shape, jnp.float32)),
                in_specs=whole(len(plane) + PLANE + 4),
                out_specs=tuple(whole(2)),
                compiler_params=params(),
                cost_estimate=small_cost(),
                name="cross",
            )(received[0], part, *plane, *plane_columns, away_best, plane_best)
        back = lax.ppermute(away_best, "dp", [(t, s) for s, t in pairs])
        if len(pairs) < peers:
            z = me // PLANE
            half = planes // 2
            back = jnp.where((z % 2 == 0) == (z < half), back, -1.0)
        best = jnp.maximum(best, back)
    best = best.reshape(-1)[:rows]
    best = jnp.maximum(best, plane_best[0].reshape(-1)[:rows])
    for n, distance in ((3, 3), (2, 2), (1, 1)):
        back = mate(plane_best[n], distance)
        best = jnp.maximum(best, back.reshape(-1)[:rows])
    return best


def solution(mesh):
    in_specs = (P(("groups", "dp"), None), P(("groups", "dp")), P(("groups", "dp")), P("groups"))
    out_specs = P(("groups", "dp"))
    return jax.shard_map(local, mesh=mesh, in_specs=in_specs, out_specs=out_specs, check_vma=False)
```

```python
import functools

import jax
import jax.numpy as jnp
from jax import lax
from jax.experimental import pallas as pl
from jax.experimental.pallas import tpu as pltpu
from jax.sharding import PartitionSpec as P

LABELS = 3
PLANE = 4
PAD = 16
BASE = 64.0
TILE = 256
AWAY_CUT = (3,)
MATE_CUT = (2, 1)
NEAR_CUT = (2, 1)
VMEM_LIMIT = 24 * 2**20


def whole(count):
    return [pl.BlockSpec(memory_space=pltpu.VMEM)] * count


def params():
    return pltpu.CompilerParams(vmem_limit_bytes=VMEM_LIMIT)


def cuts(rows, cut):
    return [rows * share // sum(cut) + (PAD if n == 0 else 0) for n, share in enumerate(cut)]


def lanes_shape(rows):
    return jax.ShapeDtypeStruct((-(-rows // 1024) * 8, 128), jnp.float32)


def pack_kernel(rows, embeddings_ref, ints_ref, *part_refs):
    label_row = rows // 128
    owner, label = ints_ref[0:8, :], ints_ref[label_row : label_row + 8, :]
    runs = ints_ref[2 * label_row : 2 * label_row + 1, :]
    first_owner = jnp.take_along_axis(jnp.broadcast_to(runs, owner.shape), owner, axis=1)
    tags = 1 + jnp.where(label == 0, first_owner * LABELS, owner * LABELS + label)
    tags = tags.astype(jnp.float32)
    high = jnp.floor(tags * (1.0 / BASE))
    digits = jnp.concatenate([high, tags - high * BASE], axis=0).astype(jnp.bfloat16)
    width = embeddings_ref.shape[1]
    digits = jnp.concatenate([digits, jnp.zeros((PAD, width - 128), jnp.bfloat16)], axis=1)
    places, first = [], 0
    for part_ref in part_refs:
        base = PAD if first == 0 else 0
        if base:
            part_ref[0:PAD, :] = digits
        count = part_ref.shape[0] - base
        places.append((part_ref, base - first, first, first + count))
        first = (first + count) % rows
    for row in range(0, rows, 128):
        values = embeddings_ref[row : row + 128, :]
        squares = jnp.sum(values * values, axis=1, keepdims=True)
        unit = (values * lax.rsqrt(squares + 1e-06)).astype(jnp.bfloat16)
        for part_ref, shift, start, stop in places:
            if start <= row < stop:
                part_ref[row + shift : row + shift + 128, :] = unit


def tag_rows(block_ref):
    digits = block_ref[0:PAD, 0:128].astype(jnp.float32)
    return digits[0:8] * BASE + digits[8:16]


def tag_columns(block_ref, rows):
    tags = tag_rows(block_ref)
    return jnp.concatenate(
        [jnp.transpose(jnp.broadcast_to(tags[n : n + 1], (128, 128))) for n in range(rows // 128)],
        axis=0,
    )


def dot_rows(values, lanes):
    return lax.dot_general(
        values, lanes, (((1,), (1,)), ((), ())), preferred_element_type=jnp.float32
    )


def unit_parts(refs):
    parts, first = [], 0
    for n, ref in enumerate(refs):
        part = ref if n else ref.at[PAD:]
        parts.append((first, part))
        first += part.shape[0]
    return parts


def take(refs, counts):
    groups = []
    for count in counts:
        groups.append(refs[:count])
        refs = refs[count:]
    return groups, refs


def fold_sublanes(values):
    rows, lanes = values.shape
    return jnp.max(values.reshape(rows // 8, 8, lanes), axis=0)


def fold_lanes(values):
    return jnp.concatenate(
        [
            jnp.max(jnp.transpose(values[first : first + 128]), axis=0, keepdims=True)
            for first in range(0, values.shape[0], 128)
        ],
        axis=0,
    )


def row_slices(block):
    slices = []
    for first, part in unit_parts(block):
        count = part.shape[0]
        for row in range(0, count, TILE):
            size = min(TILE, count - row)
            slices.append((first + row, part.at[row : row + size]))
    return slices


def plane_kernel(rows, counts, with_self, own_ref, *refs):
    blocks, refs = take(refs, counts)
    best_ref, column_refs = refs[-1 - len(counts)], refs[-len(counts) :]
    own_tags = tag_rows(own_ref)
    for block, column_ref in zip(blocks, column_refs):
        column_ref[...] = tag_columns(block[0], rows)
    for tile in range(0, rows, TILE):
        lanes = own_ref[PAD + tile : PAD + tile + TILE, :]
        best = [jnp.full((8, 128), -1.0, jnp.float32) for _ in range(0, TILE, 128)]
        for which, (block, column_ref) in enumerate(zip(blocks, column_refs)):
            for first, part in row_slices(block):
                count = part.shape[0]
                found = dot_rows(part[...], lanes)
                column = column_ref[first : first + count, :]
                for n in range(TILE // 128):
                    lane = tile + n * 128
                    match = column == own_tags[lane // 128 : lane // 128 + 1]
                    if with_self and which == 0 and first < lane + 128 and lane < first + count:
                        row_id = lax.broadcasted_iota(jnp.int32, (count, 128), 0) + first
                        lane_id = lax.broadcasted_iota(jnp.int32, (count, 128), 1) + lane
                        match = match & (row_id != lane_id)
                    masked = jnp.where(match, found[:, n * 128 : n * 128 + 128], -1.0)
                    best[n] = jnp.maximum(best[n], fold_sublanes(masked))
        for n in range(TILE // 128):
            place = pl.ds((tile + n * 128) // 128, 1)
            folded = jnp.max(best[n], axis=0, keepdims=True)
            if with_self:
                folded = jnp.maximum(folded, refs[0][place, :])
            best_ref[place, :] = folded


def cross_kernel(rows, index, counts, tags_ref, away_ref, *refs):
    blocks, refs = take(refs, counts)
    columns, refs = refs[:PLANE], refs[PLANE:]
    away_before, plane_before, away_best, plane_best = refs
    away_tags = tag_rows(tags_ref)
    away = away_ref if index else away_ref.at[PAD:]
    away_rows = away.shape[0]
    best = [jnp.full((8, 128), -1.0, jnp.float32) for _ in range(0, away_rows, 128)]
    for which in range(PLANE):
        for first, part in row_slices(blocks[which]):
            count = part.shape[0]
            row_best = jnp.full((count, 128), -1.0, jnp.float32)
            for tile in range(0, away_rows, TILE):
                lanes = min(TILE, away_rows - tile)
                found = dot_rows(part[...], away[tile : tile + lanes, :])
                column = columns[which][first : first + count, :]
                for lane in range(tile, tile + lanes, 128):
                    row = (index * away_rows + lane) // 128
                    match = column == away_tags[row : row + 1]
                    masked = jnp.where(match, found[:, lane - tile : lane - tile + 128], -1.0)
                    row_best = jnp.maximum(row_best, masked)
                    best[lane // 128] = jnp.maximum(best[lane // 128], fold_sublanes(masked))
            place = pl.ds(first // 128, count // 128)
            folded = fold_lanes(row_best)
            plane_best[which, place, :] = jnp.maximum(folded, plane_before[which, place, :])
    away_best[...] = away_before[...]
    for n, values in enumerate(best):
        place = pl.ds(index * away_rows // 128 + n, 1)
        away_best[place, :] = jnp.max(values, axis=0, keepdims=True)


def small_cost():
    return pl.CostEstimate(flops=1, bytes_accessed=1, transcendentals=0)


def plane_steps(planes):
    if planes == 4:
        return [[(0, 2), (2, 3), (3, 1)], [(0, 1), (1, 2), (3, 0)]]
    steps = []
    for distance in range(1, planes // 2 + 1):
        if 2 * distance < planes:
            steps.append([(z, (z + distance) % planes) for z in range(planes)])
        else:
            steps.append([(z, z + distance) for z in range(distance)])
    return steps


def after(value, *others):
    return lax.optimization_barrier((value,) + others)[0]


def local(embeddings, owner_index, sub_label, run_start):
    rows, width = embeddings.shape
    peers = lax.axis_size("dp")
    planes = peers // PLANE
    me = lax.axis_index("dp")
    lanes = lanes_shape(rows)

    space = -(2 * rows + peers) % 2048
    ints = jnp.concatenate([owner_index, sub_label, run_start, jnp.zeros((space,), jnp.int32)])
    ints = ints.reshape(-1, 128)
    ways = ((1,), AWAY_CUT, MATE_CUT, NEAR_CUT)
    sizes = sum((cuts(rows, way) for way in ways), [])
    packed = pl.pallas_call(
        functools.partial(pack_kernel, rows),
        out_shape=tuple(jax.ShapeDtypeStruct((size, width), jnp.bfloat16) for size in sizes),
        in_specs=whole(2),
        out_specs=tuple(whole(len(sizes))),
        compiler_params=params(),
        cost_estimate=small_cost(),
        name="pack",
    )(embeddings, ints)
    own, to_away, to_mate, to_near = take(packed, [len(way) for way in ways])[0]

    def mate(value, distance):
        return lax.ppermute(value, "dp", [(i, i ^ distance) for i in range(peers)])

    away = []
    for n, step in enumerate(plane_steps(planes)):
        pairs = [(s * PLANE + j, t * PLANE + j) for s, t in step for j in range(PLANE)]
        parts = to_away if n else own
        if n > 1:
            parts = [after(part, away[-1][1][-1]) for part in parts]
        away.append((pairs, [lax.ppermute(part, "dp", pairs) for part in parts]))
    beside = [mate(part, 2) for part in to_mate]
    near = [mate(part, 1) for part in to_near]
    across = [mate(part, 1) for part in beside]

    columns = jax.ShapeDtypeStruct((rows, 128), jnp.float32)
    best, beside_columns, across_columns = pl.pallas_call(
        functools.partial(plane_kernel, rows, (len(beside), len(across)), False),
        out_shape=(lanes, columns, columns),
        in_specs=whole(1 + len(beside) + len(across)),
        out_specs=tuple(whole(3)),
        compiler_params=params(),
        cost_estimate=small_cost(),
        name="plane_far",
    )(own[0], *beside, *across)
    best, own_columns, near_columns = pl.pallas_call(
        functools.partial(plane_kernel, rows, (1, len(near)), True),
        out_shape=(lanes, columns, columns),
        in_specs=whole(3 + len(near)),
        out_specs=tuple(whole(3)),
        compiler_params=params(),
        cost_estimate=small_cost(),
        name="plane_near",
    )(own[0], own[0], *near, best)

    plane = (own[0], *near, *beside, *across)
    plane_columns = (own_columns, near_columns, beside_columns, across_columns)
    plane_best = jnp.full((PLANE,) + lanes.shape, -1.0, jnp.float32)
    counts = (1, len(near), len(beside), len(across))
    for step, (pairs, received) in enumerate(away):
        if step:
            plane_best = after(plane_best, best)
        away_best = jnp.full(lanes.shape, -1.0, jnp.float32)
        for n, part in enumerate(received):
            away_best, plane_best = pl.pallas_call(
                functools.partial(cross_kernel, rows, n, counts),
                out_shape=(lanes, jax.ShapeDtypeStruct(plane_best.shape, jnp.float32)),
                in_specs=whole(len(plane) + PLANE + 4),
                out_specs=tuple(whole(2)),
                compiler_params=params(),
                cost_estimate=small_cost(),
                name="cross",
            )(received[0], part, *plane, *plane_columns, away_best, plane_best)
        back = lax.ppermute(away_best, "dp", [(t, s) for s, t in pairs])
        if len(pairs) < peers:
            sources = sum(1 << z for z in {s // PLANE for s, _ in pairs})
            sent = (jnp.uint32(sources) >> (me // PLANE).astype(jnp.uint32)) & 1
            back = jnp.where(sent == 1, back, -1.0)
        best = jnp.maximum(best, back)
    best = best.reshape(-1)[:rows]
    best = jnp.maximum(best, plane_best[0].reshape(-1)[:rows])
    for n, distance in ((3, 3), (2, 2), (1, 1)):
        back = mate(plane_best[n], distance)
        best = jnp.maximum(best, back.reshape(-1)[:rows])
    return best


def solution(mesh):
    in_specs = (P(("groups", "dp"), None), P(("groups", "dp")), P(("groups", "dp")), P("groups"))
    out_specs = P(("groups", "dp"))
    return jax.shard_map(local, mesh=mesh, in_specs=in_specs, out_specs=out_specs, check_vma=False)
```

```python
import functools

import jax
import jax.numpy as jnp
from jax import lax
from jax.experimental import pallas as pl
from jax.experimental.pallas import tpu as pltpu
from jax.sharding import PartitionSpec as P

LABELS = 3
PLANE = 4
PAD = 16
BASE = 64.0
TILE = 256
AWAY_CUT = (2, 1)
MATE_CUT = (2, 1)
VMEM_LIMIT = 24 * 2**20


def whole(count):
    return [pl.BlockSpec(memory_space=pltpu.VMEM)] * count


def params():
    return pltpu.CompilerParams(vmem_limit_bytes=VMEM_LIMIT)


def cuts(rows, cut):
    return [rows * share // sum(cut) + (PAD if n == 0 else 0) for n, share in enumerate(cut)]


def lanes_shape(rows):
    return jax.ShapeDtypeStruct((-(-rows // 1024) * 8, 128), jnp.float32)


def pack_kernel(rows, embeddings_ref, ints_ref, *part_refs):
    label_row = rows // 128
    owner, label = ints_ref[0:8, :], ints_ref[label_row : label_row + 8, :]
    runs = ints_ref[2 * label_row : 2 * label_row + 1, :]
    first_owner = jnp.take_along_axis(jnp.broadcast_to(runs, owner.shape), owner, axis=1)
    tags = 1 + jnp.where(label == 0, first_owner * LABELS, owner * LABELS + label)
    tags = tags.astype(jnp.float32)
    high = jnp.floor(tags * (1.0 / BASE))
    digits = jnp.concatenate([high, tags - high * BASE], axis=0).astype(jnp.bfloat16)
    width = embeddings_ref.shape[1]
    digits = jnp.concatenate([digits, jnp.zeros((PAD, width - 128), jnp.bfloat16)], axis=1)
    places, first = [], 0
    for part_ref in part_refs:
        base = PAD if first == 0 else 0
        if base:
            part_ref[0:PAD, :] = digits
        count = part_ref.shape[0] - base
        places.append((part_ref, base - first, first, first + count))
        first = (first + count) % rows
    for row in range(0, rows, 128):
        values = embeddings_ref[row : row + 128, :]
        squares = jnp.sum(values * values, axis=1, keepdims=True)
        unit = (values * lax.rsqrt(squares + 1e-06)).astype(jnp.bfloat16)
        for part_ref, shift, start, stop in places:
            if start <= row < stop:
                part_ref[row + shift : row + shift + 128, :] = unit


def tag_rows(block_ref):
    digits = block_ref[0:PAD, 0:128].astype(jnp.float32)
    return digits[0:8] * BASE + digits[8:16]


def tag_columns(block_ref, rows):
    tags = tag_rows(block_ref)
    return jnp.concatenate(
        [jnp.transpose(jnp.broadcast_to(tags[n : n + 1], (128, 128))) for n in range(rows // 128)],
        axis=0,
    )


def dot_rows(values, lanes):
    return lax.dot_general(
        values, lanes, (((1,), (1,)), ((), ())), preferred_element_type=jnp.float32
    )


def unit_parts(refs):
    parts, first = [], 0
    for n, ref in enumerate(refs):
        part = ref if n else ref.at[PAD:]
        parts.append((first, part))
        first += part.shape[0]
    return parts


def take(refs, counts):
    groups = []
    for count in counts:
        groups.append(refs[:count])
        refs = refs[count:]
    return groups, refs


def fold_sublanes(values):
    rows, lanes = values.shape
    return jnp.max(values.reshape(rows // 8, 8, lanes), axis=0)


def fold_lanes(values):
    return jnp.concatenate(
        [
            jnp.max(jnp.transpose(values[first : first + 128]), axis=0, keepdims=True)
            for first in range(0, values.shape[0], 128)
        ],
        axis=0,
    )


def row_slices(block):
    slices = []
    for first, part in unit_parts(block):
        count = part.shape[0]
        for row in range(0, count, TILE):
            size = min(TILE, count - row)
            slices.append((first + row, part.at[row : row + size]))
    return slices


def plane_kernel(rows, counts, with_self, own_ref, *refs):
    blocks, refs = take(refs, counts)
    best_ref, column_refs = refs[-1 - len(counts)], refs[-len(counts) :]
    own_tags = tag_rows(own_ref)
    for block, column_ref in zip(blocks, column_refs):
        column_ref[...] = tag_columns(block[0], rows)
    for tile in range(0, rows, TILE):
        lanes = own_ref[PAD + tile : PAD + tile + TILE, :]
        best = [jnp.full((8, 128), -1.0, jnp.float32) for _ in range(0, TILE, 128)]
        for which, (block, column_ref) in enumerate(zip(blocks, column_refs)):
            for first, part in row_slices(block):
                count = part.shape[0]
                found = dot_rows(part[...], lanes)
                column = column_ref[first : first + count, :]
                for n in range(TILE // 128):
                    lane = tile + n * 128
                    match = column == own_tags[lane // 128 : lane // 128 + 1]
                    if with_self and which == 0 and first < lane + 128 and lane < first + count:
                        row_id = lax.broadcasted_iota(jnp.int32, (count, 128), 0) + first
                        lane_id = lax.broadcasted_iota(jnp.int32, (count, 128), 1) + lane
                        match = match & (row_id != lane_id)
                    masked = jnp.where(match, found[:, n * 128 : n * 128 + 128], -1.0)
                    best[n] = jnp.maximum(best[n], fold_sublanes(masked))
        for n in range(TILE // 128):
            place = pl.ds((tile + n * 128) // 128, 1)
            folded = jnp.max(best[n], axis=0, keepdims=True)
            if with_self:
                folded = jnp.maximum(folded, refs[0][place, :])
            best_ref[place, :] = folded


def cross_kernel(rows, start, counts, tags_ref, away_ref, *refs):
    blocks, refs = take(refs, counts)
    columns, refs = refs[:PLANE], refs[PLANE:]
    away_before, plane_before, away_best, plane_best = refs
    away_tags = tag_rows(tags_ref)
    away = away_ref if start else away_ref.at[PAD:]
    away_rows = away.shape[0]
    best = [jnp.full((8, 128), -1.0, jnp.float32) for _ in range(0, away_rows, 128)]
    for which in range(PLANE):
        for first, part in row_slices(blocks[which]):
            count = part.shape[0]
            row_best = jnp.full((count, 128), -1.0, jnp.float32)
            for tile in range(0, away_rows, TILE):
                lanes = min(TILE, away_rows - tile)
                found = dot_rows(part[...], away[tile : tile + lanes, :])
                column = columns[which][first : first + count, :]
                for lane in range(tile, tile + lanes, 128):
                    row = (start + lane) // 128
                    match = column == away_tags[row : row + 1]
                    masked = jnp.where(match, found[:, lane - tile : lane - tile + 128], -1.0)
                    row_best = jnp.maximum(row_best, masked)
                    best[lane // 128] = jnp.maximum(best[lane // 128], fold_sublanes(masked))
            place = pl.ds(first // 128, count // 128)
            folded = fold_lanes(row_best)
            plane_best[which, place, :] = jnp.maximum(folded, plane_before[which, place, :])
    away_best[...] = away_before[...]
    for n, values in enumerate(best):
        place = pl.ds(start // 128 + n, 1)
        away_best[place, :] = jnp.max(values, axis=0, keepdims=True)


def small_cost():
    return pl.CostEstimate(flops=1, bytes_accessed=1, transcendentals=0)


def plane_steps(planes):
    if planes == 4:
        return [(2, 0, 3, 1), (1, 2, 3, 0)]
    return [
        [(z + distance) % planes for z in range(planes)]
        for distance in range(1, planes // 2 + 1)
    ]


def after(value, *others):
    return lax.optimization_barrier((value,) + others)[0]


def local(embeddings, owner_index, sub_label, run_start):
    rows, width = embeddings.shape
    peers = lax.axis_size("dp")
    planes = peers // PLANE
    lanes = lanes_shape(rows)

    space = -(2 * rows + peers) % 2048
    ints = jnp.concatenate([owner_index, sub_label, run_start, jnp.zeros((space,), jnp.int32)])
    ints = ints.reshape(-1, 128)
    ways = ((1,), AWAY_CUT, MATE_CUT)
    sizes = sum((cuts(rows, way) for way in ways), [])
    packed = pl.pallas_call(
        functools.partial(pack_kernel, rows),
        out_shape=tuple(jax.ShapeDtypeStruct((size, width), jnp.bfloat16) for size in sizes),
        in_specs=whole(2),
        out_specs=tuple(whole(len(sizes))),
        compiler_params=params(),
        cost_estimate=small_cost(),
        name="pack",
    )(embeddings, ints)
    own, to_away, to_mate = take(packed, [len(way) for way in ways])[0]

    def mate(value, distance):
        return lax.ppermute(value, "dp", [(i, i ^ distance) for i in range(peers)])

    away = []
    for n, step in enumerate(plane_steps(planes)):
        pairs = [(z * PLANE + j, t * PLANE + j) for z, t in enumerate(step) for j in range(PLANE)]
        parts = to_away if n else own
        if n > 1:
            parts = [after(part, away[-1][1][-1]) for part in parts]
        away.append((pairs, [lax.ppermute(part, "dp", pairs) for part in parts]))
    beside = [mate(part, 2) for part in to_mate]
    near = [mate(part, 1) for part in to_mate]
    across = [mate(part, 1) for part in beside]

    columns = jax.ShapeDtypeStruct((rows, 128), jnp.float32)
    best, beside_columns, across_columns = pl.pallas_call(
        functools.partial(plane_kernel, rows, (len(beside), len(across)), False),
        out_shape=(lanes, columns, columns),
        in_specs=whole(1 + len(beside) + len(across)),
        out_specs=tuple(whole(3)),
        compiler_params=params(),
        cost_estimate=small_cost(),
        name="plane_far",
    )(own[0], *beside, *across)
    best, own_columns, near_columns = pl.pallas_call(
        functools.partial(plane_kernel, rows, (1, len(near)), True),
        out_shape=(lanes, columns, columns),
        in_specs=whole(3 + len(near)),
        out_specs=tuple(whole(3)),
        compiler_params=params(),
        cost_estimate=small_cost(),
        name="plane_near",
    )(own[0], own[0], *near, best)

    plane = (own[0], *near, *beside, *across)
    plane_columns = (own_columns, near_columns, beside_columns, across_columns)
    plane_best = jnp.full((PLANE,) + lanes.shape, -1.0, jnp.float32)
    counts = (1, len(near), len(beside), len(across))
    backs = []
    for pairs, received in away:
        away_best = jnp.full(lanes.shape, -1.0, jnp.float32)
        start = 0
        for part in received:
            if backs and part is received[-1]:
                plane_best = after(plane_best, backs[-1])
            away_best, plane_best = pl.pallas_call(
                functools.partial(cross_kernel, rows, start, counts),
                out_shape=(lanes, jax.ShapeDtypeStruct(plane_best.shape, jnp.float32)),
                in_specs=whole(len(plane) + PLANE + 4),
                out_specs=tuple(whole(2)),
                compiler_params=params(),
                cost_estimate=small_cost(),
                name="cross",
            )(received[0], part, *plane, *plane_columns, away_best, plane_best)
            start += part.shape[0] - (0 if start else PAD)
        back = lax.ppermute(away_best, "dp", [(t, s) for s, t in pairs])
        backs.append(back)
    best = jnp.maximum(best, plane_best[0]).reshape(-1)[:rows]
    for back in backs:
        best = jnp.maximum(best, back.reshape(-1)[:rows])
    for n, distance in ((3, 3), (2, 2), (1, 1)):
        back = mate(plane_best[n], distance)
        best = jnp.maximum(best, back.reshape(-1)[:rows])
    return best


def solution(mesh):
    in_specs = (P(("groups", "dp"), None), P(("groups", "dp")), P(("groups", "dp")), P("groups"))
    out_specs = P(("groups", "dp"))
    return jax.shard_map(local, mesh=mesh, in_specs=in_specs, out_specs=out_specs, check_vma=False)
```

```python
import functools

import jax
import jax.numpy as jnp
from jax import lax
from jax.experimental import pallas as pl
from jax.experimental.pallas import tpu as pltpu
from jax.sharding import PartitionSpec as P

LABELS = 3
PLANE = 4
PAD = 16
BASE = 64.0
TILE = 256
AWAY_CUT = (5, 1)
MATE_CUT = (2, 1)
VMEM_LIMIT = 24 * 2**20


def whole(count):
    return [pl.BlockSpec(memory_space=pltpu.VMEM)] * count


def params():
    return pltpu.CompilerParams(vmem_limit_bytes=VMEM_LIMIT)


def cuts(rows, cut):
    return [rows * share // sum(cut) + (PAD if n == 0 else 0) for n, share in enumerate(cut)]


def lanes_shape(rows):
    return jax.ShapeDtypeStruct((-(-rows // 1024) * 8, 128), jnp.float32)


def pack_kernel(rows, embeddings_ref, ints_ref, *part_refs):
    label_row = rows // 128
    owner, label = ints_ref[0:8, :], ints_ref[label_row : label_row + 8, :]
    runs = ints_ref[2 * label_row : 2 * label_row + 1, :]
    first_owner = jnp.take_along_axis(jnp.broadcast_to(runs, owner.shape), owner, axis=1)
    tags = 1 + jnp.where(label == 0, first_owner * LABELS, owner * LABELS + label)
    tags = tags.astype(jnp.float32)
    high = jnp.floor(tags * (1.0 / BASE))
    digits = jnp.concatenate([high, tags - high * BASE], axis=0).astype(jnp.bfloat16)
    width = embeddings_ref.shape[1]
    digits = jnp.concatenate([digits, jnp.zeros((PAD, width - 128), jnp.bfloat16)], axis=1)
    places, first = [], 0
    for part_ref in part_refs:
        base = PAD if first == 0 else 0
        if base:
            part_ref[0:PAD, :] = digits
        count = part_ref.shape[0] - base
        places.append((part_ref, base - first, first, first + count))
        first = (first + count) % rows
    for row in range(0, rows, 128):
        values = embeddings_ref[row : row + 128, :]
        squares = jnp.sum(values * values, axis=1, keepdims=True)
        unit = (values * lax.rsqrt(squares + 1e-06)).astype(jnp.bfloat16)
        for part_ref, shift, start, stop in places:
            if start <= row < stop:
                part_ref[row + shift : row + shift + 128, :] = unit


def tag_rows(block_ref):
    digits = block_ref[0:PAD, 0:128].astype(jnp.float32)
    return digits[0:8] * BASE + digits[8:16]


def tag_columns(block_ref, rows):
    tags = tag_rows(block_ref)
    return jnp.concatenate(
        [jnp.transpose(jnp.broadcast_to(tags[n : n + 1], (128, 128))) for n in range(rows // 128)],
        axis=0,
    )


def dot_rows(values, lanes):
    return lax.dot_general(
        values, lanes, (((1,), (1,)), ((), ())), preferred_element_type=jnp.float32
    )


def unit_parts(refs):
    parts, first = [], 0
    for n, ref in enumerate(refs):
        part = ref if n else ref.at[PAD:]
        parts.append((first, part))
        first += part.shape[0]
    return parts


def take(refs, counts):
    groups = []
    for count in counts:
        groups.append(refs[:count])
        refs = refs[count:]
    return groups, refs


def fold_sublanes(values):
    rows, lanes = values.shape
    return jnp.max(values.reshape(rows // 8, 8, lanes), axis=0)


def fold_lanes(values):
    return jnp.concatenate(
        [
            jnp.max(jnp.transpose(values[first : first + 128]), axis=0, keepdims=True)
            for first in range(0, values.shape[0], 128)
        ],
        axis=0,
    )


def row_slices(block):
    slices = []
    for first, part in unit_parts(block):
        count = part.shape[0]
        for row in range(0, count, TILE):
            size = min(TILE, count - row)
            slices.append((first + row, part.at[row : row + size]))
    return slices


def plane_kernel(rows, counts, with_self, own_ref, *refs):
    blocks, refs = take(refs, counts)
    best_ref, column_refs = refs[-1 - len(counts)], refs[-len(counts) :]
    own_tags = tag_rows(own_ref)
    for block, column_ref in zip(blocks, column_refs):
        column_ref[...] = tag_columns(block[0], rows)
    for tile in range(0, rows, TILE):
        lanes = own_ref[PAD + tile : PAD + tile + TILE, :]
        best = [jnp.full((8, 128), -1.0, jnp.float32) for _ in range(0, TILE, 128)]
        for which, (block, column_ref) in enumerate(zip(blocks, column_refs)):
            for first, part in row_slices(block):
                count = part.shape[0]
                found = dot_rows(part[...], lanes)
                column = column_ref[first : first + count, :]
                for n in range(TILE // 128):
                    lane = tile + n * 128
                    match = column == own_tags[lane // 128 : lane // 128 + 1]
                    if with_self and which == 0 and first < lane + 128 and lane < first + count:
                        row_id = lax.broadcasted_iota(jnp.int32, (count, 128), 0) + first
                        lane_id = lax.broadcasted_iota(jnp.int32, (count, 128), 1) + lane
                        match = match & (row_id != lane_id)
                    masked = jnp.where(match, found[:, n * 128 : n * 128 + 128], -1.0)
                    best[n] = jnp.maximum(best[n], fold_sublanes(masked))
        for n in range(TILE // 128):
            place = pl.ds((tile + n * 128) // 128, 1)
            folded = jnp.max(best[n], axis=0, keepdims=True)
            if with_self:
                folded = jnp.maximum(folded, refs[0][place, :])
            best_ref[place, :] = folded


def cross_kernel(rows, start, counts, tags_ref, away_ref, *refs):
    blocks, refs = take(refs, counts)
    columns, refs = refs[:PLANE], refs[PLANE:]
    away_before, away_best = refs[0], refs[PLANE + 1]
    plane_before, plane_best = refs[1 : PLANE + 1], refs[PLANE + 2 :]
    away_tags = tag_rows(tags_ref)
    away = away_ref if start else away_ref.at[PAD:]
    away_rows = away.shape[0]
    best = [jnp.full((8, 128), -1.0, jnp.float32) for _ in range(0, away_rows, 128)]
    for which in range(PLANE):
        for first, part in row_slices(blocks[which]):
            count = part.shape[0]
            row_best = jnp.full((count, 128), -1.0, jnp.float32)
            for tile in range(0, away_rows, TILE):
                lanes = min(TILE, away_rows - tile)
                found = dot_rows(part[...], away[tile : tile + lanes, :])
                column = columns[which][first : first + count, :]
                for lane in range(tile, tile + lanes, 128):
                    row = (start + lane) // 128
                    match = column == away_tags[row : row + 1]
                    masked = jnp.where(match, found[:, lane - tile : lane - tile + 128], -1.0)
                    row_best = jnp.maximum(row_best, masked)
                    best[lane // 128] = jnp.maximum(best[lane // 128], fold_sublanes(masked))
            place = pl.ds(first // 128, count // 128)
            folded = fold_lanes(row_best)
            plane_best[which][place, :] = jnp.maximum(folded, plane_before[which][place, :])
    away_best[...] = away_before[...]
    for n, values in enumerate(best):
        place = pl.ds(start // 128 + n, 1)
        away_best[place, :] = jnp.max(values, axis=0, keepdims=True)


def small_cost():
    return pl.CostEstimate(flops=1, bytes_accessed=1, transcendentals=0)


def plane_steps(planes):
    if planes == 4:
        return [(2, 0, 3, 1), (1, 2, 3, 0)]
    return [
        [(z + distance) % planes for z in range(planes)]
        for distance in range(1, planes // 2 + 1)
    ]


def after(value, *others):
    return lax.optimization_barrier((value,) + others)[0]


def local(embeddings, owner_index, sub_label, run_start):
    rows, width = embeddings.shape
    peers = lax.axis_size("dp")
    planes = peers // PLANE
    lanes = lanes_shape(rows)

    space = -(2 * rows + peers) % 2048
    ints = jnp.concatenate([owner_index, sub_label, run_start, jnp.zeros((space,), jnp.int32)])
    ints = ints.reshape(-1, 128)
    ways = ((1,), AWAY_CUT, MATE_CUT)
    sizes = sum((cuts(rows, way) for way in ways), [])
    packed = pl.pallas_call(
        functools.partial(pack_kernel, rows),
        out_shape=tuple(jax.ShapeDtypeStruct((size, width), jnp.bfloat16) for size in sizes),
        in_specs=whole(2),
        out_specs=tuple(whole(len(sizes))),
        compiler_params=params(),
        cost_estimate=small_cost(),
        name="pack",
    )(embeddings, ints)
    own, to_away, to_mate = take(packed, [len(way) for way in ways])[0]

    def mate(value, distance):
        return lax.ppermute(value, "dp", [(i, i ^ distance) for i in range(peers)])

    away = []
    for n, step in enumerate(plane_steps(planes)):
        pairs = [(z * PLANE + j, t * PLANE + j) for z, t in enumerate(step) for j in range(PLANE)]
        parts = to_away if n else own
        if n > 1:
            parts = [after(part, away[-1][1][-1]) for part in parts]
        away.append((pairs, [lax.ppermute(part, "dp", pairs) for part in parts]))
    beside = [mate(part, 2) for part in to_mate]
    near = [mate(part, 1) for part in to_mate]
    across = [mate(after(part, away[0][1][0]), 1) for part in beside]

    columns = jax.ShapeDtypeStruct((rows, 128), jnp.float32)
    best, beside_columns, across_columns = pl.pallas_call(
        functools.partial(plane_kernel, rows, (len(beside), len(across)), False),
        out_shape=(lanes, columns, columns),
        in_specs=whole(1 + len(beside) + len(across)),
        out_specs=tuple(whole(3)),
        compiler_params=params(),
        cost_estimate=small_cost(),
        name="plane_far",
    )(own[0], *beside, *across)
    best, own_columns, near_columns = pl.pallas_call(
        functools.partial(plane_kernel, rows, (1, len(near)), True),
        out_shape=(lanes, columns, columns),
        in_specs=whole(3 + len(near)),
        out_specs=tuple(whole(3)),
        compiler_params=params(),
        cost_estimate=small_cost(),
        name="plane_near",
    )(own[0], own[0], *near, best)

    plane = (own[0], *near, *beside, *across)
    plane_columns = (own_columns, near_columns, beside_columns, across_columns)
    plane_best = [jnp.full(lanes.shape, -1.0, jnp.float32)] * PLANE
    counts = (1, len(near), len(beside), len(across))
    backs = []
    for pairs, received in away:
        away_best = jnp.full(lanes.shape, -1.0, jnp.float32)
        start = 0
        for part in received:
            if backs and part is received[-1]:
                away_best = after(away_best, backs[-1])
            away_best, *plane_best = pl.pallas_call(
                functools.partial(cross_kernel, rows, start, counts),
                out_shape=(lanes,) * (PLANE + 1),
                in_specs=whole(len(plane) + 2 * PLANE + 3),
                out_specs=tuple(whole(PLANE + 1)),
                compiler_params=params(),
                cost_estimate=small_cost(),
                name="cross",
            )(received[0], part, *plane, *plane_columns, away_best, *plane_best)
            start += part.shape[0] - (0 if start else PAD)
        back = lax.ppermute(away_best, "dp", [(t, s) for s, t in pairs])
        backs.append(back)
    best = jnp.maximum(best, plane_best[0]).reshape(-1)[:rows]
    for back in backs:
        best = jnp.maximum(best, back.reshape(-1)[:rows])
    for n, distance in ((3, 3), (2, 2), (1, 1)):
        back = mate(plane_best[n], distance)
        best = jnp.maximum(best, back.reshape(-1)[:rows])
    return best


def solution(mesh):
    in_specs = (P(("groups", "dp"), None), P(("groups", "dp")), P(("groups", "dp")), P("groups"))
    out_specs = P(("groups", "dp"))
    return jax.shard_map(local, mesh=mesh, in_specs=in_specs, out_specs=out_specs, check_vma=False)
```

```python
import functools

import jax
import jax.numpy as jnp
from jax import lax
from jax.experimental import pallas as pl
from jax.experimental.pallas import tpu as pltpu
from jax.sharding import PartitionSpec as P

LABELS = 3
PLANE = 4
PAD = 16
BASE = 64.0
TILE = 256
AWAY_CUT = (4, 2)
MATE_CUT = (1, 1, 1)
VMEM_LIMIT = 24 * 2**20


def whole(count):
    return [pl.BlockSpec(memory_space=pltpu.VMEM)] * count


def params():
    return pltpu.CompilerParams(vmem_limit_bytes=VMEM_LIMIT)


def cuts(rows, cut):
    return [rows * share // sum(cut) + (PAD if n == 0 else 0) for n, share in enumerate(cut)]


def lanes_shape(rows):
    return jax.ShapeDtypeStruct((-(-rows // 1024) * 8, 128), jnp.float32)


def pack_kernel(rows, embeddings_ref, ints_ref, *part_refs):
    label_row = rows // 128
    owner, label = ints_ref[0:8, :], ints_ref[label_row : label_row + 8, :]
    runs = ints_ref[2 * label_row : 2 * label_row + 1, :]
    first_owner = jnp.take_along_axis(jnp.broadcast_to(runs, owner.shape), owner, axis=1)
    tags = 1 + jnp.where(label == 0, first_owner * LABELS, owner * LABELS + label)
    tags = tags.astype(jnp.float32)
    high = jnp.floor(tags * (1.0 / BASE))
    digits = jnp.concatenate([high, tags - high * BASE], axis=0).astype(jnp.bfloat16)
    width = embeddings_ref.shape[1]
    digits = jnp.concatenate([digits, jnp.zeros((PAD, width - 128), jnp.bfloat16)], axis=1)
    places, first = [], 0
    for part_ref in part_refs:
        base = PAD if first == 0 else 0
        if base:
            part_ref[0:PAD, :] = digits
        count = part_ref.shape[0] - base
        places.append((part_ref, base - first, first, first + count))
        first = (first + count) % rows
    for row in range(0, rows, 128):
        values = embeddings_ref[row : row + 128, :]
        squares = jnp.sum(values * values, axis=1, keepdims=True)
        unit = (values * lax.rsqrt(squares + 1e-06)).astype(jnp.bfloat16)
        for part_ref, shift, start, stop in places:
            if start <= row < stop:
                part_ref[row + shift : row + shift + 128, :] = unit


def tag_rows(block_ref):
    digits = block_ref[0:PAD, 0:128].astype(jnp.float32)
    return digits[0:8] * BASE + digits[8:16]


def tag_columns(block_ref, rows):
    tags = tag_rows(block_ref)
    return jnp.concatenate(
        [jnp.transpose(jnp.broadcast_to(tags[n : n + 1], (128, 128))) for n in range(rows // 128)],
        axis=0,
    )


def dot_rows(values, lanes):
    return lax.dot_general(
        values, lanes, (((1,), (1,)), ((), ())), preferred_element_type=jnp.float32
    )


def unit_parts(refs):
    parts, first = [], 0
    for n, ref in enumerate(refs):
        part = ref if n else ref.at[PAD:]
        parts.append((first, part))
        first += part.shape[0]
    return parts


def take(refs, counts):
    groups = []
    for count in counts:
        groups.append(refs[:count])
        refs = refs[count:]
    return groups, refs


def fold_sublanes(values):
    rows, lanes = values.shape
    return jnp.max(values.reshape(rows // 8, 8, lanes), axis=0)


def fold_lanes(values):
    return jnp.concatenate(
        [
            jnp.max(jnp.transpose(values[first : first + 128]), axis=0, keepdims=True)
            for first in range(0, values.shape[0], 128)
        ],
        axis=0,
    )


def row_slices(block):
    slices = []
    for first, part in unit_parts(block):
        count = part.shape[0]
        for row in range(0, count, TILE):
            size = min(TILE, count - row)
            slices.append((first + row, part.at[row : row + size]))
    return slices


def plane_kernel(rows, counts, with_self, own_ref, *refs):
    blocks, refs = take(refs, counts)
    best_ref, column_refs = refs[-1 - len(counts)], refs[-len(counts) :]
    own_tags = tag_rows(own_ref)
    for block, column_ref in zip(blocks, column_refs):
        column_ref[...] = tag_columns(block[0], rows)
    for tile in range(0, rows, TILE):
        lanes = own_ref[PAD + tile : PAD + tile + TILE, :]
        best = [jnp.full((8, 128), -1.0, jnp.float32) for _ in range(0, TILE, 128)]
        for which, (block, column_ref) in enumerate(zip(blocks, column_refs)):
            for first, part in row_slices(block):
                count = part.shape[0]
                found = dot_rows(part[...], lanes)
                column = column_ref[first : first + count, :]
                for n in range(TILE // 128):
                    lane = tile + n * 128
                    match = column == own_tags[lane // 128 : lane // 128 + 1]
                    if with_self and which == 0 and first < lane + 128 and lane < first + count:
                        row_id = lax.broadcasted_iota(jnp.int32, (count, 128), 0) + first
                        lane_id = lax.broadcasted_iota(jnp.int32, (count, 128), 1) + lane
                        match = match & (row_id != lane_id)
                    masked = jnp.where(match, found[:, n * 128 : n * 128 + 128], -1.0)
                    best[n] = jnp.maximum(best[n], fold_sublanes(masked))
        for n in range(TILE // 128):
            place = pl.ds((tile + n * 128) // 128, 1)
            folded = jnp.max(best[n], axis=0, keepdims=True)
            if with_self:
                folded = jnp.maximum(folded, refs[0][place, :])
            best_ref[place, :] = folded


def cross_kernel(rows, start, counts, tags_ref, away_ref, *refs):
    blocks, refs = take(refs, counts)
    columns, refs = refs[:PLANE], refs[PLANE:]
    away_before, away_best = refs[0], refs[PLANE + 1]
    plane_before, plane_best = refs[1 : PLANE + 1], refs[PLANE + 2 :]
    away_tags = tag_rows(tags_ref)
    away = away_ref if start else away_ref.at[PAD:]
    away_rows = away.shape[0]
    best = [jnp.full((8, 128), -1.0, jnp.float32) for _ in range(0, away_rows, 128)]
    for which in range(PLANE):
        for first, part in row_slices(blocks[which]):
            count = part.shape[0]
            row_best = jnp.full((count, 128), -1.0, jnp.float32)
            for tile in range(0, away_rows, TILE):
                lanes = min(TILE, away_rows - tile)
                found = dot_rows(part[...], away[tile : tile + lanes, :])
                column = columns[which][first : first + count, :]
                for lane in range(tile, tile + lanes, 128):
                    row = (start + lane) // 128
                    match = column == away_tags[row : row + 1]
                    masked = jnp.where(match, found[:, lane - tile : lane - tile + 128], -1.0)
                    row_best = jnp.maximum(row_best, masked)
                    best[lane // 128] = jnp.maximum(best[lane // 128], fold_sublanes(masked))
            place = pl.ds(first // 128, count // 128)
            folded = fold_lanes(row_best)
            plane_best[which][place, :] = jnp.maximum(folded, plane_before[which][place, :])
    away_best[...] = away_before[...]
    for n, values in enumerate(best):
        place = pl.ds(start // 128 + n, 1)
        away_best[place, :] = jnp.max(values, axis=0, keepdims=True)


def small_cost():
    return pl.CostEstimate(flops=1, bytes_accessed=1, transcendentals=0)


def plane_steps(planes):
    if planes == 4:
        return [(2, 0, 3, 1), (1, 2, 3, 0)]
    return [
        [(z + distance) % planes for z in range(planes)]
        for distance in range(1, planes // 2 + 1)
    ]


def after(value, *others):
    return lax.optimization_barrier((value,) + others)[0]


def local(embeddings, owner_index, sub_label, run_start):
    rows, width = embeddings.shape
    peers = lax.axis_size("dp")
    planes = peers // PLANE
    lanes = lanes_shape(rows)

    space = -(2 * rows + peers) % 2048
    ints = jnp.concatenate([owner_index, sub_label, run_start, jnp.zeros((space,), jnp.int32)])
    ints = ints.reshape(-1, 128)
    ways = ((1,), AWAY_CUT, MATE_CUT)
    sizes = sum((cuts(rows, way) for way in ways), [])
    packed = pl.pallas_call(
        functools.partial(pack_kernel, rows),
        out_shape=tuple(jax.ShapeDtypeStruct((size, width), jnp.bfloat16) for size in sizes),
        in_specs=whole(2),
        out_specs=tuple(whole(len(sizes))),
        compiler_params=params(),
        cost_estimate=small_cost(),
        name="pack",
    )(embeddings, ints)
    own, to_away, to_mate = take(packed, [len(way) for way in ways])[0]

    def mate(value, distance):
        return lax.ppermute(value, "dp", [(i, i ^ distance) for i in range(peers)])

    away = []
    for n, step in enumerate(plane_steps(planes)):
        pairs = [(z * PLANE + j, t * PLANE + j) for z, t in enumerate(step) for j in range(PLANE)]
        parts = to_away if n else own
        if n > 1:
            parts = [after(part, away[-1][1][-1]) for part in parts]
        away.append((pairs, [lax.ppermute(part, "dp", pairs) for part in parts]))
    beside = [mate(part, 2) for part in to_mate]
    near = [mate(part, 1) for part in to_mate]
    across = [mate(after(part, away[0][1][0]), 1) for part in beside]

    columns = jax.ShapeDtypeStruct((rows, 128), jnp.float32)
    best, beside_columns, across_columns = pl.pallas_call(
        functools.partial(plane_kernel, rows, (len(beside), len(across)), False),
        out_shape=(lanes, columns, columns),
        in_specs=whole(1 + len(beside) + len(across)),
        out_specs=tuple(whole(3)),
        compiler_params=params(),
        cost_estimate=small_cost(),
        name="plane_far",
    )(own[0], *beside, *across)
    best, own_columns, near_columns = pl.pallas_call(
        functools.partial(plane_kernel, rows, (1, len(near)), True),
        out_shape=(lanes, columns, columns),
        in_specs=whole(3 + len(near)),
        out_specs=tuple(whole(3)),
        compiler_params=params(),
        cost_estimate=small_cost(),
        name="plane_near",
    )(own[0], own[0], *near, best)

    plane = (own[0], *near, *beside, *across)
    plane_columns = (own_columns, near_columns, beside_columns, across_columns)
    plane_best = [jnp.full(lanes.shape, -1.0, jnp.float32)] * PLANE
    counts = (1, len(near), len(beside), len(across))
    backs = []
    for pairs, received in away:
        away_best = jnp.full(lanes.shape, -1.0, jnp.float32)
        start = 0
        for part in received:
            if backs and part is received[-1]:
                away_best = after(away_best, backs[-1])
            away_best, *plane_best = pl.pallas_call(
                functools.partial(cross_kernel, rows, start, counts),
                out_shape=(lanes,) * (PLANE + 1),
                in_specs=whole(len(plane) + 2 * PLANE + 3),
                out_specs=tuple(whole(PLANE + 1)),
                compiler_params=params(),
                cost_estimate=small_cost(),
                name="cross",
            )(received[0], part, *plane, *plane_columns, away_best, *plane_best)
            start += part.shape[0] - (0 if start else PAD)
        back = lax.ppermute(away_best, "dp", [(t, s) for s, t in pairs])
        backs.append(back)
    best = jnp.maximum(best, plane_best[0]).reshape(-1)[:rows]
    for back in backs:
        best = jnp.maximum(best, back.reshape(-1)[:rows])
    for n, distance in ((3, 3), (2, 2), (1, 1)):
        back = mate(plane_best[n], distance)
        best = jnp.maximum(best, back.reshape(-1)[:rows])
    return best


def solution(mesh):
    in_specs = (P(("groups", "dp"), None), P(("groups", "dp")), P(("groups", "dp")), P("groups"))
    out_specs = P(("groups", "dp"))
    return jax.shard_map(local, mesh=mesh, in_specs=in_specs, out_specs=out_specs, check_vma=False)
```

```python
import functools

import jax
import jax.numpy as jnp
from jax import lax
from jax.experimental import pallas as pl
from jax.experimental.pallas import tpu as pltpu
from jax.sharding import PartitionSpec as P

LABELS = 3
PLANE = 4
PAD = 16
BASE = 64.0
TILE = 256
FIRST = 512
VMEM_LIMIT = 24 * 2**20


def whole(count):
    return [pl.BlockSpec(memory_space=pltpu.VMEM)] * count


def params():
    return pltpu.CompilerParams(vmem_limit_bytes=VMEM_LIMIT)


def lanes_shape(rows):
    return jax.ShapeDtypeStruct((-(-rows // 1024) * 8, 128), jnp.float32)


def unit_rows(values):
    squares = jnp.sum(values * values, axis=1, keepdims=True)
    return (values * lax.rsqrt(squares + 1e-06)).astype(jnp.bfloat16)


def first_kernel(embeddings_ref, first_ref):
    for row in range(0, first_ref.shape[0], 128):
        first_ref[row : row + 128, :] = unit_rows(embeddings_ref[row : row + 128, :])


def rest_kernel(rows, embeddings_ref, ints_ref, first_ref, last_ref, head_ref, tail_ref):
    label_row = rows // 128
    owner, label = ints_ref[0:8, :], ints_ref[label_row : label_row + 8, :]
    runs = ints_ref[2 * label_row : 2 * label_row + 1, :]
    first_owner = jnp.take_along_axis(jnp.broadcast_to(runs, owner.shape), owner, axis=1)
    tags = 1 + jnp.where(label == 0, first_owner * LABELS, owner * LABELS + label)
    tags = tags.astype(jnp.float32)
    high = jnp.floor(tags * (1.0 / BASE))
    digits = jnp.concatenate([high, tags - high * BASE], axis=0).astype(jnp.bfloat16)
    width = embeddings_ref.shape[1]
    digits = jnp.concatenate([digits, jnp.zeros((PAD, width - 128), jnp.bfloat16)], axis=1)
    last_ref[0:PAD, :] = digits
    head_ref[0:PAD, :] = digits
    head_ref[PAD:, :] = first_ref[...]
    first = first_ref.shape[0]
    for row in range(0, rows - first, 128):
        unit = unit_rows(embeddings_ref[first + row : first + row + 128, :])
        last_ref[PAD + row : PAD + row + 128, :] = unit
        tail_ref[row : row + 128, :] = unit


def tag_rows(block_ref):
    digits = block_ref[0:PAD, 0:128].astype(jnp.float32)
    return digits[0:8] * BASE + digits[8:16]


def tag_columns(block_ref, rows):
    tags = tag_rows(block_ref)
    return jnp.concatenate(
        [jnp.transpose(jnp.broadcast_to(tags[n : n + 1], (128, 128))) for n in range(rows // 128)],
        axis=0,
    )


def dot_rows(values, lanes):
    return lax.dot_general(
        values, lanes, (((1,), (1,)), ((), ())), preferred_element_type=jnp.float32
    )


def unit_parts(refs):
    parts, first = [], 0
    for n, ref in enumerate(refs):
        part = ref if n + 1 < len(refs) else ref.at[PAD:]
        parts.append((first, part))
        first += part.shape[0]
    return parts


def take(refs, counts):
    groups = []
    for count in counts:
        groups.append(refs[:count])
        refs = refs[count:]
    return groups, refs


def fold_sublanes(values):
    rows, lanes = values.shape
    return jnp.max(values.reshape(rows // 8, 8, lanes), axis=0)


def fold_lanes(values):
    return jnp.concatenate(
        [
            jnp.max(jnp.transpose(values[first : first + 128]), axis=0, keepdims=True)
            for first in range(0, values.shape[0], 128)
        ],
        axis=0,
    )


def row_slices(block):
    slices = []
    for first, part in unit_parts(block):
        count = part.shape[0]
        for row in range(0, count, TILE):
            size = min(TILE, count - row)
            slices.append((first + row, part.at[row : row + size]))
    return slices


def plane_kernel(rows, with_self, *refs):
    (own, one, two), refs = take(refs, (2, 2, 2))
    best_ref, column_refs = refs[-3], refs[-2:]
    own_tags = tag_rows(own[-1])
    for block, column_ref in zip((one, two), column_refs):
        column_ref[...] = tag_columns(block[-1], rows)
    for tile, own_part in row_slices(own):
        lanes = own_part[...]
        best = [jnp.full((8, 128), -1.0, jnp.float32) for _ in range(0, TILE, 128)]
        for which, (block, column_ref) in enumerate(zip((one, two), column_refs)):
            for first, part in row_slices(block):
                count = part.shape[0]
                found = dot_rows(part[...], lanes)
                column = column_ref[first : first + count, :]
                for n in range(TILE // 128):
                    lane = tile + n * 128
                    match = column == own_tags[lane // 128 : lane // 128 + 1]
                    if with_self and which == 0 and first < lane + 128 and lane < first + count:
                        row_id = lax.broadcasted_iota(jnp.int32, (count, 128), 0) + first
                        lane_id = lax.broadcasted_iota(jnp.int32, (count, 128), 1) + lane
                        match = match & (row_id != lane_id)
                    masked = jnp.where(match, found[:, n * 128 : n * 128 + 128], -1.0)
                    best[n] = jnp.maximum(best[n], fold_sublanes(masked))
        for n in range(TILE // 128):
            place = pl.ds(tile // 128 + n, 1)
            folded = jnp.max(best[n], axis=0, keepdims=True)
            if with_self:
                folded = jnp.maximum(folded, refs[0][place, :])
            best_ref[place, :] = folded


def cross_kernel(starts, bases, *refs):
    (tags, aways), refs = take(refs, (1, len(starts)))
    blocks, refs = take(refs, (2,) * PLANE)
    columns, refs = refs[:PLANE], refs[PLANE:]
    away_before, away_best = refs[0], refs[PLANE + 1]
    plane_before, plane_best = refs[1 : PLANE + 1], refs[PLANE + 2 :]
    away_tags = tag_rows(tags[0])
    tiles = []
    for start, base, away in zip(starts, bases, aways):
        for row in range(0, away.shape[0] - base, TILE):
            tiles.append((start + row, away.at[base + row : base + row + TILE]))
    best = {}
    for which in range(PLANE):
        for first, part in row_slices(blocks[which]):
            count = part.shape[0]
            row_best = jnp.full((count, 128), -1.0, jnp.float32)
            for tile, away in tiles:
                found = dot_rows(part[...], away[...])
                column = columns[which][first : first + count, :]
                for lane in range(0, TILE, 128):
                    row = (tile + lane) // 128
                    match = column == away_tags[row : row + 1]
                    masked = jnp.where(match, found[:, lane : lane + 128], -1.0)
                    row_best = jnp.maximum(row_best, masked)
                    folded = fold_sublanes(masked)
                    best[row] = jnp.maximum(best[row], folded) if row in best else folded
            place = pl.ds(first // 128, count // 128)
            folded = fold_lanes(row_best)
            plane_best[which][place, :] = jnp.maximum(folded, plane_before[which][place, :])
    away_best[...] = away_before[...]
    for row, values in best.items():
        away_best[row : row + 1, :] = jnp.max(values, axis=0, keepdims=True)


def small_cost():
    return pl.CostEstimate(flops=1, bytes_accessed=1, transcendentals=0)


def plane_steps(planes):
    if planes == 4:
        return [(2, 0, 3, 1), (1, 2, 3, 0)]
    return [
        [(z + distance) % planes for z in range(planes)]
        for distance in range(1, planes // 2 + 1)
    ]


def after(value, *others):
    return lax.optimization_barrier((value,) + others)[0]


def local(embeddings, owner_index, sub_label, run_start):
    rows, width = embeddings.shape
    peers = lax.axis_size("dp")
    planes = peers // PLANE
    lanes = lanes_shape(rows)

    space = -(2 * rows + peers) % 2048
    ints = jnp.concatenate([owner_index, sub_label, run_start, jnp.zeros((space,), jnp.int32)])
    ints = ints.reshape(-1, 128)
    def kernel(body, inputs, outputs, name):
        return pl.pallas_call(
            body,
            out_shape=tuple(outputs),
            in_specs=whole(len(inputs)),
            out_specs=tuple(whole(len(outputs))),
            compiler_params=params(),
            cost_estimate=small_cost(),
            name=name,
        )(*inputs)

    def part_shape(count):
        return jax.ShapeDtypeStruct((count, width), jnp.bfloat16)

    rest = rows - FIRST
    (first,) = kernel(first_kernel, (embeddings,), (part_shape(FIRST),), "first")
    last, head, tail = kernel(
        functools.partial(rest_kernel, rows),
        (embeddings, ints, first),
        (part_shape(PAD + rest), part_shape(PAD + FIRST), part_shape(rest)),
        "rest",
    )
    own = (first, last)

    def mate(value, distance):
        return lax.ppermute(value, "dp", [(i, i ^ distance) for i in range(peers)])

    away = []
    for n, step in enumerate(plane_steps(planes)):
        pairs = [(z * PLANE + j, t * PLANE + j) for z, t in enumerate(step) for j in range(PLANE)]
        parts = (head, tail) if n else own
        if n > 1:
            parts = [after(part, away[-1][1][-1]) for part in parts]
        away.append((pairs, [lax.ppermute(part, "dp", pairs) for part in parts]))
    beside = [mate(part, 2) for part in own]
    near = [mate(part, 1) for part in own]
    across = [mate(after(part, *away[0][1]), 1) for part in beside]

    columns = jax.ShapeDtypeStruct((rows, 128), jnp.float32)
    best, beside_columns, across_columns = kernel(
        functools.partial(plane_kernel, rows, False),
        (*own, *beside, *across),
        (lanes, columns, columns),
        "plane_far",
    )
    best, own_columns, near_columns = kernel(
        functools.partial(plane_kernel, rows, True),
        (*own, *own, *near, best),
        (lanes, columns, columns),
        "plane_near",
    )
    plane = (*own, *near, *beside, *across)
    plane += (own_columns, near_columns, beside_columns, across_columns)
    plane_best = [jnp.full(lanes.shape, -1.0, jnp.float32)] * PLANE
    backs = []
    for n, (pairs, received) in enumerate(away):
        away_best = jnp.full(lanes.shape, -1.0, jnp.float32)
        if n:
            calls = (((0,), (PAD,), received[:1]), ((FIRST,), (0,), received[1:]))
        else:
            calls = (((0, FIRST), (0, PAD), received),)
        tags = received[0] if n else received[-1]
        for starts, bases, parts in calls:
            if n and starts[0]:
                away_best = after(away_best, backs[-1])
            away_best, *plane_best = kernel(
                functools.partial(cross_kernel, starts, bases),
                (tags, *parts, *plane, away_best, *plane_best),
                (lanes,) * (PLANE + 1),
                "cross",
            )
        backs.append(lax.ppermute(away_best, "dp", [(t, s) for s, t in pairs]))
    best = jnp.maximum(best, plane_best[0]).reshape(-1)[:rows]
    for distance, values in ((3, plane_best[3]), (2, plane_best[2]), (1, plane_best[1])):
        backs.insert(-1, mate(values, distance))
    for back in backs:
        best = jnp.maximum(best, back.reshape(-1)[:rows])
    return best


def solution(mesh):
    in_specs = (P(("groups", "dp"), None), P(("groups", "dp")), P(("groups", "dp")), P("groups"))
    out_specs = P(("groups", "dp"))
    return jax.shard_map(local, mesh=mesh, in_specs=in_specs, out_specs=out_specs, check_vma=False)
```

```python
import functools

import jax
import jax.numpy as jnp
from jax import lax
from jax.experimental import pallas as pl
from jax.experimental.pallas import tpu as pltpu
from jax.sharding import PartitionSpec as P

LABELS = 3
PLANE = 4
PAD = 16
BASE = 64.0
TILE = 256
FIRST = 512
VMEM_LIMIT = 24 * 2**20


def whole(count):
    return [pl.BlockSpec(memory_space=pltpu.VMEM)] * count


def params():
    return pltpu.CompilerParams(vmem_limit_bytes=VMEM_LIMIT)


def lanes_shape(rows):
    return jax.ShapeDtypeStruct((-(-rows // 1024) * 8, 128), jnp.float32)


def unit_rows(values):
    squares = jnp.sum(values * values, axis=1, keepdims=True)
    return (values * lax.rsqrt(squares + 1e-06)).astype(jnp.bfloat16)


def first_kernel(embeddings_ref, first_ref):
    for row in range(0, first_ref.shape[0], 128):
        first_ref[row : row + 128, :] = unit_rows(embeddings_ref[row : row + 128, :])


def rest_kernel(rows, embeddings_ref, ints_ref, first_ref, last_ref, head_ref, tail_ref):
    label_row = rows // 128
    owner, label = ints_ref[0:8, :], ints_ref[label_row : label_row + 8, :]
    runs = ints_ref[2 * label_row : 2 * label_row + 1, :]
    first_owner = jnp.take_along_axis(jnp.broadcast_to(runs, owner.shape), owner, axis=1)
    tags = 1 + jnp.where(label == 0, first_owner * LABELS, owner * LABELS + label)
    tags = tags.astype(jnp.float32)
    high = jnp.floor(tags * (1.0 / BASE))
    digits = jnp.concatenate([high, tags - high * BASE], axis=0).astype(jnp.bfloat16)
    width = embeddings_ref.shape[1]
    digits = jnp.concatenate([digits, jnp.zeros((PAD, width - 128), jnp.bfloat16)], axis=1)
    last_ref[0:PAD, :] = digits
    head_ref[0:PAD, :] = digits
    head_ref[PAD:, :] = first_ref[...]
    first = first_ref.shape[0]
    for row in range(0, rows - first, 128):
        unit = unit_rows(embeddings_ref[first + row : first + row + 128, :])
        last_ref[PAD + row : PAD + row + 128, :] = unit
        tail_ref[row : row + 128, :] = unit


def tag_rows(block_ref):
    digits = block_ref[0:PAD, 0:128].astype(jnp.float32)
    return digits[0:8] * BASE + digits[8:16]


def tag_columns(block_ref, rows):
    tags = tag_rows(block_ref)
    return jnp.concatenate(
        [jnp.transpose(jnp.broadcast_to(tags[n : n + 1], (128, 128))) for n in range(rows // 128)],
        axis=0,
    )


def dot_rows(values, lanes):
    return lax.dot_general(
        values, lanes, (((1,), (1,)), ((), ())), preferred_element_type=jnp.float32
    )


def unit_parts(refs):
    parts, first = [], 0
    for n, ref in enumerate(refs):
        part = ref if n + 1 < len(refs) else ref.at[PAD:]
        parts.append((first, part))
        first += part.shape[0]
    return parts


def take(refs, counts):
    groups = []
    for count in counts:
        groups.append(refs[:count])
        refs = refs[count:]
    return groups, refs


def fold_sublanes(values):
    rows, lanes = values.shape
    return jnp.max(values.reshape(rows // 8, 8, lanes), axis=0)


def fold_lanes(values):
    return jnp.concatenate(
        [
            jnp.max(jnp.transpose(values[first : first + 128]), axis=0, keepdims=True)
            for first in range(0, values.shape[0], 128)
        ],
        axis=0,
    )


def row_slices(block):
    slices = []
    for first, part in unit_parts(block):
        count = part.shape[0]
        for row in range(0, count, TILE):
            size = min(TILE, count - row)
            slices.append((first + row, part.at[row : row + size]))
    return slices


def plane_kernel(rows, with_self, *refs):
    (own, one, two), refs = take(refs, (2, 2, 2))
    best_ref, column_refs = refs[-3], refs[-2:]
    own_tags = tag_rows(own[-1])
    for block, column_ref in zip((one, two), column_refs):
        column_ref[...] = tag_columns(block[-1], rows)
    for tile, own_part in row_slices(own):
        lanes = own_part[...]
        best = [jnp.full((8, 128), -1.0, jnp.float32) for _ in range(0, TILE, 128)]
        for which, (block, column_ref) in enumerate(zip((one, two), column_refs)):
            for first, part in row_slices(block):
                count = part.shape[0]
                found = dot_rows(part[...], lanes)
                column = column_ref[first : first + count, :]
                for n in range(TILE // 128):
                    lane = tile + n * 128
                    match = column == own_tags[lane // 128 : lane // 128 + 1]
                    if with_self and which == 0 and first < lane + 128 and lane < first + count:
                        row_id = lax.broadcasted_iota(jnp.int32, (count, 128), 0) + first
                        lane_id = lax.broadcasted_iota(jnp.int32, (count, 128), 1) + lane
                        match = match & (row_id != lane_id)
                    masked = jnp.where(match, found[:, n * 128 : n * 128 + 128], -1.0)
                    best[n] = jnp.maximum(best[n], fold_sublanes(masked))
        for n in range(TILE // 128):
            place = pl.ds(tile // 128 + n, 1)
            folded = jnp.max(best[n], axis=0, keepdims=True)
            if with_self:
                folded = jnp.maximum(folded, refs[0][place, :])
            best_ref[place, :] = folded


def cross_kernel(starts, bases, *refs):
    (tags, aways), refs = take(refs, (1, len(starts)))
    blocks, refs = take(refs, (2,) * PLANE)
    columns, refs = refs[:PLANE], refs[PLANE:]
    away_before, away_best = refs[0], refs[PLANE + 1]
    plane_before, plane_best = refs[1 : PLANE + 1], refs[PLANE + 2 :]
    away_tags = tag_rows(tags[0])
    tiles = []
    for start, base, away in zip(starts, bases, aways):
        for row in range(0, away.shape[0] - base, TILE):
            tiles.append((start + row, away.at[base + row : base + row + TILE]))
    best = {}
    for which in range(PLANE):
        for first, part in row_slices(blocks[which]):
            count = part.shape[0]
            row_best = jnp.full((count, 128), -1.0, jnp.float32)
            for tile, away in tiles:
                found = dot_rows(part[...], away[...])
                column = columns[which][first : first + count, :]
                for lane in range(0, TILE, 128):
                    row = (tile + lane) // 128
                    match = column == away_tags[row : row + 1]
                    masked = jnp.where(match, found[:, lane : lane + 128], -1.0)
                    row_best = jnp.maximum(row_best, masked)
                    folded = fold_sublanes(masked)
                    best[row] = jnp.maximum(best[row], folded) if row in best else folded
            place = pl.ds(first // 128, count // 128)
            folded = fold_lanes(row_best)
            plane_best[which][place, :] = jnp.maximum(folded, plane_before[which][place, :])
    away_best[...] = away_before[...]
    for row, values in best.items():
        away_best[row : row + 1, :] = jnp.max(values, axis=0, keepdims=True)


def small_cost():
    return pl.CostEstimate(flops=1, bytes_accessed=1, transcendentals=0)


def plane_steps(planes):
    if planes == 4:
        return [(2, 0, 3, 1), (3, 0, 1, 2)]
    return [
        [(z + distance) % planes for z in range(planes)]
        for distance in range(1, planes // 2 + 1)
    ]


def after(value, *others):
    return lax.optimization_barrier((value,) + others)[0]


def local(embeddings, owner_index, sub_label, run_start):
    rows, width = embeddings.shape
    peers = lax.axis_size("dp")
    planes = peers // PLANE
    lanes = lanes_shape(rows)

    space = -(2 * rows + peers) % 2048
    ints = jnp.concatenate([owner_index, sub_label, run_start, jnp.zeros((space,), jnp.int32)])
    ints = ints.reshape(-1, 128)
    def kernel(body, inputs, outputs, name):
        return pl.pallas_call(
            body,
            out_shape=tuple(outputs),
            in_specs=whole(len(inputs)),
            out_specs=tuple(whole(len(outputs))),
            compiler_params=params(),
            cost_estimate=small_cost(),
            name=name,
        )(*inputs)

    def part_shape(count):
        return jax.ShapeDtypeStruct((count, width), jnp.bfloat16)

    rest = rows - FIRST
    (first,) = kernel(first_kernel, (embeddings,), (part_shape(FIRST),), "first")
    last, head, tail = kernel(
        functools.partial(rest_kernel, rows),
        (embeddings, ints, first),
        (part_shape(PAD + rest), part_shape(PAD + FIRST), part_shape(rest)),
        "rest",
    )
    own = (first, last)

    def mate(value, distance):
        return lax.ppermute(value, "dp", [(i, i ^ distance) for i in range(peers)])

    away = []
    for n, step in enumerate(plane_steps(planes)):
        pairs = [(z * PLANE + j, t * PLANE + j) for z, t in enumerate(step) for j in range(PLANE)]
        parts = (head, tail) if n else own
        if n > 1:
            parts = [after(part, away[-1][1][-1]) for part in parts]
        away.append((pairs, [lax.ppermute(part, "dp", pairs) for part in parts]))
    beside = [mate(part, 2) for part in own]
    near = [mate(part, 1) for part in own]
    across = [mate(after(part, *away[0][1]), 1) for part in beside]

    columns = jax.ShapeDtypeStruct((rows, 128), jnp.float32)
    best, beside_columns, across_columns = kernel(
        functools.partial(plane_kernel, rows, False),
        (*own, *beside, *across),
        (lanes, columns, columns),
        "plane_far",
    )
    best, own_columns, near_columns = kernel(
        functools.partial(plane_kernel, rows, True),
        (*own, *own, *near, best),
        (lanes, columns, columns),
        "plane_near",
    )
    plane = (*own, *near, *beside, *across)
    plane += (own_columns, near_columns, beside_columns, across_columns)
    plane_best = [jnp.full(lanes.shape, -1.0, jnp.float32)] * PLANE
    backs = []
    for n, (pairs, received) in enumerate(away):
        away_best = jnp.full(lanes.shape, -1.0, jnp.float32)
        if n:
            calls = (((0,), (PAD,), received[:1]), ((FIRST,), (0,), received[1:]))
        else:
            calls = (((0, FIRST), (0, PAD), received),)
        tags = received[0] if n else received[-1]
        for starts, bases, parts in calls:
            if n and starts[0]:
                away_best = after(away_best, backs[-1])
            away_best, *plane_best = kernel(
                functools.partial(cross_kernel, starts, bases),
                (tags, *parts, *plane, away_best, *plane_best),
                (lanes,) * (PLANE + 1),
                "cross",
            )
        backs.append(lax.ppermute(away_best, "dp", [(t, s) for s, t in pairs]))
    best = jnp.maximum(best, plane_best[0]).reshape(-1)[:rows]
    for distance, values in ((3, plane_best[3]), (2, plane_best[2]), (1, plane_best[1])):
        backs.insert(-1, mate(values, distance))
    for back in backs:
        best = jnp.maximum(best, back.reshape(-1)[:rows])
    return best


def solution(mesh):
    in_specs = (P(("groups", "dp"), None), P(("groups", "dp")), P(("groups", "dp")), P("groups"))
    out_specs = P(("groups", "dp"))
    return jax.shard_map(local, mesh=mesh, in_specs=in_specs, out_specs=out_specs, check_vma=False)
```

```python
import functools

import jax
import jax.numpy as jnp
from jax import lax
from jax.experimental import pallas as pl
from jax.experimental.pallas import tpu as pltpu
from jax.sharding import PartitionSpec as P

LABELS = 3
PLANE = 4
PAD = 16
BASE = 64.0
TILE = 256
FIRST = 512
VMEM_LIMIT = 24 * 2**20


def whole(count):
    return [pl.BlockSpec(memory_space=pltpu.VMEM)] * count


def params():
    return pltpu.CompilerParams(vmem_limit_bytes=VMEM_LIMIT)


def lanes_shape(rows):
    return jax.ShapeDtypeStruct((-(-rows // 1024) * 8, 128), jnp.float32)


def unit_rows(values):
    squares = jnp.sum(values * values, axis=1, keepdims=True)
    return (values * lax.rsqrt(squares + 1e-06)).astype(jnp.bfloat16)


def first_kernel(embeddings_ref, first_ref):
    for row in range(0, first_ref.shape[0], 128):
        first_ref[row : row + 128, :] = unit_rows(embeddings_ref[row : row + 128, :])


def rest_kernel(rows, embeddings_ref, ints_ref, first_ref, last_ref, head_ref, tail_ref):
    label_row = rows // 128
    owner, label = ints_ref[0:8, :], ints_ref[label_row : label_row + 8, :]
    runs = ints_ref[2 * label_row : 2 * label_row + 1, :]
    first_owner = jnp.take_along_axis(jnp.broadcast_to(runs, owner.shape), owner, axis=1)
    tags = 1 + jnp.where(label == 0, first_owner * LABELS, owner * LABELS + label)
    tags = tags.astype(jnp.float32)
    high = jnp.floor(tags * (1.0 / BASE))
    digits = jnp.concatenate([high, tags - high * BASE], axis=0).astype(jnp.bfloat16)
    width = embeddings_ref.shape[1]
    digits = jnp.concatenate([digits, jnp.zeros((PAD, width - 128), jnp.bfloat16)], axis=1)
    last_ref[0:PAD, :] = digits
    head_ref[0:PAD, :] = digits
    head_ref[PAD:, :] = first_ref[...]
    first = first_ref.shape[0]
    for row in range(0, rows - first, 128):
        unit = unit_rows(embeddings_ref[first + row : first + row + 128, :])
        last_ref[PAD + row : PAD + row + 128, :] = unit
        tail_ref[row : row + 128, :] = unit


def tag_rows(block_ref):
    digits = block_ref[0:PAD, 0:128].astype(jnp.float32)
    return digits[0:8] * BASE + digits[8:16]


def tag_columns(block_ref, rows):
    tags = tag_rows(block_ref)
    return jnp.concatenate(
        [jnp.transpose(jnp.broadcast_to(tags[n : n + 1], (128, 128))) for n in range(rows // 128)],
        axis=0,
    )


def dot_rows(values, lanes):
    return lax.dot_general(
        values, lanes, (((1,), (1,)), ((), ())), preferred_element_type=jnp.float32
    )


def unit_parts(refs):
    parts, first = [], 0
    for n, ref in enumerate(refs):
        part = ref if n + 1 < len(refs) else ref.at[PAD:]
        parts.append((first, part))
        first += part.shape[0]
    return parts


def take(refs, counts):
    groups = []
    for count in counts:
        groups.append(refs[:count])
        refs = refs[count:]
    return groups, refs


def fold_sublanes(values):
    rows, lanes = values.shape
    return jnp.max(values.reshape(rows // 8, 8, lanes), axis=0)


def fold_lanes(values):
    return jnp.concatenate(
        [
            jnp.max(jnp.transpose(values[first : first + 128]), axis=0, keepdims=True)
            for first in range(0, values.shape[0], 128)
        ],
        axis=0,
    )


def row_slices(block):
    slices = []
    for first, part in unit_parts(block):
        count = part.shape[0]
        for row in range(0, count, TILE):
            size = min(TILE, count - row)
            slices.append((first + row, part.at[row : row + size]))
    return slices


def plane_kernel(rows, with_self, *refs):
    (own, one, two), refs = take(refs, (2, 2, 2))
    best_ref, column_refs = refs[-3], refs[-2:]
    own_tags = tag_rows(own[-1])
    for block, column_ref in zip((one, two), column_refs):
        column_ref[...] = tag_columns(block[-1], rows)
    for tile, own_part in row_slices(own):
        lanes = own_part[...]
        best = [jnp.full((8, 128), -1.0, jnp.float32) for _ in range(0, TILE, 128)]
        for which, (block, column_ref) in enumerate(zip((one, two), column_refs)):
            for first, part in row_slices(block):
                count = part.shape[0]
                found = dot_rows(part[...], lanes)
                column = column_ref[first : first + count, :]
                for n in range(TILE // 128):
                    lane = tile + n * 128
                    match = column == own_tags[lane // 128 : lane // 128 + 1]
                    if with_self and which == 0 and first < lane + 128 and lane < first + count:
                        row_id = lax.broadcasted_iota(jnp.int32, (count, 128), 0) + first
                        lane_id = lax.broadcasted_iota(jnp.int32, (count, 128), 1) + lane
                        match = match & (row_id != lane_id)
                    masked = jnp.where(match, found[:, n * 128 : n * 128 + 128], -1.0)
                    best[n] = jnp.maximum(best[n], fold_sublanes(masked))
        for n in range(TILE // 128):
            place = pl.ds(tile // 128 + n, 1)
            folded = jnp.max(best[n], axis=0, keepdims=True)
            if with_self:
                folded = jnp.maximum(folded, refs[0][place, :])
            best_ref[place, :] = folded


def cross_kernel(starts, bases, *refs):
    (tags, aways), refs = take(refs, (1, len(starts)))
    blocks, refs = take(refs, (2,) * PLANE)
    columns, refs = refs[:PLANE], refs[PLANE:]
    away_before, away_best = refs[0], refs[PLANE + 1]
    plane_before, plane_best = refs[1 : PLANE + 1], refs[PLANE + 2 :]
    away_tags = tag_rows(tags[0])
    tiles = []
    for start, base, away in zip(starts, bases, aways):
        for row in range(0, away.shape[0] - base, TILE):
            tiles.append((start + row, away.at[base + row : base + row + TILE]))
    best = {}
    for which in range(PLANE):
        for first, part in row_slices(blocks[which]):
            count = part.shape[0]
            row_best = jnp.full((count, 128), -1.0, jnp.float32)
            for tile, away in tiles:
                found = dot_rows(part[...], away[...])
                column = columns[which][first : first + count, :]
                for lane in range(0, TILE, 128):
                    row = (tile + lane) // 128
                    match = column == away_tags[row : row + 1]
                    masked = jnp.where(match, found[:, lane : lane + 128], -1.0)
                    row_best = jnp.maximum(row_best, masked)
                    folded = fold_sublanes(masked)
                    best[row] = jnp.maximum(best[row], folded) if row in best else folded
            place = pl.ds(first // 128, count // 128)
            folded = fold_lanes(row_best)
            plane_best[which][place, :] = jnp.maximum(folded, plane_before[which][place, :])
    away_best[...] = away_before[...]
    for row, values in best.items():
        away_best[row : row + 1, :] = jnp.max(values, axis=0, keepdims=True)


def small_cost():
    return pl.CostEstimate(flops=1, bytes_accessed=1, transcendentals=0)


def plane_steps(planes):
    if planes == 4:
        return [(3, 0, 1, 2), (2, 0, 3, 1)]
    return [
        [(z + distance) % planes for z in range(planes)]
        for distance in range(1, planes // 2 + 1)
    ]


def after(value, *others):
    if not others:
        return value
    return lax.optimization_barrier((value,) + others)[0]


def local(embeddings, owner_index, sub_label, run_start):
    rows, width = embeddings.shape
    peers = lax.axis_size("dp")
    planes = peers // PLANE
    lanes = lanes_shape(rows)

    space = -(2 * rows + peers) % 2048
    ints = jnp.concatenate([owner_index, sub_label, run_start, jnp.zeros((space,), jnp.int32)])
    ints = ints.reshape(-1, 128)
    def kernel(body, inputs, outputs, name):
        return pl.pallas_call(
            body,
            out_shape=tuple(outputs),
            in_specs=whole(len(inputs)),
            out_specs=tuple(whole(len(outputs))),
            compiler_params=params(),
            cost_estimate=small_cost(),
            name=name,
        )(*inputs)

    def part_shape(count):
        return jax.ShapeDtypeStruct((count, width), jnp.bfloat16)

    rest = rows - FIRST
    (first,) = kernel(first_kernel, (embeddings,), (part_shape(FIRST),), "first")
    last, head, tail = kernel(
        functools.partial(rest_kernel, rows),
        (embeddings, ints, first),
        (part_shape(PAD + rest), part_shape(PAD + FIRST), part_shape(rest)),
        "rest",
    )
    own = (first, last)

    def mate(value, distance):
        return lax.ppermute(value, "dp", [(i, i ^ distance) for i in range(peers)])

    away = []
    for n, step in enumerate(plane_steps(planes)):
        pairs = [(z * PLANE + j, t * PLANE + j) for z, t in enumerate(step) for j in range(PLANE)]
        parts = (head, tail) if n else own
        if n > 1:
            parts = [after(part, away[-1][1][-1]) for part in parts]
        away.append((pairs, [lax.ppermute(part, "dp", pairs) for part in parts]))
    beside = [mate(part, 2) for part in own]
    near = [mate(part, 1) for part in own]
    across = [mate(after(part, *away[0][1]), 1) for part in beside]

    columns = jax.ShapeDtypeStruct((rows, 128), jnp.float32)
    best, beside_columns, across_columns = kernel(
        functools.partial(plane_kernel, rows, False),
        (*own, *beside, *across),
        (lanes, columns, columns),
        "plane_far",
    )
    best, own_columns, near_columns = kernel(
        functools.partial(plane_kernel, rows, True),
        (*own, *own, *near, best),
        (lanes, columns, columns),
        "plane_near",
    )
    plane = (*own, *near, *beside, *across)
    plane += (own_columns, near_columns, beside_columns, across_columns)
    plane_best = [jnp.full(lanes.shape, -1.0, jnp.float32)] * PLANE
    backs = []
    for n, (pairs, received) in enumerate(away):
        away_best = jnp.full(lanes.shape, -1.0, jnp.float32)
        if n:
            calls = (((0,), (PAD,), received[:1]), ((FIRST,), (0,), received[1:]))
        else:
            calls = (((0, FIRST), (0, PAD), received),)
        tags = received[0] if n else received[-1]
        for starts, bases, parts in calls:
            away_best, *plane_best = kernel(
                functools.partial(cross_kernel, starts, bases),
                (tags, *parts, *plane, away_best, *plane_best),
                (lanes,) * (PLANE + 1),
                "cross",
            )
        answer = after(away_best, *backs[:1])
        backs.append(lax.ppermute(answer, "dp", [(t, s) for s, t in pairs]))
    best = jnp.maximum(best, plane_best[0]).reshape(-1)[:rows]
    for distance in (3, 2, 1):
        backs.insert(-1, mate(after(plane_best[distance], *backs[:1]), distance))
    for back in backs:
        best = jnp.maximum(best, back.reshape(-1)[:rows])
    return best


def solution(mesh):
    in_specs = (P(("groups", "dp"), None), P(("groups", "dp")), P(("groups", "dp")), P("groups"))
    out_specs = P(("groups", "dp"))
    return jax.shard_map(local, mesh=mesh, in_specs=in_specs, out_specs=out_specs, check_vma=False)
```

```python
import functools

import jax
import jax.numpy as jnp
from jax import lax
from jax.experimental import pallas as pl
from jax.experimental.pallas import tpu as pltpu
from jax.sharding import PartitionSpec as P

LABELS = 3
PLANE = 4
PAD = 16
BASE = 64.0
TILE = 256
FIRST = 512
VMEM_LIMIT = 24 * 2**20


def whole(count):
    return [pl.BlockSpec(memory_space=pltpu.VMEM)] * count


def params():
    return pltpu.CompilerParams(vmem_limit_bytes=VMEM_LIMIT)


def lanes_shape(rows):
    return jax.ShapeDtypeStruct((-(-rows // 1024) * 8, 128), jnp.float32)


def unit_rows(values):
    squares = jnp.sum(values * values, axis=1, keepdims=True)
    return (values * lax.rsqrt(squares + 1e-06)).astype(jnp.bfloat16)


def first_kernel(embeddings_ref, first_ref):
    for row in range(0, first_ref.shape[0], 128):
        first_ref[row : row + 128, :] = unit_rows(embeddings_ref[row : row + 128, :])


def rest_kernel(rows, embeddings_ref, ints_ref, first_ref, last_ref, head_ref, tail_ref):
    label_row = rows // 128
    owner, label = ints_ref[0:8, :], ints_ref[label_row : label_row + 8, :]
    runs = ints_ref[2 * label_row : 2 * label_row + 1, :]
    first_owner = jnp.take_along_axis(jnp.broadcast_to(runs, owner.shape), owner, axis=1)
    tags = 1 + jnp.where(label == 0, first_owner * LABELS, owner * LABELS + label)
    tags = tags.astype(jnp.float32)
    high = jnp.floor(tags * (1.0 / BASE))
    digits = jnp.concatenate([high, tags - high * BASE], axis=0).astype(jnp.bfloat16)
    width = embeddings_ref.shape[1]
    digits = jnp.concatenate([digits, jnp.zeros((PAD, width - 128), jnp.bfloat16)], axis=1)
    last_ref[0:PAD, :] = digits
    head_ref[0:PAD, :] = digits
    head_ref[PAD:, :] = first_ref[...]
    first = first_ref.shape[0]
    for row in range(0, rows - first, 128):
        unit = unit_rows(embeddings_ref[first + row : first + row + 128, :])
        last_ref[PAD + row : PAD + row + 128, :] = unit
        tail_ref[row : row + 128, :] = unit


def tag_rows(block_ref):
    digits = block_ref[0:PAD, 0:128].astype(jnp.float32)
    return digits[0:8] * BASE + digits[8:16]


def tag_columns(block_ref, rows):
    tags = tag_rows(block_ref)
    return jnp.concatenate(
        [jnp.transpose(jnp.broadcast_to(tags[n : n + 1], (128, 128))) for n in range(rows // 128)],
        axis=0,
    )


def dot_rows(values, lanes):
    return lax.dot_general(
        values, lanes, (((1,), (1,)), ((), ())), preferred_element_type=jnp.float32
    )


def unit_parts(refs):
    parts, first = [], 0
    for n, ref in enumerate(refs):
        part = ref if n + 1 < len(refs) else ref.at[PAD:]
        parts.append((first, part))
        first += part.shape[0]
    return parts


def take(refs, counts):
    groups = []
    for count in counts:
        groups.append(refs[:count])
        refs = refs[count:]
    return groups, refs


def fold_sublanes(values):
    rows, lanes = values.shape
    return jnp.max(values.reshape(rows // 8, 8, lanes), axis=0)


def fold_lanes(values):
    return jnp.concatenate(
        [
            jnp.max(jnp.transpose(values[first : first + 128]), axis=0, keepdims=True)
            for first in range(0, values.shape[0], 128)
        ],
        axis=0,
    )


def row_slices(block):
    slices = []
    for first, part in unit_parts(block):
        count = part.shape[0]
        for row in range(0, count, TILE):
            size = min(TILE, count - row)
            slices.append((first + row, part.at[row : row + size]))
    return slices


def plane_kernel(rows, with_self, *refs):
    (own, one, two), refs = take(refs, (2, 2, 2))
    best_ref, column_refs = refs[-3], refs[-2:]
    own_tags = tag_rows(own[-1])
    for block, column_ref in zip((one, two), column_refs):
        column_ref[...] = tag_columns(block[-1], rows)
    for tile, own_part in row_slices(own):
        lanes = own_part[...]
        best = [jnp.full((8, 128), -1.0, jnp.float32) for _ in range(0, TILE, 128)]
        for which, (block, column_ref) in enumerate(zip((one, two), column_refs)):
            for first, part in row_slices(block):
                count = part.shape[0]
                found = dot_rows(part[...], lanes)
                column = column_ref[first : first + count, :]
                for n in range(TILE // 128):
                    lane = tile + n * 128
                    match = column == own_tags[lane // 128 : lane // 128 + 1]
                    if with_self and which == 0 and first < lane + 128 and lane < first + count:
                        row_id = lax.broadcasted_iota(jnp.int32, (count, 128), 0) + first
                        lane_id = lax.broadcasted_iota(jnp.int32, (count, 128), 1) + lane
                        match = match & (row_id != lane_id)
                    masked = jnp.where(match, found[:, n * 128 : n * 128 + 128], -1.0)
                    best[n] = jnp.maximum(best[n], fold_sublanes(masked))
        for n in range(TILE // 128):
            place = pl.ds(tile // 128 + n, 1)
            folded = jnp.max(best[n], axis=0, keepdims=True)
            if with_self:
                folded = jnp.maximum(folded, refs[0][place, :])
            best_ref[place, :] = folded


def cross_kernel(starts, bases, *refs):
    (tags, aways), refs = take(refs, (1, len(starts)))
    blocks, refs = take(refs, (2,) * PLANE)
    columns, refs = refs[:PLANE], refs[PLANE:]
    away_before, away_best = refs[0], refs[PLANE + 1]
    plane_before, plane_best = refs[1 : PLANE + 1], refs[PLANE + 2 :]
    away_tags = tag_rows(tags[0])
    tiles = []
    for start, base, away in zip(starts, bases, aways):
        for row in range(0, away.shape[0] - base, TILE):
            tiles.append((start + row, away.at[base + row : base + row + TILE]))
    best = {}
    for which in range(PLANE):
        for first, part in row_slices(blocks[which]):
            count = part.shape[0]
            row_best = jnp.full((count, 128), -1.0, jnp.float32)
            for tile, away in tiles:
                found = dot_rows(part[...], away[...])
                column = columns[which][first : first + count, :]
                for lane in range(0, TILE, 128):
                    row = (tile + lane) // 128
                    match = column == away_tags[row : row + 1]
                    masked = jnp.where(match, found[:, lane : lane + 128], -1.0)
                    row_best = jnp.maximum(row_best, masked)
                    folded = fold_sublanes(masked)
                    best[row] = jnp.maximum(best[row], folded) if row in best else folded
            place = pl.ds(first // 128, count // 128)
            folded = fold_lanes(row_best)
            plane_best[which][place, :] = jnp.maximum(folded, plane_before[which][place, :])
    away_best[...] = away_before[...]
    for row, values in best.items():
        away_best[row : row + 1, :] = jnp.max(values, axis=0, keepdims=True)


def small_cost():
    return pl.CostEstimate(flops=1, bytes_accessed=1, transcendentals=0)


def plane_steps(planes):
    if planes == 4:
        return [(1, 2, 3, 0), (2, 0, 3, 1)]
    return [
        [(z + distance) % planes for z in range(planes)]
        for distance in range(1, planes // 2 + 1)
    ]


def after(value, *others):
    if not others:
        return value
    return lax.optimization_barrier((value,) + others)[0]


def local(embeddings, owner_index, sub_label, run_start):
    rows, width = embeddings.shape
    peers = lax.axis_size("dp")
    planes = peers // PLANE
    lanes = lanes_shape(rows)

    space = -(2 * rows + peers) % 2048
    ints = jnp.concatenate([owner_index, sub_label, run_start, jnp.zeros((space,), jnp.int32)])
    ints = ints.reshape(-1, 128)
    def kernel(body, inputs, outputs, name):
        return pl.pallas_call(
            body,
            out_shape=tuple(outputs),
            in_specs=whole(len(inputs)),
            out_specs=tuple(whole(len(outputs))),
            compiler_params=params(),
            cost_estimate=small_cost(),
            name=name,
        )(*inputs)

    def part_shape(count):
        return jax.ShapeDtypeStruct((count, width), jnp.bfloat16)

    rest = rows - FIRST
    (first,) = kernel(first_kernel, (embeddings,), (part_shape(FIRST),), "first")
    last, head, tail = kernel(
        functools.partial(rest_kernel, rows),
        (embeddings, ints, first),
        (part_shape(PAD + rest), part_shape(PAD + FIRST), part_shape(rest)),
        "rest",
    )
    own = (first, last)

    def mate(value, distance):
        return lax.ppermute(value, "dp", [(i, i ^ distance) for i in range(peers)])

    away = []
    for n, step in enumerate(plane_steps(planes)):
        pairs = [(z * PLANE + j, t * PLANE + j) for z, t in enumerate(step) for j in range(PLANE)]
        parts = (head, tail) if n else own
        if n > 1:
            parts = [after(part, away[-1][1][-1]) for part in parts]
        away.append((pairs, [lax.ppermute(part, "dp", pairs) for part in parts]))
    beside = [mate(part, 2) for part in own]
    near = [mate(part, 1) for part in own]
    across = [mate(after(part, *away[0][1]), 1) for part in beside]

    columns = jax.ShapeDtypeStruct((rows, 128), jnp.float32)
    best, beside_columns, across_columns = kernel(
        functools.partial(plane_kernel, rows, False),
        (*own, *beside, *across),
        (lanes, columns, columns),
        "plane_far",
    )
    best, own_columns, near_columns = kernel(
        functools.partial(plane_kernel, rows, True),
        (*own, *own, *near, best),
        (lanes, columns, columns),
        "plane_near",
    )
    plane = (*own, *near, *beside, *across)
    plane += (own_columns, near_columns, beside_columns, across_columns)
    plane_best = [jnp.full(lanes.shape, -1.0, jnp.float32)] * PLANE
    backs = []
    for n, (pairs, received) in enumerate(away):
        away_best = jnp.full(lanes.shape, -1.0, jnp.float32)
        if n:
            calls = (((0,), (PAD,), received[:1]), ((FIRST,), (0,), received[1:]))
        else:
            calls = (((0, FIRST), (0, PAD), received),)
        tags = received[0] if n else received[-1]
        for starts, bases, parts in calls:
            away_best, *plane_best = kernel(
                functools.partial(cross_kernel, starts, bases),
                (tags, *parts, *plane, away_best, *plane_best),
                (lanes,) * (PLANE + 1),
                "cross",
            )
        answer = after(away_best, *backs[:1])
        backs.append(lax.ppermute(answer, "dp", [(t, s) for s, t in pairs]))
    best = jnp.maximum(best, plane_best[0]).reshape(-1)[:rows]
    for distance in (3, 2, 1):
        backs.append(mate(after(plane_best[distance], *backs[:1]), distance))
    for back in backs:
        best = jnp.maximum(best, back.reshape(-1)[:rows])
    return best


def solution(mesh):
    in_specs = (P(("groups", "dp"), None), P(("groups", "dp")), P(("groups", "dp")), P("groups"))
    out_specs = P(("groups", "dp"))
    return jax.shard_map(local, mesh=mesh, in_specs=in_specs, out_specs=out_specs, check_vma=False)
```

```python
import functools

import jax
import jax.numpy as jnp
from jax import lax
from jax.experimental import pallas as pl
from jax.experimental.pallas import tpu as pltpu
from jax.sharding import PartitionSpec as P

LABELS = 3
PLANE = 4
PAD = 16
BASE = 64.0
TILE = 256
FIRST = 512
HEAD = 512
VMEM_LIMIT = 24 * 2**20


def whole(count):
    return [pl.BlockSpec(memory_space=pltpu.VMEM)] * count


def params():
    return pltpu.CompilerParams(vmem_limit_bytes=VMEM_LIMIT)


def lanes_shape(rows):
    return jax.ShapeDtypeStruct((-(-rows // 1024) * 8, 128), jnp.float32)


def unit_rows(values):
    squares = jnp.sum(values * values, axis=1, keepdims=True)
    return (values * lax.rsqrt(squares + 1e-06)).astype(jnp.bfloat16)


def first_kernel(embeddings_ref, first_ref):
    for row in range(0, first_ref.shape[0], 128):
        first_ref[row : row + 128, :] = unit_rows(embeddings_ref[row : row + 128, :])


def rest_kernel(rows, embeddings_ref, ints_ref, first_ref, last_ref, head_ref, tail_ref):
    label_row = rows // 128
    owner, label = ints_ref[0:8, :], ints_ref[label_row : label_row + 8, :]
    runs = ints_ref[2 * label_row : 2 * label_row + 1, :]
    first_owner = jnp.take_along_axis(jnp.broadcast_to(runs, owner.shape), owner, axis=1)
    tags = 1 + jnp.where(label == 0, first_owner * LABELS, owner * LABELS + label)
    tags = tags.astype(jnp.float32)
    high = jnp.floor(tags * (1.0 / BASE))
    digits = jnp.concatenate([high, tags - high * BASE], axis=0).astype(jnp.bfloat16)
    width = embeddings_ref.shape[1]
    digits = jnp.concatenate([digits, jnp.zeros((PAD, width - 128), jnp.bfloat16)], axis=1)
    last_ref[0:PAD, :] = digits
    head_ref[0:PAD, :] = digits
    first = first_ref.shape[0]
    head = head_ref.shape[0] - PAD
    head_ref[PAD : PAD + first, :] = first_ref[...]
    for row in range(first, rows, 128):
        unit = unit_rows(embeddings_ref[row : row + 128, :])
        last_ref[PAD + row - first : PAD + row - first + 128, :] = unit
        if row < head:
            head_ref[PAD + row : PAD + row + 128, :] = unit
        else:
            tail_ref[row - head : row - head + 128, :] = unit


def tag_rows(block_ref):
    digits = block_ref[0:PAD, 0:128].astype(jnp.float32)
    return digits[0:8] * BASE + digits[8:16]


def tag_columns(block_ref, first, count):
    tags = tag_rows(block_ref)
    parts = [
        jnp.transpose(jnp.broadcast_to(tags[n : n + 1], (128, 128)))
        for n in range(first // 128, (first + count) // 128)
    ]
    return jnp.concatenate(parts, axis=0)


def dot_rows(values, lanes):
    return lax.dot_general(
        values, lanes, (((1,), (1,)), ((), ())), preferred_element_type=jnp.float32
    )


def unit_parts(refs):
    parts, first = [], 0
    for n, ref in enumerate(refs):
        part = ref if n + 1 < len(refs) else ref.at[PAD:]
        parts.append((first, part))
        first += part.shape[0]
    return parts


def take(refs, counts):
    groups = []
    for count in counts:
        groups.append(refs[:count])
        refs = refs[count:]
    return groups, refs


def fold_sublanes(values):
    rows, lanes = values.shape
    return jnp.max(values.reshape(rows // 8, 8, lanes), axis=0)


def fold_lanes(values):
    return jnp.concatenate(
        [
            jnp.max(jnp.transpose(values[first : first + 128]), axis=0, keepdims=True)
            for first in range(0, values.shape[0], 128)
        ],
        axis=0,
    )


def row_slices(block):
    slices = []
    for first, part in unit_parts(block):
        count = part.shape[0]
        for row in range(0, count, TILE):
            size = min(TILE, count - row)
            slices.append((first + row, part.at[row : row + size]))
    return slices


def plane_kernel(rows, with_self, *refs):
    (own, one, two), refs = take(refs, (2, 2, 2))
    best_ref = refs[-1]
    own_tags = tag_rows(own[-1])
    columns = [tag_columns(block[-1], 0, rows) for block in (one, two)]
    for tile, own_part in row_slices(own):
        lanes = own_part[...]
        best = [jnp.full((8, 128), -1.0, jnp.float32) for _ in range(0, TILE, 128)]
        for which, block in enumerate((one, two)):
            for first, part in row_slices(block):
                count = part.shape[0]
                found = dot_rows(part[...], lanes)
                column = columns[which][first : first + count]
                for n in range(TILE // 128):
                    lane = tile + n * 128
                    match = column == own_tags[lane // 128 : lane // 128 + 1]
                    if with_self and which == 0 and first < lane + 128 and lane < first + count:
                        row_id = lax.broadcasted_iota(jnp.int32, (count, 128), 0) + first
                        lane_id = lax.broadcasted_iota(jnp.int32, (count, 128), 1) + lane
                        match = match & (row_id != lane_id)
                    masked = jnp.where(match, found[:, n * 128 : n * 128 + 128], -1.0)
                    best[n] = jnp.maximum(best[n], fold_sublanes(masked))
        for n in range(TILE // 128):
            place = pl.ds(tile // 128 + n, 1)
            folded = jnp.max(best[n], axis=0, keepdims=True)
            if with_self:
                folded = jnp.maximum(folded, refs[0][place, :])
            best_ref[place, :] = folded


def cross_kernel(starts, bases, *refs):
    (tags, aways), refs = take(refs, (1, len(starts)))
    blocks, refs = take(refs, (2,) * PLANE)
    away_before, away_best = refs[0], refs[PLANE + 1]
    plane_before, plane_best = refs[1 : PLANE + 1], refs[PLANE + 2 :]
    plane_tags = [tag_rows(block[-1]) for block in blocks]
    away_best[...] = away_before[...]
    best = {}
    for start, base, away in zip(starts, bases, aways):
        for tile in range(0, away.shape[0] - base, TILE):
            values = away[base + tile : base + tile + TILE, :]
            column = tag_columns(tags[0], start + tile, TILE)
            row_best = jnp.full((TILE, 128), -1.0, jnp.float32)
            for which in range(PLANE):
                for first, part in row_slices(blocks[which]):
                    found = dot_rows(values, part[...])
                    for lane in range(0, part.shape[0], 128):
                        row = (first + lane) // 128
                        match = column == plane_tags[which][row : row + 1]
                        masked = jnp.where(match, found[:, lane : lane + 128], -1.0)
                        row_best = jnp.maximum(row_best, masked)
                        folded = fold_sublanes(masked)
                        place = which, row
                        best[place] = jnp.maximum(best[place], folded) if place in best else folded
            place = pl.ds((start + tile) // 128, TILE // 128)
            away_best[place, :] = fold_lanes(row_best)
    for which in range(PLANE):
        plane_best[which][...] = plane_before[which][...]
    for (which, row), values in best.items():
        folded = jnp.max(values, axis=0, keepdims=True)
        place = pl.ds(row, 1)
        plane_best[which][place, :] = jnp.maximum(folded, plane_before[which][place, :])


def small_cost():
    return pl.CostEstimate(flops=1, bytes_accessed=1, transcendentals=0)


def plane_steps(planes):
    if planes == 4:
        return [(3, 0, 1, 2), (2, 0, 3, 1)]
    return [
        [(z + distance) % planes for z in range(planes)]
        for distance in range(1, planes // 2 + 1)
    ]


def after(value, *others):
    if not others:
        return value
    return lax.optimization_barrier((value,) + others)[0]


def local(embeddings, owner_index, sub_label, run_start):
    rows, width = embeddings.shape
    peers = lax.axis_size("dp")
    planes = peers // PLANE
    lanes = lanes_shape(rows)

    space = -(2 * rows + peers) % 2048
    ints = jnp.concatenate([owner_index, sub_label, run_start, jnp.zeros((space,), jnp.int32)])
    ints = ints.reshape(-1, 128)
    def kernel(body, inputs, outputs, name):
        return pl.pallas_call(
            body,
            out_shape=tuple(outputs),
            in_specs=whole(len(inputs)),
            out_specs=tuple(whole(len(outputs))),
            compiler_params=params(),
            cost_estimate=small_cost(),
            name=name,
        )(*inputs)

    def part_shape(count):
        return jax.ShapeDtypeStruct((count, width), jnp.bfloat16)

    (first,) = kernel(first_kernel, (embeddings[:FIRST],), (part_shape(FIRST),), "first")
    last, head, tail = kernel(
        functools.partial(rest_kernel, rows),
        (embeddings, ints, first),
        (part_shape(PAD + rows - FIRST), part_shape(PAD + HEAD), part_shape(rows - HEAD)),
        "rest",
    )
    own = (first, last)

    def mate(value, distance):
        return lax.ppermute(value, "dp", [(i, i ^ distance) for i in range(peers)])

    away = []
    for n, step in enumerate(plane_steps(planes)):
        pairs = [(z * PLANE + j, t * PLANE + j) for z, t in enumerate(step) for j in range(PLANE)]
        parts = (head, tail) if n else own
        if n > 1:
            parts = [after(part, away[-1][1][-1]) for part in parts]
        away.append((pairs, [lax.ppermute(part, "dp", pairs) for part in parts]))
    beside = [mate(part, 2) for part in own]
    near = [mate(part, 1) for part in own]
    across = [mate(after(part, *away[0][1]), 1) for part in beside]

    (best,) = kernel(
        functools.partial(plane_kernel, rows, False),
        (*own, *beside, *across),
        (lanes,),
        "plane_far",
    )
    (best,) = kernel(
        functools.partial(plane_kernel, rows, True),
        (*own, *own, *near, best),
        (lanes,),
        "plane_near",
    )
    plane = (*own, *near, *beside, *across)
    plane_best = [best] + [jnp.full(lanes.shape, -1.0, jnp.float32)] * (PLANE - 1)
    backs = []
    for n, (pairs, received) in enumerate(away):
        away_best = jnp.full(lanes.shape, -1.0, jnp.float32)
        if n:
            calls = (((0,), (PAD,), received[:1]), ((HEAD,), (0,), received[1:]))
        else:
            calls = (((0, FIRST), (0, PAD), received),)
        tags = received[0] if n else received[-1]
        for starts, bases, parts in calls:
            away_best, *plane_best = kernel(
                functools.partial(cross_kernel, starts, bases),
                (tags, *parts, *plane, away_best, *plane_best),
                (lanes,) * (PLANE + 1),
                "cross",
            )
        backs.append(lax.ppermute(away_best, "dp", [(t, s) for s, t in pairs]))
    best = plane_best[0].reshape(-1)[:rows]
    for distance in (3, 2, 1):
        backs.append(mate(after(plane_best[distance], *backs[:1]), distance))
    for back in backs:
        best = jnp.maximum(best, back.reshape(-1)[:rows])
    return best


def solution(mesh):
    in_specs = (P(("groups", "dp"), None), P(("groups", "dp")), P(("groups", "dp")), P("groups"))
    out_specs = P(("groups", "dp"))
    return jax.shard_map(local, mesh=mesh, in_specs=in_specs, out_specs=out_specs, check_vma=False)
```

```python
import functools

import jax
import jax.numpy as jnp
from jax import lax
from jax.experimental import pallas as pl
from jax.experimental.pallas import tpu as pltpu
from jax.sharding import PartitionSpec as P

LABELS = 3
PLANE = 4
PAD = 16
BASE = 64.0
TILE = 256
FIRST = 512
HEAD = 512
VMEM_LIMIT = 24 * 2**20


def whole(count):
    return [pl.BlockSpec(memory_space=pltpu.VMEM)] * count


def params():
    return pltpu.CompilerParams(vmem_limit_bytes=VMEM_LIMIT)


def lanes_shape(rows):
    return jax.ShapeDtypeStruct((-(-rows // 1024) * 8, 128), jnp.float32)


def unit_rows(values):
    squares = jnp.sum(values * values, axis=1, keepdims=True)
    return (values * lax.rsqrt(squares + 1e-06)).astype(jnp.bfloat16)


def first_kernel(embeddings_ref, first_ref):
    for row in range(0, first_ref.shape[0], 128):
        first_ref[row : row + 128, :] = unit_rows(embeddings_ref[row : row + 128, :])


def rest_kernel(rows, embeddings_ref, ints_ref, first_ref, last_ref, head_ref, tail_ref):
    label_row = rows // 128
    owner, label = ints_ref[0:8, :], ints_ref[label_row : label_row + 8, :]
    runs = ints_ref[2 * label_row : 2 * label_row + 1, :]
    first_owner = jnp.take_along_axis(jnp.broadcast_to(runs, owner.shape), owner, axis=1)
    tags = 1 + jnp.where(label == 0, first_owner * LABELS, owner * LABELS + label)
    tags = tags.astype(jnp.float32)
    high = jnp.floor(tags * (1.0 / BASE))
    digits = jnp.concatenate([high, tags - high * BASE], axis=0).astype(jnp.bfloat16)
    width = embeddings_ref.shape[1]
    digits = jnp.concatenate([digits, jnp.zeros((PAD, width - 128), jnp.bfloat16)], axis=1)
    last_ref[0:PAD, :] = digits
    head_ref[0:PAD, :] = digits
    first = first_ref.shape[0]
    head = head_ref.shape[0] - PAD
    head_ref[PAD : PAD + first, :] = first_ref[...]
    for row in range(first, rows, 128):
        unit = unit_rows(embeddings_ref[row : row + 128, :])
        last_ref[PAD + row - first : PAD + row - first + 128, :] = unit
        if row < head:
            head_ref[PAD + row : PAD + row + 128, :] = unit
        else:
            tail_ref[row - head : row - head + 128, :] = unit


def tag_rows(block_ref):
    digits = block_ref[0:PAD, 0:128].astype(jnp.float32)
    return digits[0:8] * BASE + digits[8:16]


def tag_columns(block_ref, first, count):
    tags = tag_rows(block_ref)
    parts = [
        jnp.transpose(jnp.broadcast_to(tags[n : n + 1], (128, 128)))
        for n in range(first // 128, (first + count) // 128)
    ]
    return jnp.concatenate(parts, axis=0)


def dot_rows(values, lanes):
    return lax.dot_general(
        values, lanes, (((1,), (1,)), ((), ())), preferred_element_type=jnp.float32
    )


def unit_parts(refs):
    parts, first = [], 0
    for n, ref in enumerate(refs):
        part = ref if n + 1 < len(refs) else ref.at[PAD:]
        parts.append((first, part))
        first += part.shape[0]
    return parts


def take(refs, counts):
    groups = []
    for count in counts:
        groups.append(refs[:count])
        refs = refs[count:]
    return groups, refs


def fold_sublanes(values):
    rows, lanes = values.shape
    return jnp.max(values.reshape(rows // 8, 8, lanes), axis=0)


def fold_lanes(values):
    return jnp.concatenate(
        [
            jnp.max(jnp.transpose(values[first : first + 128]), axis=0, keepdims=True)
            for first in range(0, values.shape[0], 128)
        ],
        axis=0,
    )


def row_slices(block):
    slices = []
    for first, part in unit_parts(block):
        count = part.shape[0]
        for row in range(0, count, TILE):
            size = min(TILE, count - row)
            slices.append((first + row, part.at[row : row + size]))
    return slices


def plane_kernel(rows, with_self, *refs):
    (own, one, two), refs = take(refs, (2, 2, 2))
    best_ref = refs[-1]
    own_tags = tag_rows(own[-1])
    columns = [tag_columns(block[-1], 0, rows) for block in (one, two)]
    for tile, own_part in row_slices(own):
        lanes = own_part[...]
        best = [jnp.full((8, 128), -1.0, jnp.float32) for _ in range(0, TILE, 128)]
        for which, block in enumerate((one, two)):
            for first, part in row_slices(block):
                count = part.shape[0]
                found = dot_rows(part[...], lanes)
                column = columns[which][first : first + count]
                for n in range(TILE // 128):
                    lane = tile + n * 128
                    match = column == own_tags[lane // 128 : lane // 128 + 1]
                    if with_self and which == 0 and first < lane + 128 and lane < first + count:
                        row_id = lax.broadcasted_iota(jnp.int32, (count, 128), 0) + first
                        lane_id = lax.broadcasted_iota(jnp.int32, (count, 128), 1) + lane
                        match = match & (row_id != lane_id)
                    masked = jnp.where(match, found[:, n * 128 : n * 128 + 128], -1.0)
                    best[n] = jnp.maximum(best[n], fold_sublanes(masked))
        for n in range(TILE // 128):
            place = pl.ds(tile // 128 + n, 1)
            folded = jnp.max(best[n], axis=0, keepdims=True)
            if with_self:
                folded = jnp.maximum(folded, refs[0][place, :])
            best_ref[place, :] = folded


def cross_kernel(starts, bases, *refs):
    (tags, aways), refs = take(refs, (1, len(starts)))
    blocks, refs = take(refs, (2,) * PLANE)
    away_before, away_best = refs[0], refs[PLANE + 1]
    plane_before, plane_best = refs[1 : PLANE + 1], refs[PLANE + 2 :]
    plane_tags = [tag_rows(block[-1]) for block in blocks]
    away_best[...] = away_before[...]
    best = {}
    for start, base, away in zip(starts, bases, aways):
        for tile in range(0, away.shape[0] - base, TILE):
            values = away[base + tile : base + tile + TILE, :]
            column = tag_columns(tags[0], start + tile, TILE)
            row_best = jnp.full((TILE, 128), -1.0, jnp.float32)
            for which in range(PLANE):
                for first, part in row_slices(blocks[which]):
                    found = dot_rows(values, part[...])
                    for lane in range(0, part.shape[0], 128):
                        row = (first + lane) // 128
                        match = column == plane_tags[which][row : row + 1]
                        masked = jnp.where(match, found[:, lane : lane + 128], -1.0)
                        row_best = jnp.maximum(row_best, masked)
                        folded = fold_sublanes(masked)
                        place = which, row
                        best[place] = jnp.maximum(best[place], folded) if place in best else folded
            place = pl.ds((start + tile) // 128, TILE // 128)
            away_best[place, :] = fold_lanes(row_best)
    for which in range(PLANE):
        plane_best[which][...] = plane_before[which][...]
    for (which, row), values in best.items():
        folded = jnp.max(values, axis=0, keepdims=True)
        place = pl.ds(row, 1)
        plane_best[which][place, :] = jnp.maximum(folded, plane_before[which][place, :])


def small_cost():
    return pl.CostEstimate(flops=1, bytes_accessed=1, transcendentals=0)


def plane_steps(planes):
    if planes == 4:
        return [[(0, 2), (1, 0), (2, 3), (3, 1)], [(0, 3), (2, 1)]]
    return [
        [(z, (z + distance) % planes) for z in range(planes)]
        for distance in range(1, planes // 2 + 1)
    ]


def after(value, *others):
    if not others:
        return value
    return lax.optimization_barrier((value,) + others)[0]


def local(embeddings, owner_index, sub_label, run_start):
    rows, width = embeddings.shape
    peers = lax.axis_size("dp")
    planes = peers // PLANE
    lanes = lanes_shape(rows)

    space = -(2 * rows + peers) % 2048
    ints = jnp.concatenate([owner_index, sub_label, run_start, jnp.zeros((space,), jnp.int32)])
    ints = ints.reshape(-1, 128)
    def kernel(body, inputs, outputs, name):
        return pl.pallas_call(
            body,
            out_shape=tuple(outputs),
            in_specs=whole(len(inputs)),
            out_specs=tuple(whole(len(outputs))),
            compiler_params=params(),
            cost_estimate=small_cost(),
            name=name,
        )(*inputs)

    def part_shape(count):
        return jax.ShapeDtypeStruct((count, width), jnp.bfloat16)

    (first,) = kernel(first_kernel, (embeddings,), (part_shape(FIRST),), "first")
    last, head, tail = kernel(
        functools.partial(rest_kernel, rows),
        (embeddings, ints, first),
        (part_shape(PAD + rows - FIRST), part_shape(PAD + HEAD), part_shape(rows - HEAD)),
        "rest",
    )
    own = (first, last)

    def mate(value, distance):
        return lax.ppermute(value, "dp", [(i, i ^ distance) for i in range(peers)])

    away = []
    for n, step in enumerate(plane_steps(planes)):
        pairs = [(z * PLANE + j, t * PLANE + j) for z, t in step for j in range(PLANE)]
        parts = (head, tail) if n else own
        if n > 1:
            parts = [after(part, away[-1][1][-1]) for part in parts]
        away.append((pairs, [lax.ppermute(part, "dp", pairs) for part in parts]))
    beside = [mate(part, 2) for part in own]
    near = [mate(part, 1) for part in own]
    across = [mate(after(part, *away[0][1]), 1) for part in beside]

    (best,) = kernel(
        functools.partial(plane_kernel, rows, False),
        (*own, *beside, *across),
        (lanes,),
        "plane_far",
    )
    (best,) = kernel(
        functools.partial(plane_kernel, rows, True),
        (*own, *own, *near, best),
        (lanes,),
        "plane_near",
    )
    plane = (*own, *near, *beside, *across)
    plane_best = [best] + [jnp.full(lanes.shape, -1.0, jnp.float32)] * (PLANE - 1)
    backs, masks = [], {}
    for n, (pairs, received) in enumerate(away):
        away_best = jnp.full(lanes.shape, -1.0, jnp.float32)
        if n:
            calls = (((0,), (PAD,), received[:1]), ((HEAD,), (0,), received[1:]))
        else:
            calls = (((0, FIRST), (0, PAD), received),)
        tags = received[0] if n else received[-1]
        for starts, bases, parts in calls:
            away_best, *plane_best = kernel(
                functools.partial(cross_kernel, starts, bases),
                (tags, *parts, *plane, away_best, *plane_best),
                (lanes,) * (PLANE + 1),
                "cross",
            )
        backs.append(lax.ppermute(away_best, "dp", [(t, s) for s, t in pairs]))
        if len(pairs) < peers:
            sources = sum(1 << z for z in {s // PLANE for s, _ in pairs})
            sent = (jnp.int32(sources) >> (lax.axis_index("dp") // PLANE)) & 1
            masks[n] = jnp.broadcast_to(sent == 1, (rows,))
    best = plane_best[0].reshape(-1)[:rows]
    for distance in (3, 2, 1):
        backs.append(mate(after(plane_best[distance], *backs[:1]), distance))
    for n, back in enumerate(backs):
        back = back.reshape(-1)[:rows]
        best = jnp.maximum(best, jnp.where(masks[n], back, -1.0) if n in masks else back)
    return best


def solution(mesh):
    in_specs = (P(("groups", "dp"), None), P(("groups", "dp")), P(("groups", "dp")), P("groups"))
    out_specs = P(("groups", "dp"))
    return jax.shard_map(local, mesh=mesh, in_specs=in_specs, out_specs=out_specs, check_vma=False)
```

```python
import functools

import jax
import jax.numpy as jnp
from jax import lax
from jax.experimental import pallas as pl
from jax.experimental.pallas import tpu as pltpu
from jax.sharding import PartitionSpec as P

LABELS = 3
PLANE = 4
PAD = 16
BASE = 64.0
TILE = 256
FIRST = 512
HEAD = 512
VMEM_LIMIT = 24 * 2**20


def whole(count):
    return [pl.BlockSpec(memory_space=pltpu.VMEM)] * count


def params():
    return pltpu.CompilerParams(vmem_limit_bytes=VMEM_LIMIT)


def lanes_shape(rows):
    return jax.ShapeDtypeStruct((-(-rows // 1024) * 8, 128), jnp.float32)


def unit_rows(values):
    squares = jnp.sum(values * values, axis=1, keepdims=True)
    return (values * lax.rsqrt(squares + 1e-06)).astype(jnp.bfloat16)


def first_kernel(embeddings_ref, first_ref):
    for row in range(0, first_ref.shape[0], 128):
        first_ref[row : row + 128, :] = unit_rows(embeddings_ref[row : row + 128, :])


def rest_kernel(rows, embeddings_ref, ints_ref, first_ref, last_ref, head_ref, tail_ref):
    label_row = rows // 128
    owner, label = ints_ref[0:8, :], ints_ref[label_row : label_row + 8, :]
    runs = ints_ref[2 * label_row : 2 * label_row + 1, :]
    first_owner = jnp.take_along_axis(jnp.broadcast_to(runs, owner.shape), owner, axis=1)
    tags = 1 + jnp.where(label == 0, first_owner * LABELS, owner * LABELS + label)
    tags = tags.astype(jnp.float32)
    high = jnp.floor(tags * (1.0 / BASE))
    digits = jnp.concatenate([high, tags - high * BASE], axis=0).astype(jnp.bfloat16)
    width = embeddings_ref.shape[1]
    digits = jnp.concatenate([digits, jnp.zeros((PAD, width - 128), jnp.bfloat16)], axis=1)
    last_ref[0:PAD, :] = digits
    head_ref[0:PAD, :] = digits
    first = first_ref.shape[0]
    head = head_ref.shape[0] - PAD
    head_ref[PAD : PAD + first, :] = first_ref[...]
    for row in range(first, rows, 128):
        unit = unit_rows(embeddings_ref[row : row + 128, :])
        last_ref[PAD + row - first : PAD + row - first + 128, :] = unit
        if row < head:
            head_ref[PAD + row : PAD + row + 128, :] = unit
        else:
            tail_ref[row - head : row - head + 128, :] = unit


def tag_rows(block_ref):
    digits = block_ref[0:PAD, 0:128].astype(jnp.float32)
    return digits[0:8] * BASE + digits[8:16]


def tag_columns(block_ref, first, count):
    tags = tag_rows(block_ref)
    parts = [
        jnp.transpose(jnp.broadcast_to(tags[n : n + 1], (128, 128)))
        for n in range(first // 128, (first + count) // 128)
    ]
    return jnp.concatenate(parts, axis=0)


def dot_rows(values, lanes):
    return lax.dot_general(
        values, lanes, (((1,), (1,)), ((), ())), preferred_element_type=jnp.float32
    )


def unit_parts(refs):
    parts, first = [], 0
    for n, ref in enumerate(refs):
        part = ref if n + 1 < len(refs) else ref.at[PAD:]
        parts.append((first, part))
        first += part.shape[0]
    return parts


def take(refs, counts):
    groups = []
    for count in counts:
        groups.append(refs[:count])
        refs = refs[count:]
    return groups, refs


def fold_sublanes(values):
    rows, lanes = values.shape
    return jnp.max(values.reshape(rows // 8, 8, lanes), axis=0)


def fold_lanes(values):
    return jnp.concatenate(
        [
            jnp.max(jnp.transpose(values[first : first + 128]), axis=0, keepdims=True)
            for first in range(0, values.shape[0], 128)
        ],
        axis=0,
    )


def row_slices(block):
    slices = []
    for first, part in unit_parts(block):
        count = part.shape[0]
        for row in range(0, count, TILE):
            size = min(TILE, count - row)
            slices.append((first + row, part.at[row : row + size]))
    return slices


def plane_kernel(rows, with_self, *refs):
    (own, one, two), refs = take(refs, (2, 2, 2))
    best_ref = refs[-1]
    own_tags = tag_rows(own[-1])
    columns = [tag_columns(block[-1], 0, rows) for block in (one, two)]
    for tile, own_part in row_slices(own):
        lanes = own_part[...]
        best = [jnp.full((8, 128), -1.0, jnp.float32) for _ in range(0, TILE, 128)]
        for which, block in enumerate((one, two)):
            for first, part in row_slices(block):
                count = part.shape[0]
                found = dot_rows(part[...], lanes)
                column = columns[which][first : first + count]
                for n in range(TILE // 128):
                    lane = tile + n * 128
                    match = column == own_tags[lane // 128 : lane // 128 + 1]
                    if with_self and which == 0 and first < lane + 128 and lane < first + count:
                        row_id = lax.broadcasted_iota(jnp.int32, (count, 128), 0) + first
                        lane_id = lax.broadcasted_iota(jnp.int32, (count, 128), 1) + lane
                        match = match & (row_id != lane_id)
                    masked = jnp.where(match, found[:, n * 128 : n * 128 + 128], -1.0)
                    best[n] = jnp.maximum(best[n], fold_sublanes(masked))
        for n in range(TILE // 128):
            place = pl.ds(tile // 128 + n, 1)
            folded = jnp.max(best[n], axis=0, keepdims=True)
            if with_self:
                folded = jnp.maximum(folded, refs[0][place, :])
            best_ref[place, :] = folded


def cross_kernel(starts, bases, *refs):
    (tags, aways), refs = take(refs, (1, len(starts)))
    blocks, refs = take(refs, (2,) * PLANE)
    away_before, away_best = refs[0], refs[PLANE + 1]
    plane_before, plane_best = refs[1 : PLANE + 1], refs[PLANE + 2 :]
    plane_tags = [tag_rows(block[-1]) for block in blocks]
    away_best[...] = away_before[...]
    best = {}
    for start, base, away in zip(starts, bases, aways):
        for tile in range(0, away.shape[0] - base, TILE):
            values = away[base + tile : base + tile + TILE, :]
            column = tag_columns(tags[0], start + tile, TILE)
            row_best = jnp.full((TILE, 128), -1.0, jnp.float32)
            for which in range(PLANE):
                for first, part in row_slices(blocks[which]):
                    found = dot_rows(values, part[...])
                    for lane in range(0, part.shape[0], 128):
                        row = (first + lane) // 128
                        match = column == plane_tags[which][row : row + 1]
                        masked = jnp.where(match, found[:, lane : lane + 128], -1.0)
                        row_best = jnp.maximum(row_best, masked)
                        folded = fold_sublanes(masked)
                        place = which, row
                        best[place] = jnp.maximum(best[place], folded) if place in best else folded
            place = pl.ds((start + tile) // 128, TILE // 128)
            away_best[place, :] = fold_lanes(row_best)
    for which in range(PLANE):
        plane_best[which][...] = plane_before[which][...]
    for (which, row), values in best.items():
        folded = jnp.max(values, axis=0, keepdims=True)
        place = pl.ds(row, 1)
        plane_best[which][place, :] = jnp.maximum(folded, plane_before[which][place, :])


def small_cost():
    return pl.CostEstimate(flops=1, bytes_accessed=1, transcendentals=0)


def plane_steps(planes):
    if planes == 4:
        return [[(0, 2), (1, 0), (2, 3), (3, 1)], [(3, 0), (1, 2)]]
    return [
        [(z, (z + distance) % planes) for z in range(planes)]
        for distance in range(1, planes // 2 + 1)
    ]


def after(value, *others):
    if not others:
        return value
    return lax.optimization_barrier((value,) + others)[0]


def local(embeddings, owner_index, sub_label, run_start):
    rows, width = embeddings.shape
    peers = lax.axis_size("dp")
    planes = peers // PLANE
    lanes = lanes_shape(rows)

    space = -(2 * rows + peers) % 2048
    ints = jnp.concatenate([owner_index, sub_label, run_start, jnp.zeros((space,), jnp.int32)])
    ints = ints.reshape(-1, 128)
    def kernel(body, inputs, outputs, name):
        return pl.pallas_call(
            body,
            out_shape=tuple(outputs),
            in_specs=whole(len(inputs)),
            out_specs=tuple(whole(len(outputs))),
            compiler_params=params(),
            cost_estimate=small_cost(),
            name=name,
        )(*inputs)

    def part_shape(count):
        return jax.ShapeDtypeStruct((count, width), jnp.bfloat16)

    (first,) = kernel(first_kernel, (embeddings,), (part_shape(FIRST),), "first")
    last, head, tail = kernel(
        functools.partial(rest_kernel, rows),
        (embeddings, ints, first),
        (part_shape(PAD + rows - FIRST), part_shape(PAD + HEAD), part_shape(rows - HEAD)),
        "rest",
    )
    own = (first, last)

    def mate(value, distance):
        return lax.ppermute(value, "dp", [(i, i ^ distance) for i in range(peers)])

    away = []
    for n, step in enumerate(plane_steps(planes)):
        pairs = [(z * PLANE + j, t * PLANE + j) for z, t in step for j in range(PLANE)]
        parts = (head, tail) if n else own
        if n > 1:
            parts = [after(part, away[-1][1][-1]) for part in parts]
        away.append((pairs, [lax.ppermute(part, "dp", pairs) for part in parts]))
    beside = [mate(part, 2) for part in own]
    near = [mate(part, 1) for part in own]
    across = [mate(after(part, *away[0][1]), 1) for part in beside]

    (best,) = kernel(
        functools.partial(plane_kernel, rows, False),
        (*own, *beside, *across),
        (lanes,),
        "plane_far",
    )
    (best,) = kernel(
        functools.partial(plane_kernel, rows, True),
        (*own, *own, *near, best),
        (lanes,),
        "plane_near",
    )
    plane = (*own, *near, *beside, *across)
    plane_best = [best] + [jnp.full(lanes.shape, -1.0, jnp.float32)] * (PLANE - 1)
    backs, masks = [], {}
    for n, (pairs, received) in enumerate(away):
        away_best = jnp.full(lanes.shape, -1.0, jnp.float32)
        if n:
            calls = (((0,), (PAD,), received[:1]), ((HEAD,), (0,), received[1:]))
        else:
            calls = (((0, FIRST), (0, PAD), received),)
        tags = received[0] if n else received[-1]
        for starts, bases, parts in calls:
            away_best, *plane_best = kernel(
                functools.partial(cross_kernel, starts, bases),
                (tags, *parts, *plane, away_best, *plane_best),
                (lanes,) * (PLANE + 1),
                "cross",
            )
        backs.append(lax.ppermute(away_best, "dp", [(t, s) for s, t in pairs]))
        if len(pairs) < peers:
            sources = sum(1 << z for z in {s // PLANE for s, _ in pairs})
            sent = (jnp.int32(sources) >> (lax.axis_index("dp") // PLANE)) & 1
            masks[n] = jnp.broadcast_to(sent == 1, (rows,))
    best = plane_best[0].reshape(-1)[:rows]
    for distance in (3, 2, 1):
        backs.append(mate(after(plane_best[distance], *backs[:1]), distance))
    for n, back in enumerate(backs):
        back = back.reshape(-1)[:rows]
        best = jnp.maximum(best, jnp.where(masks[n], back, -1.0) if n in masks else back)
    return best


def solution(mesh):
    in_specs = (P(("groups", "dp"), None), P(("groups", "dp")), P(("groups", "dp")), P("groups"))
    out_specs = P(("groups", "dp"))
    return jax.shard_map(local, mesh=mesh, in_specs=in_specs, out_specs=out_specs, check_vma=False)
```

```python
import functools

import jax
import jax.numpy as jnp
from jax import lax
from jax.experimental import pallas as pl
from jax.experimental.pallas import tpu as pltpu
from jax.sharding import PartitionSpec as P

LABELS = 3
PLANE = 4
PAD = 16
BASE = 64.0
TILE = 256
FIRST = 512
HEAD = 512
VMEM_LIMIT = 24 * 2**20


def whole(count):
    return [pl.BlockSpec(memory_space=pltpu.VMEM)] * count


def params():
    return pltpu.CompilerParams(vmem_limit_bytes=VMEM_LIMIT)


def lanes_shape(rows):
    return jax.ShapeDtypeStruct((-(-rows // 1024) * 8, 128), jnp.float32)


def unit_rows(values):
    squares = jnp.sum(values * values, axis=1, keepdims=True)
    return (values * lax.rsqrt(squares + 1e-06)).astype(jnp.bfloat16)


def first_kernel(embeddings_ref, first_ref):
    for row in range(0, first_ref.shape[0], 128):
        first_ref[row : row + 128, :] = unit_rows(embeddings_ref[row : row + 128, :])


def rest_kernel(rows, embeddings_ref, ints_ref, first_ref, last_ref, head_ref, tail_ref):
    label_row = rows // 128
    owner, label = ints_ref[0:8, :], ints_ref[label_row : label_row + 8, :]
    runs = ints_ref[2 * label_row : 2 * label_row + 1, :]
    first_owner = jnp.take_along_axis(jnp.broadcast_to(runs, owner.shape), owner, axis=1)
    tags = 1 + jnp.where(label == 0, first_owner * LABELS, owner * LABELS + label)
    tags = tags.astype(jnp.float32)
    high = jnp.floor(tags * (1.0 / BASE))
    digits = jnp.concatenate([high, tags - high * BASE], axis=0).astype(jnp.bfloat16)
    width = embeddings_ref.shape[1]
    digits = jnp.concatenate([digits, jnp.zeros((PAD, width - 128), jnp.bfloat16)], axis=1)
    last_ref[0:PAD, :] = digits
    head_ref[0:PAD, :] = digits
    first = first_ref.shape[0]
    head = head_ref.shape[0] - PAD
    head_ref[PAD : PAD + first, :] = first_ref[...]
    for row in range(first, rows, 128):
        unit = unit_rows(embeddings_ref[row : row + 128, :])
        last_ref[PAD + row - first : PAD + row - first + 128, :] = unit
        if row < head:
            head_ref[PAD + row : PAD + row + 128, :] = unit
        else:
            tail_ref[row - head : row - head + 128, :] = unit


def tag_rows(block_ref):
    digits = block_ref[0:PAD, 0:128].astype(jnp.float32)
    return digits[0:8] * BASE + digits[8:16]


def tag_columns(block_ref, first, count):
    tags = tag_rows(block_ref)
    parts = [
        jnp.transpose(jnp.broadcast_to(tags[n : n + 1], (128, 128)))
        for n in range(first // 128, (first + count) // 128)
    ]
    return jnp.concatenate(parts, axis=0)


def dot_rows(values, lanes):
    return lax.dot_general(
        values, lanes, (((1,), (1,)), ((), ())), preferred_element_type=jnp.float32
    )


def unit_parts(refs):
    parts, first = [], 0
    for n, ref in enumerate(refs):
        part = ref if n + 1 < len(refs) else ref.at[PAD:]
        parts.append((first, part))
        first += part.shape[0]
    return parts


def take(refs, counts):
    groups = []
    for count in counts:
        groups.append(refs[:count])
        refs = refs[count:]
    return groups, refs


def fold_sublanes(values):
    rows, lanes = values.shape
    return jnp.max(values.reshape(rows // 8, 8, lanes), axis=0)


def fold_lanes(values):
    return jnp.concatenate(
        [
            jnp.max(jnp.transpose(values[first : first + 128]), axis=0, keepdims=True)
            for first in range(0, values.shape[0], 128)
        ],
        axis=0,
    )


def row_slices(block):
    slices = []
    for first, part in unit_parts(block):
        count = part.shape[0]
        for row in range(0, count, TILE):
            size = min(TILE, count - row)
            slices.append((first + row, part.at[row : row + size]))
    return slices


def plane_kernel(rows, with_self, *refs):
    (own, one, two), refs = take(refs, (2, 2, 2))
    best_ref = refs[-1]
    own_tags = tag_rows(own[-1])
    columns = [tag_columns(block[-1], 0, rows) for block in (one, two)]
    for tile, own_part in row_slices(own):
        lanes = own_part[...]
        best = [jnp.full((8, 128), -1.0, jnp.float32) for _ in range(0, TILE, 128)]
        for which, block in enumerate((one, two)):
            for first, part in row_slices(block):
                count = part.shape[0]
                found = dot_rows(part[...], lanes)
                column = columns[which][first : first + count]
                for n in range(TILE // 128):
                    lane = tile + n * 128
                    match = column == own_tags[lane // 128 : lane // 128 + 1]
                    if with_self and which == 0 and first < lane + 128 and lane < first + count:
                        row_id = lax.broadcasted_iota(jnp.int32, (count, 128), 0) + first
                        lane_id = lax.broadcasted_iota(jnp.int32, (count, 128), 1) + lane
                        match = match & (row_id != lane_id)
                    masked = jnp.where(match, found[:, n * 128 : n * 128 + 128], -1.0)
                    best[n] = jnp.maximum(best[n], fold_sublanes(masked))
        for n in range(TILE // 128):
            place = pl.ds(tile // 128 + n, 1)
            folded = jnp.max(best[n], axis=0, keepdims=True)
            if with_self:
                folded = jnp.maximum(folded, refs[0][place, :])
            best_ref[place, :] = folded


def cross_kernel(starts, bases, *refs):
    (tags, aways), refs = take(refs, (1, len(starts)))
    blocks, refs = take(refs, (2,) * PLANE)
    away_before, away_best = refs[0], refs[PLANE + 1]
    plane_before, plane_best = refs[1 : PLANE + 1], refs[PLANE + 2 :]
    plane_tags = [tag_rows(block[-1]) for block in blocks]
    away_best[...] = away_before[...]
    best = {}
    for start, base, away in zip(starts, bases, aways):
        for tile in range(0, away.shape[0] - base, TILE):
            values = away[base + tile : base + tile + TILE, :]
            column = tag_columns(tags[0], start + tile, TILE)
            row_best = jnp.full((TILE, 128), -1.0, jnp.float32)
            for which in range(PLANE):
                for first, part in row_slices(blocks[which]):
                    found = dot_rows(values, part[...])
                    for lane in range(0, part.shape[0], 128):
                        row = (first + lane) // 128
                        match = column == plane_tags[which][row : row + 1]
                        masked = jnp.where(match, found[:, lane : lane + 128], -1.0)
                        row_best = jnp.maximum(row_best, masked)
                        folded = fold_sublanes(masked)
                        place = which, row
                        best[place] = jnp.maximum(best[place], folded) if place in best else folded
            place = pl.ds((start + tile) // 128, TILE // 128)
            away_best[place, :] = fold_lanes(row_best)
    for which in range(PLANE):
        plane_best[which][...] = plane_before[which][...]
    for (which, row), values in best.items():
        folded = jnp.max(values, axis=0, keepdims=True)
        place = pl.ds(row, 1)
        plane_best[which][place, :] = jnp.maximum(folded, plane_before[which][place, :])


def small_cost():
    return pl.CostEstimate(flops=1, bytes_accessed=1, transcendentals=0)


def plane_steps(planes):
    if planes == 4:
        return [[(0, 3), (1, 0), (2, 1), (3, 2)], [(0, 2), (3, 1)]]
    return [
        [(z, (z + distance) % planes) for z in range(planes)]
        for distance in range(1, planes // 2 + 1)
    ]


def after(value, *others):
    if not others:
        return value
    return lax.optimization_barrier((value,) + others)[0]


def local(embeddings, owner_index, sub_label, run_start):
    rows, width = embeddings.shape
    peers = lax.axis_size("dp")
    planes = peers // PLANE
    lanes = lanes_shape(rows)

    space = -(2 * rows + peers) % 2048
    ints = jnp.concatenate([owner_index, sub_label, run_start, jnp.zeros((space,), jnp.int32)])
    ints = ints.reshape(-1, 128)
    def kernel(body, inputs, outputs, name):
        return pl.pallas_call(
            body,
            out_shape=tuple(outputs),
            in_specs=whole(len(inputs)),
            out_specs=tuple(whole(len(outputs))),
            compiler_params=params(),
            cost_estimate=small_cost(),
            name=name,
        )(*inputs)

    def part_shape(count):
        return jax.ShapeDtypeStruct((count, width), jnp.bfloat16)

    (first,) = kernel(first_kernel, (embeddings,), (part_shape(FIRST),), "first")
    last, head, tail = kernel(
        functools.partial(rest_kernel, rows),
        (embeddings, ints, first),
        (part_shape(PAD + rows - FIRST), part_shape(PAD + HEAD), part_shape(rows - HEAD)),
        "rest",
    )
    own = (first, last)

    def mate(value, distance):
        return lax.ppermute(value, "dp", [(i, i ^ distance) for i in range(peers)])

    away = []
    for n, step in enumerate(plane_steps(planes)):
        pairs = [(z * PLANE + j, t * PLANE + j) for z, t in step for j in range(PLANE)]
        parts = (head, tail) if n else own
        if n > 1:
            parts = [after(part, away[-1][1][-1]) for part in parts]
        away.append((pairs, [lax.ppermute(part, "dp", pairs) for part in parts]))
    beside = [mate(part, 2) for part in own]
    near = [mate(part, 1) for part in own]
    across = [mate(after(part, *away[0][1]), 1) for part in beside]

    (best,) = kernel(
        functools.partial(plane_kernel, rows, False),
        (*own, *beside, *across),
        (lanes,),
        "plane_far",
    )
    (best,) = kernel(
        functools.partial(plane_kernel, rows, True),
        (*own, *own, *near, best),
        (lanes,),
        "plane_near",
    )
    plane = (*own, *near, *beside, *across)
    plane_best = [best] + [jnp.full(lanes.shape, -1.0, jnp.float32)] * (PLANE - 1)
    backs, masks = [], {}
    for n, (pairs, received) in enumerate(away):
        away_best = jnp.full(lanes.shape, -1.0, jnp.float32)
        if n:
            calls = (((0,), (PAD,), received[:1]), ((HEAD,), (0,), received[1:]))
        else:
            calls = (((0, FIRST), (0, PAD), received),)
        tags = received[0] if n else received[-1]
        for starts, bases, parts in calls:
            away_best, *plane_best = kernel(
                functools.partial(cross_kernel, starts, bases),
                (tags, *parts, *plane, away_best, *plane_best),
                (lanes,) * (PLANE + 1),
                "cross",
            )
        backs.append(lax.ppermute(away_best, "dp", [(t, s) for s, t in pairs]))
        if len(pairs) < peers:
            sources = sum(1 << z for z in {s // PLANE for s, _ in pairs})
            sent = (jnp.int32(sources) >> (lax.axis_index("dp") // PLANE)) & 1
            masks[n] = jnp.broadcast_to(sent == 1, (rows,))
    best = plane_best[0].reshape(-1)[:rows]
    for distance in (3, 2, 1):
        backs.append(mate(after(plane_best[distance], *backs[:1]), distance))
    for n, back in enumerate(backs):
        back = back.reshape(-1)[:rows]
        best = jnp.maximum(best, jnp.where(masks[n], back, -1.0) if n in masks else back)
    return best


def solution(mesh):
    in_specs = (P(("groups", "dp"), None), P(("groups", "dp")), P(("groups", "dp")), P("groups"))
    out_specs = P(("groups", "dp"))
    return jax.shard_map(local, mesh=mesh, in_specs=in_specs, out_specs=out_specs, check_vma=False)
```

```python
import functools

import jax
import jax.numpy as jnp
from jax import lax
from jax.experimental import pallas as pl
from jax.experimental.pallas import tpu as pltpu
from jax.sharding import PartitionSpec as P

LABELS = 3
PLANE = 4
PAD = 16
BASE = 64.0
TILE = 256
FIRST = 512
VMEM_LIMIT = 24 * 2**20


def whole(count):
    return [pl.BlockSpec(memory_space=pltpu.VMEM)] * count


def params():
    return pltpu.CompilerParams(vmem_limit_bytes=VMEM_LIMIT)


def lanes_shape(rows):
    return jax.ShapeDtypeStruct((-(-rows // 1024) * 8, 128), jnp.float32)


def unit_rows(values):
    squares = jnp.sum(values * values, axis=1, keepdims=True)
    return (values * lax.rsqrt(squares + 1e-06)).astype(jnp.bfloat16)


def first_kernel(embeddings_ref, first_ref):
    for row in range(0, first_ref.shape[0], 128):
        first_ref[row : row + 128, :] = unit_rows(embeddings_ref[row : row + 128, :])


def rest_kernel(
    rows, embeddings_ref, ints_ref, first_ref, tags_ref, last_ref, block_ref, tail_ref
):
    label_row = rows // 128
    owner, label = ints_ref[0:8, :], ints_ref[label_row : label_row + 8, :]
    runs = ints_ref[2 * label_row : 2 * label_row + 1, :]
    first_owner = jnp.take_along_axis(jnp.broadcast_to(runs, owner.shape), owner, axis=1)
    tags = 1 + jnp.where(label == 0, first_owner * LABELS, owner * LABELS + label)
    tags = tags.astype(jnp.float32)
    high = jnp.floor(tags * (1.0 / BASE))
    digits = jnp.concatenate([high, tags - high * BASE], axis=0).astype(jnp.bfloat16)
    tags_ref[...] = digits
    width = embeddings_ref.shape[1]
    digits = jnp.concatenate([digits, jnp.zeros((PAD, width - 128), jnp.bfloat16)], axis=1)
    first = first_ref.shape[0]
    last_ref[0:PAD, :] = digits
    block_ref[0:PAD, :] = digits
    block_ref[PAD : PAD + first, :] = first_ref[...]
    for row in range(first, rows, 128):
        unit = unit_rows(embeddings_ref[row : row + 128, :])
        last_ref[PAD + row - first : PAD + row - first + 128, :] = unit
        block_ref[PAD + row : PAD + row + 128, :] = unit
        tail_ref[row - first : row - first + 128, :] = unit


def tag_rows(block_ref):
    digits = block_ref[0:PAD, 0:128].astype(jnp.float32)
    return digits[0:8] * BASE + digits[8:16]


def tag_columns(block_ref, first, count):
    tags = tag_rows(block_ref)
    parts = [
        jnp.transpose(jnp.broadcast_to(tags[n : n + 1], (128, 128)))
        for n in range(first // 128, (first + count) // 128)
    ]
    return jnp.concatenate(parts, axis=0)


def dot_rows(values, lanes):
    return lax.dot_general(
        values, lanes, (((1,), (1,)), ((), ())), preferred_element_type=jnp.float32
    )


def unit_parts(refs):
    parts, first = [], 0
    for n, ref in enumerate(refs):
        part = ref if n + 1 < len(refs) else ref.at[PAD:]
        parts.append((first, part))
        first += part.shape[0]
    return parts


def take(refs, counts):
    groups = []
    for count in counts:
        groups.append(refs[:count])
        refs = refs[count:]
    return groups, refs


def fold_sublanes(values):
    rows, lanes = values.shape
    return jnp.max(values.reshape(rows // 8, 8, lanes), axis=0)


def fold_lanes(values):
    return jnp.concatenate(
        [
            jnp.max(jnp.transpose(values[first : first + 128]), axis=0, keepdims=True)
            for first in range(0, values.shape[0], 128)
        ],
        axis=0,
    )


def row_slices(block):
    slices = []
    for first, part in unit_parts(block):
        count = part.shape[0]
        for row in range(0, count, TILE):
            size = min(TILE, count - row)
            slices.append((first + row, part.at[row : row + size]))
    return slices


def plane_kernel(rows, with_self, *refs):
    (own, one, two), refs = take(refs, (2, 2, 2))
    best_ref = refs[-1]
    own_tags = tag_rows(own[-1])
    columns = [tag_columns(block[-1], 0, rows) for block in (one, two)]
    for tile, own_part in row_slices(own):
        lanes = own_part[...]
        best = [jnp.full((8, 128), -1.0, jnp.float32) for _ in range(0, TILE, 128)]
        for which, block in enumerate((one, two)):
            for first, part in row_slices(block):
                count = part.shape[0]
                found = dot_rows(part[...], lanes)
                column = columns[which][first : first + count]
                for n in range(TILE // 128):
                    lane = tile + n * 128
                    match = column == own_tags[lane // 128 : lane // 128 + 1]
                    if with_self and which == 0 and first < lane + 128 and lane < first + count:
                        row_id = lax.broadcasted_iota(jnp.int32, (count, 128), 0) + first
                        lane_id = lax.broadcasted_iota(jnp.int32, (count, 128), 1) + lane
                        match = match & (row_id != lane_id)
                    masked = jnp.where(match, found[:, n * 128 : n * 128 + 128], -1.0)
                    best[n] = jnp.maximum(best[n], fold_sublanes(masked))
        for n in range(TILE // 128):
            place = pl.ds(tile // 128 + n, 1)
            folded = jnp.max(best[n], axis=0, keepdims=True)
            if with_self:
                folded = jnp.maximum(folded, refs[0][place, :])
            best_ref[place, :] = folded


def cross_kernel(start, base, *refs):
    (tags, (away,)), refs = take(refs, (1, 1))
    blocks, refs = take(refs, (2,) * PLANE)
    away_before, away_best = refs[0], refs[PLANE + 1]
    plane_before, plane_best = refs[1 : PLANE + 1], refs[PLANE + 2 :]
    plane_tags = [tag_rows(block[-1]) for block in blocks]
    away_best[...] = away_before[...]
    best = {}
    for tile in range(0, away.shape[0] - base, TILE):
        values = away[base + tile : base + tile + TILE, :]
        column = tag_columns(tags[0], start + tile, TILE)
        row_best = jnp.full((TILE, 128), -1.0, jnp.float32)
        for which in range(PLANE):
            for first, part in row_slices(blocks[which]):
                found = dot_rows(values, part[...])
                for lane in range(0, part.shape[0], 128):
                    row = (first + lane) // 128
                    match = column == plane_tags[which][row : row + 1]
                    masked = jnp.where(match, found[:, lane : lane + 128], -1.0)
                    row_best = jnp.maximum(row_best, masked)
                    folded = fold_sublanes(masked)
                    place = which, row
                    best[place] = jnp.maximum(best[place], folded) if place in best else folded
        place = pl.ds((start + tile) // 128, TILE // 128)
        away_best[place, :] = fold_lanes(row_best)
    for which in range(PLANE):
        plane_best[which][...] = plane_before[which][...]
    for (which, row), values in best.items():
        folded = jnp.max(values, axis=0, keepdims=True)
        place = pl.ds(row, 1)
        plane_best[which][place, :] = jnp.maximum(folded, plane_before[which][place, :])


def small_cost():
    return pl.CostEstimate(flops=1, bytes_accessed=1, transcendentals=0)


def plane_steps(planes):
    if planes == 4:
        return [[(0, 2), (1, 0), (2, 3), (3, 1)], [(0, 3), (2, 1)]]
    return [
        [(z, (z + distance) % planes) for z in range(planes)]
        for distance in range(1, planes // 2 + 1)
    ]


def after(value, *others):
    if not others:
        return value
    return lax.optimization_barrier((value,) + others)[0]


def local(embeddings, owner_index, sub_label, run_start):
    rows, width = embeddings.shape
    peers = lax.axis_size("dp")
    planes = peers // PLANE
    lanes = lanes_shape(rows)

    space = -(2 * rows + peers) % 2048
    ints = jnp.concatenate([owner_index, sub_label, run_start, jnp.zeros((space,), jnp.int32)])
    ints = ints.reshape(-1, 128)
    def kernel(body, inputs, outputs, name):
        return pl.pallas_call(
            body,
            out_shape=tuple(outputs),
            in_specs=whole(len(inputs)),
            out_specs=tuple(whole(len(outputs))),
            compiler_params=params(),
            cost_estimate=small_cost(),
            name=name,
        )(*inputs)

    def part_shape(count):
        return jax.ShapeDtypeStruct((count, width), jnp.bfloat16)

    (first,) = kernel(first_kernel, (embeddings,), (part_shape(FIRST),), "first")
    tags, last, block, tail = kernel(
        functools.partial(rest_kernel, rows),
        (embeddings, ints, first),
        (
            jax.ShapeDtypeStruct((PAD, 128), jnp.bfloat16),
            part_shape(PAD + rows - FIRST),
            part_shape(PAD + rows),
            part_shape(rows - FIRST),
        ),
        "rest",
    )
    own = (first, last)

    def mate(value, distance):
        return lax.ppermute(value, "dp", [(i, i ^ distance) for i in range(peers)])

    def moved(value, step, back=False):
        pairs = [(z * PLANE + j, t * PLANE + j) for z, t in step for j in range(PLANE)]
        return lax.ppermute(value, "dp", [(t, s) for s, t in pairs] if back else pairs)

    split, *others = plane_steps(planes)
    away = [moved(first, split)]
    for n, step in enumerate(others):
        away.append(moved(after(block, away[-1]) if n else block, step))
    away_tags = moved(tags, split)
    away_tail = moved(tail, split)
    beside = [mate(part, 2) for part in own]
    near = [mate(part, 1) for part in own]
    across = [mate(after(part, away[0], away_tags), 1) for part in beside]

    (best,) = kernel(
        functools.partial(plane_kernel, rows, False),
        (*own, *beside, *across),
        (lanes,),
        "plane_far",
    )
    (best,) = kernel(
        functools.partial(plane_kernel, rows, True),
        (*own, *own, *near, best),
        (lanes,),
        "plane_near",
    )
    plane = (*own, *near, *beside, *across)
    plane_best = [best] + [jnp.full(lanes.shape, -1.0, jnp.float32)] * (PLANE - 1)
    backs, masks = [], {}
    empty = jnp.full(lanes.shape, -1.0, jnp.float32)

    def crossed(part, part_tags, start, base, away_best, plane_best):
        away_best, *plane_best = kernel(
            functools.partial(cross_kernel, start, base),
            (part_tags, part, *plane, away_best, *plane_best),
            (lanes,) * (PLANE + 1),
            "cross",
        )
        return away_best, plane_best

    split_best, plane_best = crossed(away[0], away_tags, 0, 0, empty, plane_best)
    for n, step in enumerate(others):
        part = away[n + 1]
        away_best, plane_best = crossed(part, part, 0, PAD, empty, plane_best)
        backs.append(moved(away_best, step, back=True))
        if len(step) < planes:
            sources = sum(1 << z for z, _ in step)
            sent = (jnp.int32(sources) >> (lax.axis_index("dp") // PLANE)) & 1
            masks[n] = jnp.broadcast_to(sent == 1, (rows,))
    split_best, plane_best = crossed(away_tail, away_tags, FIRST, 0, split_best, plane_best)
    first_backs = tuple(backs)
    backs.append(moved(split_best, split, back=True))
    best = plane_best[0].reshape(-1)[:rows]
    for distance in (3, 2, 1):
        backs.append(mate(after(plane_best[distance], *first_backs), distance))
    for n, back in enumerate(backs):
        back = back.reshape(-1)[:rows]
        best = jnp.maximum(best, jnp.where(masks[n], back, -1.0) if n in masks else back)
    return best


def solution(mesh):
    in_specs = (P(("groups", "dp"), None), P(("groups", "dp")), P(("groups", "dp")), P("groups"))
    out_specs = P(("groups", "dp"))
    return jax.shard_map(local, mesh=mesh, in_specs=in_specs, out_specs=out_specs, check_vma=False)
```

```python
import functools

import jax
import jax.numpy as jnp
from jax import lax
from jax.experimental import pallas as pl
from jax.experimental.pallas import tpu as pltpu
from jax.sharding import PartitionSpec as P

LABELS = 3
PLANE = 4
PAD = 16
BASE = 64.0
TILE = 256
FIRST = 512
LATE = 128
HALF = 640
VMEM_LIMIT = 24 * 2**20


def whole(count):
    return [pl.BlockSpec(memory_space=pltpu.VMEM)] * count


def params():
    return pltpu.CompilerParams(vmem_limit_bytes=VMEM_LIMIT)


def lanes_shape(rows):
    return jax.ShapeDtypeStruct((-(-rows // 1024) * 8, 128), jnp.float32)


def unit_rows(values):
    squares = jnp.sum(values * values, axis=1, keepdims=True)
    return (values * lax.rsqrt(squares + 1e-06)).astype(jnp.bfloat16)


def first_kernel(embeddings_ref, first_ref):
    for row in range(0, first_ref.shape[0], 128):
        first_ref[row : row + 128, :] = unit_rows(embeddings_ref[row : row + 128, :])


def rest_kernel(
    rows, embeddings_ref, ints_ref, first_ref, next_ref, last_ref, head_ref, half_ref, tail_ref
):
    label_row = rows // 128
    owner, label = ints_ref[0:8, :], ints_ref[label_row : label_row + 8, :]
    runs = ints_ref[2 * label_row : 2 * label_row + 1, :]
    first_owner = jnp.take_along_axis(jnp.broadcast_to(runs, owner.shape), owner, axis=1)
    tags = 1 + jnp.where(label == 0, first_owner * LABELS, owner * LABELS + label)
    tags = tags.astype(jnp.float32)
    high = jnp.floor(tags * (1.0 / BASE))
    digits = jnp.concatenate([high, tags - high * BASE], axis=0).astype(jnp.bfloat16)
    width = embeddings_ref.shape[1]
    digits = jnp.concatenate([digits, jnp.zeros((PAD, width - 128), jnp.bfloat16)], axis=1)
    first = first_ref.shape[0]
    next_ref[0:PAD, :] = digits
    last_ref[0:PAD, :] = digits
    head_ref[0:PAD, :] = digits
    head_ref[PAD : PAD + first, :] = first_ref[...]
    for row in range(first, rows, 128):
        unit = unit_rows(embeddings_ref[row : row + 128, :])
        last_ref[PAD + row - first : PAD + row - first + 128, :] = unit
        if row < HALF:
            head_ref[PAD + row : PAD + row + 128, :] = unit
        else:
            half_ref[row - HALF : row - HALF + 128, :] = unit
        late = row - (rows - LATE)
        if late < 0:
            next_ref[PAD + row - first : PAD + row - first + 128, :] = unit
        else:
            tail_ref[late : late + 128, :] = unit


def tag_rows(block_ref):
    digits = block_ref[0:PAD, 0:128].astype(jnp.float32)
    return digits[0:8] * BASE + digits[8:16]


def tag_columns(block_ref, first, count):
    tags = tag_rows(block_ref)
    parts = [
        jnp.transpose(jnp.broadcast_to(tags[n : n + 1], (128, 128)))
        for n in range(first // 128, (first + count) // 128)
    ]
    return jnp.concatenate(parts, axis=0)


def dot_rows(values, lanes):
    return lax.dot_general(
        values, lanes, (((1,), (1,)), ((), ())), preferred_element_type=jnp.float32
    )


def unit_parts(refs):
    parts, first = [], 0
    for n, ref in enumerate(refs):
        part = ref if n + 1 < len(refs) else ref.at[PAD:]
        parts.append((first, part))
        first += part.shape[0]
    return parts


def take(refs, counts):
    groups = []
    for count in counts:
        groups.append(refs[:count])
        refs = refs[count:]
    return groups, refs


def fold_sublanes(values):
    rows, lanes = values.shape
    return jnp.max(values.reshape(rows // 8, 8, lanes), axis=0)


def fold_lanes(values):
    return jnp.concatenate(
        [
            jnp.max(jnp.transpose(values[first : first + 128]), axis=0, keepdims=True)
            for first in range(0, values.shape[0], 128)
        ],
        axis=0,
    )


def row_slices(block):
    slices = []
    for first, part in unit_parts(block):
        count = part.shape[0]
        for row in range(0, count, TILE):
            size = min(TILE, count - row)
            slices.append((first + row, part.at[row : row + size]))
    return slices


def plane_kernel(rows, with_self, *refs):
    (own, one, two), refs = take(refs, (2, 2, 2))
    best_ref = refs[-1]
    own_tags = tag_rows(own[-1])
    columns = [tag_columns(block[-1], 0, rows) for block in (one, two)]
    for tile, own_part in row_slices(own):
        lanes = own_part[...]
        best = [jnp.full((8, 128), -1.0, jnp.float32) for _ in range(0, TILE, 128)]
        for which, block in enumerate((one, two)):
            for first, part in row_slices(block):
                count = part.shape[0]
                found = dot_rows(part[...], lanes)
                column = columns[which][first : first + count]
                for n in range(TILE // 128):
                    lane = tile + n * 128
                    match = column == own_tags[lane // 128 : lane // 128 + 1]
                    if with_self and which == 0 and first < lane + 128 and lane < first + count:
                        row_id = lax.broadcasted_iota(jnp.int32, (count, 128), 0) + first
                        lane_id = lax.broadcasted_iota(jnp.int32, (count, 128), 1) + lane
                        match = match & (row_id != lane_id)
                    masked = jnp.where(match, found[:, n * 128 : n * 128 + 128], -1.0)
                    best[n] = jnp.maximum(best[n], fold_sublanes(masked))
        for n in range(TILE // 128):
            place = pl.ds(tile // 128 + n, 1)
            folded = jnp.max(best[n], axis=0, keepdims=True)
            if with_self:
                folded = jnp.maximum(folded, refs[0][place, :])
            best_ref[place, :] = folded


def cross_kernel(start, base, *refs):
    (tags, (away,)), refs = take(refs, (1, 1))
    blocks, refs = take(refs, (2,) * PLANE)
    away_before, away_best = refs[0], refs[PLANE + 1]
    plane_before, plane_best = refs[1 : PLANE + 1], refs[PLANE + 2 :]
    plane_tags = [tag_rows(block[-1]) for block in blocks]
    away_best[...] = away_before[...]
    best = {}
    for tile in range(0, away.shape[0] - base, TILE):
        count = min(TILE, away.shape[0] - base - tile)
        values = away[base + tile : base + tile + count, :]
        column = tag_columns(tags[0], start + tile, count)
        row_best = jnp.full((count, 128), -1.0, jnp.float32)
        for which in range(PLANE):
            for first, part in row_slices(blocks[which]):
                found = dot_rows(values, part[...])
                for lane in range(0, part.shape[0], 128):
                    row = (first + lane) // 128
                    match = column == plane_tags[which][row : row + 1]
                    masked = jnp.where(match, found[:, lane : lane + 128], -1.0)
                    row_best = jnp.maximum(row_best, masked)
                    folded = fold_sublanes(masked)
                    place = which, row
                    best[place] = jnp.maximum(best[place], folded) if place in best else folded
        place = pl.ds((start + tile) // 128, count // 128)
        away_best[place, :] = fold_lanes(row_best)
    for which in range(PLANE):
        plane_best[which][...] = plane_before[which][...]
    for (which, row), values in best.items():
        folded = jnp.max(values, axis=0, keepdims=True)
        place = pl.ds(row, 1)
        plane_best[which][place, :] = jnp.maximum(folded, plane_before[which][place, :])


def small_cost():
    return pl.CostEstimate(flops=1, bytes_accessed=1, transcendentals=0)


def plane_steps(planes):
    if planes == 4:
        return [[(0, 2), (1, 0), (2, 3), (3, 1)], [(0, 3), (2, 1)]]
    return [
        [(z, (z + distance) % planes) for z in range(planes)]
        for distance in range(1, planes // 2 + 1)
    ]


def after(value, *others):
    if not others:
        return value
    return lax.optimization_barrier((value,) + others)[0]


def local(embeddings, owner_index, sub_label, run_start):
    rows, width = embeddings.shape
    peers = lax.axis_size("dp")
    planes = peers // PLANE
    lanes = lanes_shape(rows)

    space = -(2 * rows + peers) % 2048
    ints = jnp.concatenate([owner_index, sub_label, run_start, jnp.zeros((space,), jnp.int32)])
    ints = ints.reshape(-1, 128)
    def kernel(body, inputs, outputs, name):
        return pl.pallas_call(
            body,
            out_shape=tuple(outputs),
            in_specs=whole(len(inputs)),
            out_specs=tuple(whole(len(outputs))),
            compiler_params=params(),
            cost_estimate=small_cost(),
            name=name,
        )(*inputs)

    def part_shape(count):
        return jax.ShapeDtypeStruct((count, width), jnp.bfloat16)

    (first,) = kernel(first_kernel, (embeddings,), (part_shape(FIRST),), "first")
    after_first, last, head, half, tail = kernel(
        functools.partial(rest_kernel, rows),
        (embeddings, ints, first),
        (
            part_shape(PAD + rows - FIRST - LATE),
            part_shape(PAD + rows - FIRST),
            part_shape(PAD + HALF),
            part_shape(rows - HALF),
            part_shape(LATE),
        ),
        "rest",
    )
    own = (first, last)

    def mate(value, distance):
        return lax.ppermute(value, "dp", [(i, i ^ distance) for i in range(peers)])

    def moved(value, step, back=False):
        pairs = [(z * PLANE + j, t * PLANE + j) for z, t in step for j in range(PLANE)]
        return lax.ppermute(value, "dp", [(t, s) for s, t in pairs] if back else pairs)

    split, *others = plane_steps(planes)
    away = [moved(first, split)]
    for n, step in enumerate(others):
        parts = [after(part, *away[-1]) if n else part for part in (head, half)]
        away.append([moved(part, step) for part in parts])
    away_next = moved(after_first, split)
    away_tail = moved(tail, split)
    beside = [mate(part, 2) for part in own]
    near = [mate(part, 1) for part in own]
    across = [mate(after(part, away[0], away_next), 1) for part in beside]

    (best,) = kernel(
        functools.partial(plane_kernel, rows, False),
        (*own, *beside, *across),
        (lanes,),
        "plane_far",
    )
    (best,) = kernel(
        functools.partial(plane_kernel, rows, True),
        (*own, *own, *near, best),
        (lanes,),
        "plane_near",
    )
    plane = (*own, *near, *beside, *across)
    plane_best = [best] + [jnp.full(lanes.shape, -1.0, jnp.float32)] * (PLANE - 1)
    backs, masks = [], {}
    empty = jnp.full(lanes.shape, -1.0, jnp.float32)

    def crossed(part, part_tags, start, base, away_best, plane_best):
        away_best, *plane_best = kernel(
            functools.partial(cross_kernel, start, base),
            (part_tags, part, *plane, away_best, *plane_best),
            (lanes,) * (PLANE + 1),
            "cross",
        )
        return away_best, plane_best

    split_best, plane_best = crossed(away[0], away_next, 0, 0, empty, plane_best)
    split_best, plane_best = crossed(away_next, away_next, FIRST, PAD, split_best, plane_best)
    for n, step in enumerate(others):
        one, two = away[n + 1]
        away_best, plane_best = crossed(one, one, 0, PAD, empty, plane_best)
        away_best, plane_best = crossed(two, one, HALF, 0, away_best, plane_best)
        backs.append(moved(away_best, step, back=True))
        if len(step) < planes:
            sources = sum(1 << z for z, _ in step)
            sent = (jnp.int32(sources) >> (lax.axis_index("dp") // PLANE)) & 1
            masks[n] = jnp.broadcast_to(sent == 1, (rows,))
    split_best, plane_best = crossed(away_tail, away_next, rows - LATE, 0, split_best, plane_best)
    first_backs = tuple(backs)
    backs.append(moved(split_best, split, back=True))
    best = plane_best[0].reshape(-1)[:rows]
    for distance in (3, 2, 1):
        backs.append(mate(after(plane_best[distance], *first_backs), distance))
    for n, back in enumerate(backs):
        back = back.reshape(-1)[:rows]
        best = jnp.maximum(best, jnp.where(masks[n], back, -1.0) if n in masks else back)
    return best


def solution(mesh):
    in_specs = (P(("groups", "dp"), None), P(("groups", "dp")), P(("groups", "dp")), P("groups"))
    out_specs = P(("groups", "dp"))
    return jax.shard_map(local, mesh=mesh, in_specs=in_specs, out_specs=out_specs, check_vma=False)
```

```python
import functools

import jax
import jax.numpy as jnp
from jax import lax
from jax.experimental import pallas as pl
from jax.experimental.pallas import tpu as pltpu
from jax.sharding import PartitionSpec as P

LABELS = 3
PLANE = 4
PAD = 16
BASE = 64.0
TILE = 256
FIRST = 512
HEAD = 512
VMEM_LIMIT = 24 * 2**20


def whole(count):
    return [pl.BlockSpec(memory_space=pltpu.VMEM)] * count


def params():
    return pltpu.CompilerParams(vmem_limit_bytes=VMEM_LIMIT)


def lanes_shape(rows):
    return jax.ShapeDtypeStruct((-(-rows // 1024) * 8, 128), jnp.float32)


def unit_rows(values):
    squares = jnp.sum(values * values, axis=1, keepdims=True)
    return (values * lax.rsqrt(squares + 1e-06)).astype(jnp.bfloat16)


def first_kernel(embeddings_ref, first_ref):
    for row in range(0, first_ref.shape[0], 128):
        first_ref[row : row + 128, :] = unit_rows(embeddings_ref[row : row + 128, :])


def rest_kernel(rows, embeddings_ref, ints_ref, first_ref, last_ref, head_ref, tail_ref):
    label_row = rows // 128
    owner, label = ints_ref[0:8, :], ints_ref[label_row : label_row + 8, :]
    runs = ints_ref[2 * label_row : 2 * label_row + 1, :]
    first_owner = jnp.take_along_axis(jnp.broadcast_to(runs, owner.shape), owner, axis=1)
    tags = 1 + jnp.where(label == 0, first_owner * LABELS, owner * LABELS + label)
    tags = tags.astype(jnp.float32)
    high = jnp.floor(tags * (1.0 / BASE))
    digits = jnp.concatenate([high, tags - high * BASE], axis=0).astype(jnp.bfloat16)
    width = embeddings_ref.shape[1]
    digits = jnp.concatenate([digits, jnp.zeros((PAD, width - 128), jnp.bfloat16)], axis=1)
    last_ref[0:PAD, :] = digits
    head_ref[0:PAD, :] = digits
    first = first_ref.shape[0]
    head = head_ref.shape[0] - PAD
    head_ref[PAD : PAD + first, :] = first_ref[...]
    for row in range(first, rows, 128):
        unit = unit_rows(embeddings_ref[row : row + 128, :])
        last_ref[PAD + row - first : PAD + row - first + 128, :] = unit
        if row < head:
            head_ref[PAD + row : PAD + row + 128, :] = unit
        else:
            tail_ref[row - head : row - head + 128, :] = unit


def tag_rows(block_ref):
    digits = block_ref[0:PAD, 0:128].astype(jnp.float32)
    return digits[0:8] * BASE + digits[8:16]


def tag_columns(block_ref, first, count):
    tags = tag_rows(block_ref)
    parts = [
        jnp.transpose(jnp.broadcast_to(tags[n : n + 1], (128, 128)))
        for n in range(first // 128, (first + count) // 128)
    ]
    return jnp.concatenate(parts, axis=0)


def dot_rows(values, lanes):
    return lax.dot_general(
        values, lanes, (((1,), (1,)), ((), ())), preferred_element_type=jnp.float32
    )


def unit_parts(refs):
    parts, first = [], 0
    for n, ref in enumerate(refs):
        part = ref if n + 1 < len(refs) else ref.at[PAD:]
        parts.append((first, part))
        first += part.shape[0]
    return parts


def take(refs, counts):
    groups = []
    for count in counts:
        groups.append(refs[:count])
        refs = refs[count:]
    return groups, refs


def fold_sublanes(values):
    rows, lanes = values.shape
    return jnp.max(values.reshape(rows // 8, 8, lanes), axis=0)


def fold_lanes(values):
    return jnp.concatenate(
        [
            jnp.max(jnp.transpose(values[first : first + 128]), axis=0, keepdims=True)
            for first in range(0, values.shape[0], 128)
        ],
        axis=0,
    )


def row_slices(block):
    slices = []
    for first, part in unit_parts(block):
        count = part.shape[0]
        for row in range(0, count, TILE):
            size = min(TILE, count - row)
            slices.append((first + row, part.at[row : row + size]))
    return slices


def plane_kernel(rows, with_self, *refs):
    (own, one, two), refs = take(refs, (2, 2, 2))
    best_ref = refs[-1]
    own_tags = tag_rows(own[-1])
    columns = [tag_columns(block[-1], 0, rows) for block in (one, two)]
    for tile, own_part in row_slices(own):
        lanes = own_part[...]
        best = [jnp.full((8, 128), -1.0, jnp.float32) for _ in range(0, TILE, 128)]
        for which, block in enumerate((one, two)):
            for first, part in row_slices(block):
                count = part.shape[0]
                found = dot_rows(part[...], lanes)
                column = columns[which][first : first + count]
                for n in range(TILE // 128):
                    lane = tile + n * 128
                    match = column == own_tags[lane // 128 : lane // 128 + 1]
                    if with_self and which == 0 and first < lane + 128 and lane < first + count:
                        row_id = lax.broadcasted_iota(jnp.int32, (count, 128), 0) + first
                        lane_id = lax.broadcasted_iota(jnp.int32, (count, 128), 1) + lane
                        match = match & (row_id != lane_id)
                    masked = jnp.where(match, found[:, n * 128 : n * 128 + 128], -1.0)
                    best[n] = jnp.maximum(best[n], fold_sublanes(masked))
        for n in range(TILE // 128):
            place = pl.ds(tile // 128 + n, 1)
            folded = jnp.max(best[n], axis=0, keepdims=True)
            if with_self:
                folded = jnp.maximum(folded, refs[0][place, :])
            best_ref[place, :] = folded


def cross_kernel(starts, bases, *refs):
    (tags, aways), refs = take(refs, (1, len(starts)))
    blocks, refs = take(refs, (2,) * PLANE)
    away_before, away_best = refs[0], refs[PLANE + 1]
    plane_before, plane_best = refs[1 : PLANE + 1], refs[PLANE + 2 :]
    plane_tags = [tag_rows(block[-1]) for block in blocks]
    away_best[...] = away_before[...]
    best = {}
    for start, base, away in zip(starts, bases, aways):
        for tile in range(0, away.shape[0] - base, TILE):
            values = away[base + tile : base + tile + TILE, :]
            column = tag_columns(tags[0], start + tile, TILE)
            row_best = jnp.full((TILE, 128), -1.0, jnp.float32)
            for which in range(PLANE):
                for first, part in row_slices(blocks[which]):
                    found = dot_rows(values, part[...])
                    for lane in range(0, part.shape[0], 128):
                        row = (first + lane) // 128
                        match = column == plane_tags[which][row : row + 1]
                        masked = jnp.where(match, found[:, lane : lane + 128], -1.0)
                        row_best = jnp.maximum(row_best, masked)
                        folded = fold_sublanes(masked)
                        place = which, row
                        best[place] = jnp.maximum(best[place], folded) if place in best else folded
            place = pl.ds((start + tile) // 128, TILE // 128)
            away_best[place, :] = fold_lanes(row_best)
    for which in range(PLANE):
        plane_best[which][...] = plane_before[which][...]
    for (which, row), values in best.items():
        folded = jnp.max(values, axis=0, keepdims=True)
        place = pl.ds(row, 1)
        plane_best[which][place, :] = jnp.maximum(folded, plane_before[which][place, :])


def small_cost():
    return pl.CostEstimate(flops=1, bytes_accessed=1, transcendentals=0)


def plane_steps(planes):
    if planes == 4:
        return [[(0, 2), (1, 0), (2, 3), (3, 1)], [(3, 0), (1, 2)]]
    return [
        [(z, (z + distance) % planes) for z in range(planes)]
        for distance in range(1, planes // 2 + 1)
    ]


def after(value, *others):
    if not others:
        return value
    return lax.optimization_barrier((value,) + others)[0]


def local(embeddings, owner_index, sub_label, run_start):
    rows, width = embeddings.shape
    peers = lax.axis_size("dp")
    planes = peers // PLANE
    lanes = lanes_shape(rows)

    space = -(2 * rows + peers) % 2048
    ints = jnp.concatenate([owner_index, sub_label, run_start, jnp.zeros((space,), jnp.int32)])
    ints = ints.reshape(-1, 128)
    def kernel(body, inputs, outputs, name):
        return pl.pallas_call(
            body,
            out_shape=tuple(outputs),
            in_specs=whole(len(inputs)),
            out_specs=tuple(whole(len(outputs))),
            compiler_params=params(),
            cost_estimate=small_cost(),
            name=name,
        )(*inputs)

    def part_shape(count):
        return jax.ShapeDtypeStruct((count, width), jnp.bfloat16)

    (first,) = kernel(first_kernel, (embeddings,), (part_shape(FIRST),), "first")
    last, head, tail = kernel(
        functools.partial(rest_kernel, rows),
        (embeddings, ints, first),
        (part_shape(PAD + rows - FIRST), part_shape(PAD + HEAD), part_shape(rows - HEAD)),
        "rest",
    )
    own = (first, last)

    def mate(value, distance):
        return lax.ppermute(value, "dp", [(i, i ^ distance) for i in range(peers)])

    away = []
    for n, step in enumerate(plane_steps(planes)):
        pairs = [(z * PLANE + j, t * PLANE + j) for z, t in step for j in range(PLANE)]
        parts = (head, tail) if n else own
        if n > 1:
            parts = [after(part, away[-1][1][-1]) for part in parts]
        away.append((pairs, [lax.ppermute(part, "dp", pairs) for part in parts]))
    beside = [mate(part, 2) for part in own]
    near = [mate(part, 1) for part in own]
    across = [mate(after(part, *away[0][1]), 1) for part in beside]

    (best,) = kernel(
        functools.partial(plane_kernel, rows, False),
        (*own, *beside, *across),
        (lanes,),
        "plane_far",
    )
    (best,) = kernel(
        functools.partial(plane_kernel, rows, True),
        (*own, *own, *near, best),
        (lanes,),
        "plane_near",
    )
    plane = (*own, *near, *beside, *across)
    plane_best = [best] + [jnp.full(lanes.shape, -1.0, jnp.float32)] * (PLANE - 1)
    backs = []
    for n, (pairs, received) in enumerate(away):
        away_best = jnp.full(lanes.shape, -1.0, jnp.float32)
        if n:
            calls = (((0,), (PAD,), received[:1]), ((HEAD,), (0,), received[1:]))
        else:
            calls = (((0, FIRST), (0, PAD), received),)
        tags = received[0] if n else received[-1]
        for starts, bases, parts in calls:
            away_best, *plane_best = kernel(
                functools.partial(cross_kernel, starts, bases),
                (tags, *parts, *plane, away_best, *plane_best),
                (lanes,) * (PLANE + 1),
                "cross",
            )
        answer = after(away_best, *(back for back, _ in backs[:1]))
        back = lax.ppermute(answer, "dp", [(t, s) for s, t in pairs]).reshape(-1)[:rows]
        sent = None
        if len(pairs) < peers:
            sources = sum(1 << z for z in {s // PLANE for s, _ in pairs})
            sent = (jnp.int32(sources) >> (lax.axis_index("dp") // PLANE)) & 1
        backs.append((back, sent))
    best = plane_best[0].reshape(-1)[:rows]
    for distance in (3, 2, 1):
        back = mate(after(plane_best[distance], backs[0][0]), distance)
        backs.insert(-1, (back.reshape(-1)[:rows], None))
    for back, sent in backs:
        best = jnp.maximum(back if sent is None else jnp.where(sent == 1, back, -1.0), best)
    return best


def solution(mesh):
    in_specs = (P(("groups", "dp"), None), P(("groups", "dp")), P(("groups", "dp")), P("groups"))
    out_specs = P(("groups", "dp"))
    return jax.shard_map(local, mesh=mesh, in_specs=in_specs, out_specs=out_specs, check_vma=False)
```

```python
import functools

import jax
import jax.numpy as jnp
from jax import lax
from jax.experimental import pallas as pl
from jax.experimental.pallas import tpu as pltpu
from jax.sharding import PartitionSpec as P

LABELS = 3
PLANE = 4
PAD = 16
BASE = 64.0
TILE = 256
FIRST = 512
HEAD = 512
VMEM_LIMIT = 24 * 2**20


def whole(count):
    return [pl.BlockSpec(memory_space=pltpu.VMEM)] * count


def params():
    return pltpu.CompilerParams(vmem_limit_bytes=VMEM_LIMIT)


def lanes_shape(rows):
    return jax.ShapeDtypeStruct((-(-rows // 1024) * 8, 128), jnp.float32)


def unit_rows(values):
    squares = jnp.sum(values * values, axis=1, keepdims=True)
    return (values * lax.rsqrt(squares + 1e-06)).astype(jnp.bfloat16)


def first_kernel(embeddings_ref, first_ref):
    for row in range(0, first_ref.shape[0], 128):
        first_ref[row : row + 128, :] = unit_rows(embeddings_ref[row : row + 128, :])


def rest_kernel(rows, embeddings_ref, ints_ref, first_ref, last_ref, head_ref, tail_ref):
    label_row = rows // 128
    owner, label = ints_ref[0:8, :], ints_ref[label_row : label_row + 8, :]
    runs = ints_ref[2 * label_row : 2 * label_row + 1, :]
    first_owner = jnp.take_along_axis(jnp.broadcast_to(runs, owner.shape), owner, axis=1)
    tags = 1 + jnp.where(label == 0, first_owner * LABELS, owner * LABELS + label)
    tags = tags.astype(jnp.float32)
    high = jnp.floor(tags * (1.0 / BASE))
    digits = jnp.concatenate([high, tags - high * BASE], axis=0).astype(jnp.bfloat16)
    width = embeddings_ref.shape[1]
    digits = jnp.concatenate([digits, jnp.zeros((PAD, width - 128), jnp.bfloat16)], axis=1)
    last_ref[0:PAD, :] = digits
    head_ref[0:PAD, :] = digits
    first = first_ref.shape[0]
    head = head_ref.shape[0] - PAD
    head_ref[PAD : PAD + first, :] = first_ref[...]
    for row in range(first, rows, 128):
        unit = unit_rows(embeddings_ref[row : row + 128, :])
        last_ref[PAD + row - first : PAD + row - first + 128, :] = unit
        if row < head:
            head_ref[PAD + row : PAD + row + 128, :] = unit
        else:
            tail_ref[row - head : row - head + 128, :] = unit


def tag_rows(block_ref):
    digits = block_ref[0:PAD, 0:128].astype(jnp.float32)
    return digits[0:8] * BASE + digits[8:16]


def tag_columns(block_ref, first, count):
    tags = tag_rows(block_ref)
    parts = [
        jnp.transpose(jnp.broadcast_to(tags[n : n + 1], (128, 128)))
        for n in range(first // 128, (first + count) // 128)
    ]
    return jnp.concatenate(parts, axis=0)


def dot_rows(values, lanes):
    return lax.dot_general(
        values, lanes, (((1,), (1,)), ((), ())), preferred_element_type=jnp.float32
    )


def unit_parts(refs):
    parts, first = [], 0
    for n, ref in enumerate(refs):
        part = ref if n + 1 < len(refs) else ref.at[PAD:]
        parts.append((first, part))
        first += part.shape[0]
    return parts


def take(refs, counts):
    groups = []
    for count in counts:
        groups.append(refs[:count])
        refs = refs[count:]
    return groups, refs


def fold_sublanes(values):
    rows, lanes = values.shape
    return jnp.max(values.reshape(rows // 8, 8, lanes), axis=0)


def fold_lanes(values):
    return jnp.concatenate(
        [
            jnp.max(jnp.transpose(values[first : first + 128]), axis=0, keepdims=True)
            for first in range(0, values.shape[0], 128)
        ],
        axis=0,
    )


def row_slices(block):
    slices = []
    for first, part in unit_parts(block):
        count = part.shape[0]
        for row in range(0, count, TILE):
            size = min(TILE, count - row)
            slices.append((first + row, part.at[row : row + size]))
    return slices


def plane_kernel(rows, with_self, *refs):
    (own, one, two), refs = take(refs, (2, 2, 2))
    best_ref = refs[-1]
    own_tags = tag_rows(own[-1])
    columns = [tag_columns(block[-1], 0, rows) for block in (one, two)]
    for tile, own_part in row_slices(own):
        lanes = own_part[...]
        best = [jnp.full((8, 128), -1.0, jnp.float32) for _ in range(0, TILE, 128)]
        for which, block in enumerate((one, two)):
            for first, part in row_slices(block):
                count = part.shape[0]
                found = dot_rows(part[...], lanes)
                column = columns[which][first : first + count]
                for n in range(TILE // 128):
                    lane = tile + n * 128
                    match = column == own_tags[lane // 128 : lane // 128 + 1]
                    if with_self and which == 0 and first < lane + 128 and lane < first + count:
                        row_id = lax.broadcasted_iota(jnp.int32, (count, 128), 0) + first
                        lane_id = lax.broadcasted_iota(jnp.int32, (count, 128), 1) + lane
                        match = match & (row_id != lane_id)
                    masked = jnp.where(match, found[:, n * 128 : n * 128 + 128], -1.0)
                    best[n] = jnp.maximum(best[n], fold_sublanes(masked))
        for n in range(TILE // 128):
            place = pl.ds(tile // 128 + n, 1)
            folded = jnp.max(best[n], axis=0, keepdims=True)
            if with_self:
                folded = jnp.maximum(folded, refs[0][place, :])
            best_ref[place, :] = folded


def cross_kernel(starts, bases, *refs):
    (tags, aways), refs = take(refs, (1, len(starts)))
    blocks, refs = take(refs, (2,) * PLANE)
    away_before, away_best = refs[0], refs[PLANE + 1]
    plane_before, plane_best = refs[1 : PLANE + 1], refs[PLANE + 2 :]
    plane_tags = [tag_rows(block[-1]) for block in blocks]
    away_best[...] = away_before[...]
    best = {}
    for start, base, away in zip(starts, bases, aways):
        for tile in range(0, away.shape[0] - base, TILE):
            values = away[base + tile : base + tile + TILE, :]
            column = tag_columns(tags[0], start + tile, TILE)
            row_best = jnp.full((TILE, 128), -1.0, jnp.float32)
            for which in range(PLANE):
                for first, part in row_slices(blocks[which]):
                    found = dot_rows(values, part[...])
                    for lane in range(0, part.shape[0], 128):
                        row = (first + lane) // 128
                        match = column == plane_tags[which][row : row + 1]
                        masked = jnp.where(match, found[:, lane : lane + 128], -1.0)
                        row_best = jnp.maximum(row_best, masked)
                        folded = fold_sublanes(masked)
                        place = which, row
                        best[place] = jnp.maximum(best[place], folded) if place in best else folded
            place = pl.ds((start + tile) // 128, TILE // 128)
            away_best[place, :] = fold_lanes(row_best)
    for which in range(PLANE):
        plane_best[which][...] = plane_before[which][...]
    for (which, row), values in best.items():
        folded = jnp.max(values, axis=0, keepdims=True)
        place = pl.ds(row, 1)
        plane_best[which][place, :] = jnp.maximum(folded, plane_before[which][place, :])


def small_cost():
    return pl.CostEstimate(flops=1, bytes_accessed=1, transcendentals=0)


def plane_steps(planes):
    if planes == 4:
        return [[(0, 2), (1, 0), (2, 3), (3, 1)], [(3, 0), (1, 2)]]
    return [
        [(z, (z + distance) % planes) for z in range(planes)]
        for distance in range(1, planes // 2 + 1)
    ]


def after(value, *others):
    if not others:
        return value
    return lax.optimization_barrier((value,) + others)[0]


def local(embeddings, owner_index, sub_label, run_start):
    rows, width = embeddings.shape
    peers = lax.axis_size("dp")
    planes = peers // PLANE
    lanes = lanes_shape(rows)

    space = -(2 * rows + peers) % 2048
    ints = jnp.concatenate([owner_index, sub_label, run_start, jnp.zeros((space,), jnp.int32)])
    ints = ints.reshape(-1, 128)
    def kernel(body, inputs, outputs, name):
        return pl.pallas_call(
            body,
            out_shape=tuple(outputs),
            in_specs=whole(len(inputs)),
            out_specs=tuple(whole(len(outputs))),
            compiler_params=params(),
            cost_estimate=small_cost(),
            name=name,
        )(*inputs)

    def part_shape(count):
        return jax.ShapeDtypeStruct((count, width), jnp.bfloat16)

    (first,) = kernel(first_kernel, (embeddings,), (part_shape(FIRST),), "first")
    last, head, tail = kernel(
        functools.partial(rest_kernel, rows),
        (embeddings, ints, first),
        (part_shape(PAD + rows - FIRST), part_shape(PAD + HEAD), part_shape(rows - HEAD)),
        "rest",
    )
    own = (first, last)

    def mate(value, distance):
        return lax.ppermute(value, "dp", [(i, i ^ distance) for i in range(peers)])

    away = []
    for n, step in enumerate(plane_steps(planes)):
        pairs = [(z * PLANE + j, t * PLANE + j) for z, t in step for j in range(PLANE)]
        parts = (head, tail) if n else own
        if n > 1:
            parts = [after(part, away[-1][1][-1]) for part in parts]
        away.append((pairs, [lax.ppermute(part, "dp", pairs) for part in parts]))
    beside = [mate(part, 2) for part in own]
    near = [mate(part, 1) for part in own]
    across = [mate(after(part, *away[0][1]), 1) for part in beside]

    (best,) = kernel(
        functools.partial(plane_kernel, rows, False),
        (*own, *beside, *across),
        (lanes,),
        "plane_far",
    )
    (best,) = kernel(
        functools.partial(plane_kernel, rows, True),
        (*own, *own, *near, best),
        (lanes,),
        "plane_near",
    )
    plane = (*own, *near, *beside, *across)
    plane_best = [best] + [jnp.full(lanes.shape, -1.0, jnp.float32)] * (PLANE - 1)
    backs = []
    for n, (pairs, received) in enumerate(away):
        away_best = jnp.full(lanes.shape, -1.0, jnp.float32)
        if n:
            calls = (((0,), (PAD,), received[:1]), ((HEAD,), (0,), received[1:]))
        else:
            calls = (((0, FIRST), (0, PAD), received),)
        tags = received[0] if n else received[-1]
        for starts, bases, parts in calls:
            away_best, *plane_best = kernel(
                functools.partial(cross_kernel, starts, bases),
                (tags, *parts, *plane, away_best, *plane_best),
                (lanes,) * (PLANE + 1),
                "cross",
            )
        answer = after(away_best, *(back for back, _ in backs[:1]))
        back = lax.ppermute(answer, "dp", [(t, s) for s, t in pairs]).reshape(-1)[:rows]
        sent = None
        if len(pairs) < peers:
            sources = sum(1 << z for z in {s // PLANE for s, _ in pairs})
            sent = (jnp.int32(sources) >> (lax.axis_index("dp") // PLANE)) & 1
        backs.append((back, sent))
    best = plane_best[0].reshape(-1)[:rows]
    for distance in (3, 2, 1):
        back = mate(after(plane_best[distance], backs[0][0]), distance)
        backs.append((back.reshape(-1)[:rows], None))
    for back, sent in backs:
        best = jnp.maximum(back if sent is None else jnp.where(sent == 1, back, -1.0), best)
    return best


def solution(mesh):
    in_specs = (P(("groups", "dp"), None), P(("groups", "dp")), P(("groups", "dp")), P("groups"))
    out_specs = P(("groups", "dp"))
    return jax.shard_map(local, mesh=mesh, in_specs=in_specs, out_specs=out_specs, check_vma=False)
```

```python
import functools

import jax
import jax.numpy as jnp
from jax import lax
from jax.experimental import pallas as pl
from jax.experimental.pallas import tpu as pltpu
from jax.sharding import PartitionSpec as P

LABELS = 3
PLANE = 4
PAD = 16
BASE = 64.0
TILE = 256
WIDE = 512
FIRST = 512
HEAD = 512
VMEM_LIMIT = 24 * 2**20


def whole(count):
    return [pl.BlockSpec(memory_space=pltpu.VMEM)] * count


def params():
    return pltpu.CompilerParams(vmem_limit_bytes=VMEM_LIMIT)


def lanes_shape(rows):
    return jax.ShapeDtypeStruct((-(-rows // 1024) * 8, 128), jnp.float32)


def unit_rows(values):
    squares = jnp.sum(values * values, axis=1, keepdims=True)
    return (values * lax.rsqrt(squares + 1e-06)).astype(jnp.bfloat16)


def first_kernel(embeddings_ref, first_ref):
    for row in range(0, first_ref.shape[0], 128):
        first_ref[row : row + 128, :] = unit_rows(embeddings_ref[row : row + 128, :])


def rest_kernel(rows, embeddings_ref, ints_ref, first_ref, last_ref, head_ref, tail_ref):
    label_row = rows // 128
    owner, label = ints_ref[0:8, :], ints_ref[label_row : label_row + 8, :]
    runs = ints_ref[2 * label_row : 2 * label_row + 1, :]
    first_owner = jnp.take_along_axis(jnp.broadcast_to(runs, owner.shape), owner, axis=1)
    tags = 1 + jnp.where(label == 0, first_owner * LABELS, owner * LABELS + label)
    tags = tags.astype(jnp.float32)
    high = jnp.floor(tags * (1.0 / BASE))
    digits = jnp.concatenate([high, tags - high * BASE], axis=0).astype(jnp.bfloat16)
    width = embeddings_ref.shape[1]
    digits = jnp.concatenate([digits, jnp.zeros((PAD, width - 128), jnp.bfloat16)], axis=1)
    last_ref[0:PAD, :] = digits
    head_ref[0:PAD, :] = digits
    first = first_ref.shape[0]
    head = head_ref.shape[0] - PAD
    head_ref[PAD : PAD + first, :] = first_ref[...]
    for row in range(first, rows, 128):
        unit = unit_rows(embeddings_ref[row : row + 128, :])
        last_ref[PAD + row - first : PAD + row - first + 128, :] = unit
        if row < head:
            head_ref[PAD + row : PAD + row + 128, :] = unit
        else:
            tail_ref[row - head : row - head + 128, :] = unit


def tag_rows(block_ref):
    digits = block_ref[0:PAD, 0:128].astype(jnp.float32)
    return digits[0:8] * BASE + digits[8:16]


def tag_columns(block_ref, first, count):
    tags = tag_rows(block_ref)
    parts = [
        jnp.transpose(jnp.broadcast_to(tags[n : n + 1], (128, 128)))
        for n in range(first // 128, (first + count) // 128)
    ]
    return jnp.concatenate(parts, axis=0)


def dot_rows(values, lanes):
    return lax.dot_general(
        values, lanes, (((1,), (1,)), ((), ())), preferred_element_type=jnp.float32
    )


def unit_parts(refs):
    parts, first = [], 0
    for n, ref in enumerate(refs):
        part = ref if n + 1 < len(refs) else ref.at[PAD:]
        parts.append((first, part))
        first += part.shape[0]
    return parts


def take(refs, counts):
    groups = []
    for count in counts:
        groups.append(refs[:count])
        refs = refs[count:]
    return groups, refs


def fold_sublanes(values):
    rows, lanes = values.shape
    return jnp.max(values.reshape(rows // 8, 8, lanes), axis=0)


def fold_lanes(values):
    return jnp.concatenate(
        [
            jnp.max(jnp.transpose(values[first : first + 128]), axis=0, keepdims=True)
            for first in range(0, values.shape[0], 128)
        ],
        axis=0,
    )


def row_slices(block, most=TILE):
    slices = []
    for first, part in unit_parts(block):
        count = part.shape[0]
        for row in range(0, count, most):
            size = min(most, count - row)
            slices.append((first + row, part.at[row : row + size]))
    return slices


def plane_kernel(rows, with_self, *refs):
    (own, one, two), refs = take(refs, (2, 2, 2))
    best_ref = refs[-1]
    own_tags = tag_rows(own[-1])
    columns = [tag_columns(block[-1], 0, rows) for block in (one, two)]
    for tile, own_part in row_slices(own):
        lanes = own_part[...]
        best = [jnp.full((8, 128), -1.0, jnp.float32) for _ in range(0, TILE, 128)]
        for which, block in enumerate((one, two)):
            for first, part in row_slices(block):
                count = part.shape[0]
                found = dot_rows(part[...], lanes)
                column = columns[which][first : first + count]
                for n in range(TILE // 128):
                    lane = tile + n * 128
                    match = column == own_tags[lane // 128 : lane // 128 + 1]
                    if with_self and which == 0 and first < lane + 128 and lane < first + count:
                        row_id = lax.broadcasted_iota(jnp.int32, (count, 128), 0) + first
                        lane_id = lax.broadcasted_iota(jnp.int32, (count, 128), 1) + lane
                        match = match & (row_id != lane_id)
                    masked = jnp.where(match, found[:, n * 128 : n * 128 + 128], -1.0)
                    best[n] = jnp.maximum(best[n], fold_sublanes(masked))
        for n in range(TILE // 128):
            place = pl.ds(tile // 128 + n, 1)
            folded = jnp.max(best[n], axis=0, keepdims=True)
            if with_self:
                folded = jnp.maximum(folded, refs[0][place, :])
            best_ref[place, :] = folded


def cross_kernel(starts, bases, *refs):
    (tags, aways), refs = take(refs, (1, len(starts)))
    blocks, refs = take(refs, (2,) * PLANE)
    away_before, away_best = refs[0], refs[PLANE + 1]
    plane_before, plane_best = refs[1 : PLANE + 1], refs[PLANE + 2 :]
    plane_tags = [tag_rows(block[-1]) for block in blocks]
    away_best[...] = away_before[...]
    best = {}
    for start, base, away in zip(starts, bases, aways):
        for tile in range(0, away.shape[0] - base, TILE):
            values = away[base + tile : base + tile + TILE, :]
            column = tag_columns(tags[0], start + tile, TILE)
            row_best = jnp.full((TILE, 128), -1.0, jnp.float32)
            for which in range(PLANE):
                for first, part in row_slices(blocks[which], WIDE):
                    found = dot_rows(values, part[...])
                    for lane in range(0, part.shape[0], 128):
                        row = (first + lane) // 128
                        match = column == plane_tags[which][row : row + 1]
                        masked = jnp.where(match, found[:, lane : lane + 128], -1.0)
                        row_best = jnp.maximum(row_best, masked)
                        folded = fold_sublanes(masked)
                        place = which, row
                        best[place] = jnp.maximum(best[place], folded) if place in best else folded
            place = pl.ds((start + tile) // 128, TILE // 128)
            away_best[place, :] = fold_lanes(row_best)
    for which in range(PLANE):
        plane_best[which][...] = plane_before[which][...]
    for (which, row), values in best.items():
        folded = jnp.max(values, axis=0, keepdims=True)
        place = pl.ds(row, 1)
        plane_best[which][place, :] = jnp.maximum(folded, plane_before[which][place, :])


def small_cost():
    return pl.CostEstimate(flops=1, bytes_accessed=1, transcendentals=0)


def plane_steps(planes):
    if planes == 4:
        return [[(0, 2), (1, 0), (2, 3), (3, 1)], [(0, 3), (2, 1)]]
    return [
        [(z, (z + distance) % planes) for z in range(planes)]
        for distance in range(1, planes // 2 + 1)
    ]


def after(value, *others):
    if not others:
        return value
    return lax.optimization_barrier((value,) + others)[0]


def local(embeddings, owner_index, sub_label, run_start):
    rows, width = embeddings.shape
    peers = lax.axis_size("dp")
    planes = peers // PLANE
    lanes = lanes_shape(rows)

    space = -(2 * rows + peers) % 2048
    ints = jnp.concatenate([owner_index, sub_label, run_start, jnp.zeros((space,), jnp.int32)])
    ints = ints.reshape(-1, 128)
    def kernel(body, inputs, outputs, name):
        return pl.pallas_call(
            body,
            out_shape=tuple(outputs),
            in_specs=whole(len(inputs)),
            out_specs=tuple(whole(len(outputs))),
            compiler_params=params(),
            cost_estimate=small_cost(),
            name=name,
        )(*inputs)

    def part_shape(count):
        return jax.ShapeDtypeStruct((count, width), jnp.bfloat16)

    (first,) = kernel(first_kernel, (embeddings,), (part_shape(FIRST),), "first")
    last, head, tail = kernel(
        functools.partial(rest_kernel, rows),
        (embeddings, ints, first),
        (part_shape(PAD + rows - FIRST), part_shape(PAD + HEAD), part_shape(rows - HEAD)),
        "rest",
    )
    own = (first, last)

    def mate(value, distance):
        return lax.ppermute(value, "dp", [(i, i ^ distance) for i in range(peers)])

    away = []
    for n, step in enumerate(plane_steps(planes)):
        pairs = [(z * PLANE + j, t * PLANE + j) for z, t in step for j in range(PLANE)]
        parts = (head, tail) if n else own
        if n > 1:
            parts = [after(part, away[-1][1][-1]) for part in parts]
        away.append((pairs, [lax.ppermute(part, "dp", pairs) for part in parts]))
    beside = [mate(part, 2) for part in own]
    near = [mate(part, 1) for part in own]
    across = [mate(after(part, *away[0][1]), 1) for part in beside]

    (best,) = kernel(
        functools.partial(plane_kernel, rows, False),
        (*own, *beside, *across),
        (lanes,),
        "plane_far",
    )
    (best,) = kernel(
        functools.partial(plane_kernel, rows, True),
        (*own, *own, *near, best),
        (lanes,),
        "plane_near",
    )
    plane = (*own, *near, *beside, *across)
    plane_best = [best] + [jnp.full(lanes.shape, -1.0, jnp.float32)] * (PLANE - 1)
    backs, masks = [], {}
    for n, (pairs, received) in enumerate(away):
        away_best = jnp.full(lanes.shape, -1.0, jnp.float32)
        if n:
            calls = (((0,), (PAD,), received[:1]), ((HEAD,), (0,), received[1:]))
        else:
            calls = (((0, FIRST), (0, PAD), received),)
        tags = received[0] if n else received[-1]
        for starts, bases, parts in calls:
            away_best, *plane_best = kernel(
                functools.partial(cross_kernel, starts, bases),
                (tags, *parts, *plane, away_best, *plane_best),
                (lanes,) * (PLANE + 1),
                "cross",
            )
        backs.append(lax.ppermute(away_best, "dp", [(t, s) for s, t in pairs]))
        if len(pairs) < peers:
            sources = sum(1 << z for z in {s // PLANE for s, _ in pairs})
            sent = (jnp.int32(sources) >> (lax.axis_index("dp") // PLANE)) & 1
            masks[n] = jnp.broadcast_to(sent == 1, (rows,))
    best = plane_best[0].reshape(-1)[:rows]
    for distance in (3, 2, 1):
        backs.append(mate(after(plane_best[distance], *backs[:1]), distance))
    for n, back in enumerate(backs):
        back = back.reshape(-1)[:rows]
        best = jnp.maximum(best, jnp.where(masks[n], back, -1.0) if n in masks else back)
    return best


def solution(mesh):
    in_specs = (P(("groups", "dp"), None), P(("groups", "dp")), P(("groups", "dp")), P("groups"))
    out_specs = P(("groups", "dp"))
    return jax.shard_map(local, mesh=mesh, in_specs=in_specs, out_specs=out_specs, check_vma=False)
```

```python
import functools

import jax
import jax.numpy as jnp
from jax import lax
from jax.experimental import pallas as pl
from jax.experimental.pallas import tpu as pltpu
from jax.sharding import PartitionSpec as P

LABELS = 3
PLANE = 4
PAD = 16
BASE = 64.0
TILE = 256
FIRST = 512
HEAD = 512
VMEM_LIMIT = 24 * 2**20


def whole(count):
    return [pl.BlockSpec(memory_space=pltpu.VMEM)] * count


def params():
    return pltpu.CompilerParams(vmem_limit_bytes=VMEM_LIMIT)


def lanes_shape(rows):
    return jax.ShapeDtypeStruct((-(-rows // 1024) * 8, 128), jnp.float32)


def unit_rows(values):
    squares = jnp.sum(values * values, axis=1, keepdims=True)
    return (values * lax.rsqrt(squares + 1e-06)).astype(jnp.bfloat16)


def first_kernel(embeddings_ref, first_ref):
    for row in range(0, first_ref.shape[0], 128):
        first_ref[row : row + 128, :] = unit_rows(embeddings_ref[row : row + 128, :])


def rest_kernel(rows, embeddings_ref, ints_ref, first_ref, last_ref, head_ref, tail_ref):
    label_row = rows // 128
    owner, label = ints_ref[0:8, :], ints_ref[label_row : label_row + 8, :]
    runs = ints_ref[2 * label_row : 2 * label_row + 1, :]
    first_owner = jnp.take_along_axis(jnp.broadcast_to(runs, owner.shape), owner, axis=1)
    tags = 1 + jnp.where(label == 0, first_owner * LABELS, owner * LABELS + label)
    tags = tags.astype(jnp.float32)
    high = jnp.floor(tags * (1.0 / BASE))
    digits = jnp.concatenate([high, tags - high * BASE], axis=0).astype(jnp.bfloat16)
    width = embeddings_ref.shape[1]
    digits = jnp.concatenate([digits, jnp.zeros((PAD, width - 128), jnp.bfloat16)], axis=1)
    last_ref[0:PAD, :] = digits
    head_ref[0:PAD, :] = digits
    first = first_ref.shape[0]
    head = head_ref.shape[0] - PAD
    head_ref[PAD : PAD + first, :] = first_ref[...]
    for row in range(first, rows, 128):
        unit = unit_rows(embeddings_ref[row : row + 128, :])
        last_ref[PAD + row - first : PAD + row - first + 128, :] = unit
        if row < head:
            head_ref[PAD + row : PAD + row + 128, :] = unit
        else:
            tail_ref[row - head : row - head + 128, :] = unit


def tag_rows(block_ref):
    digits = block_ref[0:PAD, 0:128].astype(jnp.float32)
    return digits[0:8] * BASE + digits[8:16]


def tag_columns(block_ref, first, count):
    tags = tag_rows(block_ref)
    parts = [
        jnp.transpose(jnp.broadcast_to(tags[n : n + 1], (128, 128)))
        for n in range(first // 128, (first + count) // 128)
    ]
    return jnp.concatenate(parts, axis=0)


def dot_rows(values, lanes):
    return lax.dot_general(
        values, lanes, (((1,), (1,)), ((), ())), preferred_element_type=jnp.float32
    )


def unit_parts(refs):
    parts, first = [], 0
    for n, ref in enumerate(refs):
        part = ref if n + 1 < len(refs) else ref.at[PAD:]
        parts.append((first, part))
        first += part.shape[0]
    return parts


def take(refs, counts):
    groups = []
    for count in counts:
        groups.append(refs[:count])
        refs = refs[count:]
    return groups, refs


def fold_sublanes(values):
    rows, lanes = values.shape
    return jnp.max(values.reshape(rows // 8, 8, lanes), axis=0)


def fold_lanes(values):
    return jnp.concatenate(
        [
            jnp.max(jnp.transpose(values[first : first + 128]), axis=0, keepdims=True)
            for first in range(0, values.shape[0], 128)
        ],
        axis=0,
    )


def row_slices(block):
    slices = []
    for first, part in unit_parts(block):
        count = part.shape[0]
        for row in range(0, count, TILE):
            size = min(TILE, count - row)
            slices.append((first + row, part.at[row : row + size]))
    return slices


def plane_kernel(rows, with_self, *refs):
    (own, one, two), refs = take(refs, (2, 2, 2))
    best_ref = refs[-1]
    own_tags = tag_rows(own[-1])
    columns = [tag_columns(block[-1], 0, rows) for block in (one, two)]
    for tile, own_part in row_slices(own):
        lanes = own_part[...]
        best = [jnp.full((8, 128), -1.0, jnp.float32) for _ in range(0, TILE, 128)]
        for which, block in enumerate((one, two)):
            for first, part in row_slices(block):
                count = part.shape[0]
                found = dot_rows(part[...], lanes)
                column = columns[which][first : first + count]
                for n in range(TILE // 128):
                    lane = tile + n * 128
                    match = column == own_tags[lane // 128 : lane // 128 + 1]
                    if with_self and which == 0 and first < lane + 128 and lane < first + count:
                        row_id = lax.broadcasted_iota(jnp.int32, (count, 128), 0) + first
                        lane_id = lax.broadcasted_iota(jnp.int32, (count, 128), 1) + lane
                        match = match & (row_id != lane_id)
                    masked = jnp.where(match, found[:, n * 128 : n * 128 + 128], -1.0)
                    best[n] = jnp.maximum(best[n], fold_sublanes(masked))
        for n in range(TILE // 128):
            place = pl.ds(tile // 128 + n, 1)
            folded = jnp.max(best[n], axis=0, keepdims=True)
            if with_self:
                folded = jnp.maximum(folded, refs[0][place, :])
            best_ref[place, :] = folded


def cross_kernel(starts, bases, *refs):
    (tags, aways), refs = take(refs, (1, len(starts)))
    blocks, refs = take(refs, (2,) * PLANE)
    away_before, away_best = refs[0], refs[PLANE + 1]
    plane_before, plane_best = refs[1 : PLANE + 1], refs[PLANE + 2 :]
    plane_tags = [tag_rows(block[-1]) for block in blocks]
    away_best[...] = away_before[...]
    best = {}
    for start, base, away in zip(starts, bases, aways):
        for tile in range(0, away.shape[0] - base, TILE):
            values = away[base + tile : base + tile + TILE, :]
            column = tag_columns(tags[0], start + tile, TILE)
            row_best = jnp.full((TILE, 128), -1.0, jnp.float32)
            for which in range(PLANE):
                for first, part in row_slices(blocks[which]):
                    found = dot_rows(values, part[...])
                    for lane in range(0, part.shape[0], 128):
                        row = (first + lane) // 128
                        match = column == plane_tags[which][row : row + 1]
                        masked = jnp.where(match, found[:, lane : lane + 128], -1.0)
                        row_best = jnp.maximum(row_best, masked)
                        folded = fold_sublanes(masked)
                        place = which, row
                        best[place] = jnp.maximum(best[place], folded) if place in best else folded
            place = pl.ds((start + tile) // 128, TILE // 128)
            away_best[place, :] = fold_lanes(row_best)
    for which in range(PLANE):
        plane_best[which][...] = plane_before[which][...]
    for (which, row), values in best.items():
        folded = jnp.max(values, axis=0, keepdims=True)
        place = pl.ds(row, 1)
        plane_best[which][place, :] = jnp.maximum(folded, plane_before[which][place, :])


def small_cost():
    return pl.CostEstimate(flops=1, bytes_accessed=1, transcendentals=0)


def plane_steps(planes):
    if planes == 4:
        return [[(0, 2), (1, 0), (2, 3), (3, 1)], [(0, 3), (2, 1)]]
    return [
        [(z, (z + distance) % planes) for z in range(planes)]
        for distance in range(1, planes // 2 + 1)
    ]


def after(value, *others):
    if not others:
        return value
    return lax.optimization_barrier((value,) + others)[0]


def local(embeddings, owner_index, sub_label, run_start):
    rows, width = embeddings.shape
    peers = lax.axis_size("dp")
    planes = peers // PLANE
    lanes = lanes_shape(rows)

    space = -(2 * rows + peers) % 2048
    ints = jnp.concatenate([owner_index, sub_label, run_start, jnp.zeros((space,), jnp.int32)])
    ints = ints.reshape(-1, 128)
    def kernel(body, inputs, outputs, name):
        return pl.pallas_call(
            body,
            out_shape=tuple(outputs),
            in_specs=whole(len(inputs)),
            out_specs=tuple(whole(len(outputs))),
            compiler_params=params(),
            cost_estimate=small_cost(),
            name=name,
        )(*inputs)

    def part_shape(count):
        return jax.ShapeDtypeStruct((count, width), jnp.bfloat16)

    (first,) = kernel(first_kernel, (embeddings,), (part_shape(FIRST),), "first")
    last, head, tail = kernel(
        functools.partial(rest_kernel, rows),
        (embeddings, ints, first),
        (part_shape(PAD + rows - FIRST), part_shape(PAD + HEAD), part_shape(rows - HEAD)),
        "rest",
    )
    own = (first, last)

    def mate(value, distance):
        return lax.ppermute(value, "dp", [(i, i ^ distance) for i in range(peers)])

    away = []
    for n, step in enumerate(plane_steps(planes)):
        pairs = [(z * PLANE + j, t * PLANE + j) for z, t in step for j in range(PLANE)]
        parts = (head, tail) if n else own
        if n > 1:
            parts = [after(part, away[-1][1][-1]) for part in parts]
        away.append((pairs, [lax.ppermute(part, "dp", pairs) for part in parts]))
    beside = [mate(part, 2) for part in own]
    near = [mate(part, 1) for part in own]
    across = [mate(after(part, *away[0][1]), 1) for part in beside]

    (best,) = kernel(
        functools.partial(plane_kernel, rows, False),
        (*own, *beside, *across),
        (lanes,),
        "plane_far",
    )
    (best,) = kernel(
        functools.partial(plane_kernel, rows, True),
        (*own, *own, *near, best),
        (lanes,),
        "plane_near",
    )
    plane = (*own, *near, *beside, *across)
    plane_best = [best] + [jnp.full(lanes.shape, -1.0, jnp.float32)] * (PLANE - 1)
    backs, masks = [], {}
    for n, (pairs, received) in enumerate(away):
        away_best = jnp.full(lanes.shape, -1.0, jnp.float32)
        if n:
            calls = (((0,), (PAD,), received[:1]), ((HEAD,), (0,), received[1:]))
        else:
            calls = (((0, FIRST), (0, PAD), received),)
        tags = received[0] if n else received[-1]
        for starts, bases, parts in calls:
            away_best, *plane_best = kernel(
                functools.partial(cross_kernel, starts, bases),
                (tags, *parts, *plane, away_best, *plane_best),
                (lanes,) * (PLANE + 1),
                "cross",
            )
        backs.append(lax.ppermute(away_best, "dp", [(t, s) for s, t in pairs]))
        if len(pairs) < peers:
            sources = sum(1 << z for z in {s // PLANE for s, _ in pairs})
            sent = (jnp.int32(sources) >> (lax.axis_index("dp") // PLANE)) & 1
            masks[n] = jnp.broadcast_to(sent == 1, (rows,))
    best = plane_best[0].reshape(-1)[:rows]
    for distance in (3, 2, 1):
        backs.append(mate(after(plane_best[distance], *backs[:1]), distance))
    for n, back in enumerate(backs):
        back = back.reshape(-1)[:rows]
        best = jnp.maximum(jnp.where(masks[n], back, -1.0) if n in masks else back, best)
    return best


def solution(mesh):
    in_specs = (P(("groups", "dp"), None), P(("groups", "dp")), P(("groups", "dp")), P("groups"))
    out_specs = P(("groups", "dp"))
    return jax.shard_map(local, mesh=mesh, in_specs=in_specs, out_specs=out_specs, check_vma=False)
```
